32 devices in a mesh: group: 4 (over y, x), seq: 4 (over z), wshard: 2 (over core).
Axes of the slice: x: 2, y: 2, z: 4, core: 2. Of those that a mesh axis runs over, the one named last changes fastest.
Arguments:
- tokens: bfloat16 [6144, 2048], P(('group', 'seq', 'wshard')), may hold values from -6 to 6
- cotangent: bfloat16 [6144, 2048], P(('group', 'seq', 'wshard')), may hold values from -6 to 6
- dealing: int32 [6144], P(('group', 'seq', 'wshard')), may hold values from 0 to 3, as said below
- lengths: int32 [4, 2, 4], P('group', 'wshard'), may hold values from 1 to 624, as said below
- attn_gain: bfloat16 [2048], P(('seq', 'wshard')), may hold values from 0.5 to 1.5
- w_in: bfloat16 [2048, 12288], P(('seq', 'wshard')), may hold values from -0.125 to 0.125
- w_ab: bfloat16 [2048, 32], P(('seq', 'wshard')), may hold values from -0.125 to 0.125
- conv_w: bfloat16 [4, 8192], P(None, ('seq', 'wshard')), may hold values from -3 to 3
- decay_log: float32 [16], replicated, may hold values from -6 to 1
- dt_bias: float32 [16], replicated, may hold values from -5 to -1
- o_gain: bfloat16 [256], P(('seq', 'wshard')), may hold values from 0.5 to 1.5
- w_out: bfloat16 [4096, 2048], P(('seq', 'wshard')), may hold values from -0.09375 to 0.09375
- ffn_gain: bfloat16 [2048], P(('seq', 'wshard')), may hold values from 0.5 to 1.5
- w_gu: bfloat16 [2048, 11264], P(('seq', 'wshard')), may hold values from -0.125 to 0.125
- w_down: bfloat16 [5632, 2048], P(('seq', 'wshard')), may hold values from -0.078125 to 0.078125
Outputs:
- output: bfloat16 [6144, 2048], P(('group', 'seq', 'wshard'))
- input_grad: bfloat16 [6144, 2048], P(('group', 'seq', 'wshard'))
- grad_attn_gain: float32 [2048], P(('seq', 'wshard'))
- grad_w_in: float32 [2048, 12288], P(('seq', 'wshard'))
- grad_w_ab: float32 [2048, 32], P(('seq', 'wshard'))
- grad_conv_w: float32 [4, 8192], P(None, ('seq', 'wshard'))
- grad_decay_log: float32 [16], replicated
- grad_dt_bias: float32 [16], replicated
- grad_o_gain: float32 [256], P(('seq', 'wshard'))
- grad_w_out: float32 [4096, 2048], P(('seq', 'wshard'))
- grad_ffn_gain: float32 [2048], P(('seq', 'wshard'))
- grad_w_gu: float32 [2048, 11264], P(('seq', 'wshard'))
- grad_w_down: float32 [5632, 2048], P(('seq', 'wshard'))
The draws below stay inside these ranges and needn't reach their ends.
Inputs may be any that keep to these rules, and one draw needn't show every extreme that they name: `dealing`: on every device each group index appears exactly 192 // 4 times. The lengths of a lane sum to 768 or less, the positions after them are padding; one length of each lane, at a place drawn from the seed, is at least 577, and the others are at most 48.
All inputs are finite; a program needn't handle non-finite values.
Results may differ from the reference program's by a relative error of at most 0.023.
The reference program's roundings to bfloat16 on the way count: a program that leaves them out, or rounds other values in their place, can miss the bound.
Values may be sent and summed in bfloat16 or wider, within the bound.
A program may use at most 576 MiB of HBM per device.

```python
import jax
import jax.numpy as jnp
from jax import lax

D = 2048
H = 16
DK = 128
DV = 256
FF = 5632
CONV = 4
SPAN = 64
TOK_DEV = 192
SEQS = 4
HK = 2048
HV = 4096
GROUP_TOK = 768
LANES = 8
TOKENS = 6144
N_GROUP = 4
N_SEQ = 4
N_WSHARD = 2


def draw_dealing(key, part):
    key = jax.random.fold_in(key, 11)
    device_count = TOKENS // TOK_DEV
    key_list = jax.random.split(key, device_count)
    orders = jax.vmap(lambda single_key: jax.random.permutation(single_key, TOK_DEV))(key_list)
    return (orders // (TOK_DEV // N_GROUP)).reshape(TOKENS).astype(jnp.int32)


def draw_lengths(key, part):
    key = jax.random.fold_in(key, 23)
    lane_count = N_GROUP * N_WSHARD
    short_most = TOK_DEV // SEQS
    key_short, key_pad, key_long, key_lane = jax.random.split(key, 4)
    shorts = jax.random.randint(key_short, (lane_count, SEQS), 1, short_most + 1)
    padding = jax.random.randint(key_pad, (lane_count, 1), 0, short_most)
    zero_lane = jax.random.randint(key_lane, (1, 1), 0, lane_count)
    padding = jnp.where(jnp.arange(lane_count)[:, None] == zero_lane, 0, padding)
    where_long = jax.random.randint(key_long, (lane_count, 1), 0, SEQS)
    places = jnp.arange(SEQS)[None, :]
    is_long = places == where_long
    longest = N_SEQ * TOK_DEV - (SEQS - 1) * short_most - padding
    return jnp.where(is_long, longest, shorts).reshape(N_GROUP, N_WSHARD, SEQS).astype(jnp.int32)


def level_of(rng, extent, shards, least, largest):
    factor_of = 1.0
    for axis_at, shards_of in shards:
        steps = jax.random.uniform(jax.random.fold_in(jax.random.fold_in(rng, 6), axis_at), (shards_of,), jnp.float32, least / len(shards), largest / len(shards))
        factor_of = factor_of * jnp.repeat(jnp.exp(steps), extent[axis_at] // shards_of).reshape((-1,) + (1,) * (len(extent) - 1 - axis_at))
    return factor_of


def gaussian(key, dims, deviation, limit, shards=(), held_as=jnp.bfloat16):
    level = level_of(key, dims, shards, -0.22, 0.18) if shards else 1.0
    drawn = jax.random.normal(key, dims, jnp.float32) * deviation * level
    return jnp.minimum(jnp.maximum(drawn, -limit), limit).astype(held_as)


def setup_inputs(seed: int = 0) -> dict:
    arg_keys = jax.random.split(jax.random.key(seed), 16)
    tokens = gaussian(arg_keys[0], (TOKENS, D), 1.0, 6.0, ((0, 32),))
    cotangent = gaussian(arg_keys[1], (TOKENS, D), 1.0, 6.0, ((0, 32),))
    dealing = draw_dealing(jax.random.fold_in(arg_keys[15], 71), 0)
    lengths = draw_lengths(jax.random.fold_in(arg_keys[15], 71), 0)
    attn_gain = jnp.clip(1.0 + 0.1 * jax.random.normal(arg_keys[4], (D,), jnp.float32), 0.5, 1.5).astype(jnp.bfloat16)
    w_in = gaussian(arg_keys[5], (D, 2 * HK + 2 * HV), D ** -0.5, 0.125, ((0, 8),))
    w_ab = gaussian(arg_keys[6], (D, 2 * H), D ** -0.5, 0.125, ((0, 8),))
    conv_w = gaussian(arg_keys[7], (CONV, 2 * HK + HV), 0.5, 3.0, ((1, 8),))
    decay_log = jnp.clip(jax.random.uniform(arg_keys[8], (H,), jnp.float32, -6.0, 1.0), -6.0, 1.0)
    dt_bias = jnp.clip(jax.random.uniform(arg_keys[9], (H,), jnp.float32, -5.0, -1.0), -5.0, -1.0)
    o_gain = jnp.clip(1.0 + 0.1 * jax.random.normal(arg_keys[10], (DV,), jnp.float32), 0.5, 1.5).astype(jnp.bfloat16)
    w_out = gaussian(arg_keys[11], (HV, D), HV ** -0.5, 0.09375, ((0, 8),))
    ffn_gain = jnp.clip(1.0 + 0.1 * jax.random.normal(arg_keys[12], (D,), jnp.float32), 0.5, 1.5).astype(jnp.bfloat16)
    w_gu = gaussian(arg_keys[13], (D, 2 * FF), D ** -0.5, 0.125, ((0, 8),))
    w_down = gaussian(arg_keys[14], (FF, D), FF ** -0.5, 0.078125, ((0, 8),))
    return {"tokens": tokens, "cotangent": cotangent, "dealing": dealing, "lengths": lengths, "attn_gain": attn_gain, "w_in": w_in, "w_ab": w_ab, "conv_w": conv_w, "decay_log": decay_log, "dt_bias": dt_bias, "o_gain": o_gain, "w_out": w_out, "ffn_gain": ffn_gain, "w_gu": w_gu, "w_down": w_down}


precise = lax.Precision.HIGHEST
eps_norm = 1e-06

@jax.custom_vjp
def low(v):
    return lax.optimization_barrier(v.astype(jnp.bfloat16)).astype(jnp.float32)

@jax.custom_vjp
def low_back(v):
    return v

def low_keep(v):
    return (low(v), None)

def low_pass(kept, grad):
    return (grad,)

def back_keep(v):
    return (v, None)

def back_low(kept, grad):
    return (low(grad),)
low.defvjp(low_keep, low_pass)
low_back.defvjp(back_keep, back_low)

def rms_scale(values, gain):
    return values * lax.rsqrt(lax.optimization_barrier(jnp.mean(values * values, axis=-1, keepdims=True)) + eps_norm) * gain

def unit_rows(values):
    return values * lax.rsqrt(lax.optimization_barrier(jnp.sum(values * values, axis=-1, keepdims=True)) + eps_norm)

def matmul(left, right):
    return jnp.einsum('td,df->tf', left, right, precision=precise)

def delta_block(carried, inputs):
    query_rows, key_rows, value_rows, beta_rows, decay_rows, start_rows = inputs
    width = query_rows.shape[0]
    counted = jnp.cumsum(start_rows)
    same_seq = counted[:, None] == counted[None, :]
    keeping = (counted == 0).astype(jnp.float32)
    cumulative = jnp.cumsum(decay_rows, axis=0)
    places = jnp.arange(width)
    lower_eq = (places[:, None] >= places[None, :]) & same_seq
    lower_st = (places[:, None] > places[None, :]) & same_seq
    spread = (cumulative[:, None, :] - cumulative[None, :, :]).transpose(2, 0, 1)
    weights_eq = jnp.where(lower_eq[None], jnp.exp(jnp.where(lower_eq[None], spread, 0.0)), 0.0)
    key_prod = jnp.einsum('ihd,jhd->hij', key_rows, key_rows, precision=precise)
    coupling = jnp.where(lower_st[None], beta_rows.T[:, :, None] * key_prod * weights_eq, 0.0)
    system = coupling + jnp.eye(width, dtype=jnp.float32)
    growth = jnp.exp(cumulative) * keeping[:, None]
    key_state = jnp.einsum('chd,hde->che', key_rows, carried, precision=precise)
    right_side = beta_rows[:, :, None] * (value_rows - growth[:, :, None] * key_state)
    solved = lax.linalg.triangular_solve(system, right_side.transpose(1, 0, 2), left_side=True, lower=True, unit_diagonal=True)
    mixing = jnp.einsum('ihd,jhd->hij', query_rows, key_rows, precision=precise) * weights_eq
    scale = query_rows.shape[2] ** (-0.5)
    outputs = growth[:, :, None] * jnp.einsum('chd,hde->che', query_rows, carried, precision=precise)
    outputs = scale * (outputs + jnp.einsum('hij,hje->ihe', mixing, solved, precision=precise))
    last_row = weights_eq[:, -1, :]
    new_carried = growth[-1][:, None, None] * carried + jnp.einsum('hj,jhd,hje->hde', last_row, key_rows, solved, precision=precise)
    return (new_carried, outputs)

def lane_mixer(lane_pack):
    query_rows, key_rows, value_rows, beta_rows, decay_rows, start_rows = lane_pack
    blocks = query_rows.shape[0] // SPAN

    def in_blocks(array):
        return array.reshape((blocks, SPAN) + array.shape[1:])
    initial = jnp.zeros((H, DK, DV), jnp.float32)
    final_state, outputs = lax.scan(jax.checkpoint(delta_block), initial, (in_blocks(query_rows), in_blocks(key_rows), in_blocks(value_rows), in_blocks(beta_rows), in_blocks(decay_rows), in_blocks(start_rows)))
    return outputs.reshape(GROUP_TOK, H, DV)

def block_forward(lane_tokens, attn_gain, w_in, w_ab, conv_w, decay_log, dt_bias, o_gain, w_out, ffn_gain, w_gu, w_down, start_flags, valid):
    lane_count = lane_tokens.shape[0]
    lane_len = lane_tokens.shape[1]
    normed = low(rms_scale(lane_tokens, attn_gain)).reshape(-1, D)
    proj = low_back(matmul(normed, w_in)).reshape(lane_count, lane_len, -1)
    gates_ab = low_back(matmul(normed, w_ab)).reshape(lane_count, lane_len, 2 * H)
    width_qkv = 2 * HK + HV
    conv_in = low(proj[..., :width_qkv])
    out_gate = proj[..., width_qkv:]
    segment = jnp.cumsum(start_flags, axis=1)
    conv_sum = jnp.zeros_like(conv_in)
    for shift_by in range(CONV):
        rows_back = jnp.pad(conv_in, ((0, 0), (shift_by, 0), (0, 0)))[:, :lane_len]
        seg_back = jnp.pad(segment, ((0, 0), (shift_by, 0)), constant_values=-1)[:, :lane_len]
        conv_sum = conv_sum + conv_w[shift_by] * rows_back * (seg_back == segment).astype(jnp.float32)[..., None]
    act = jax.nn.silu(conv_sum)
    queries = low(unit_rows(act[..., :HK].reshape(lane_count, lane_len, H, DK)))
    keys_all = low(unit_rows(act[..., HK:2 * HK].reshape(lane_count, lane_len, H, DK)))
    values = low(act[..., 2 * HK:].reshape(lane_count, lane_len, H, DV))
    beta = jax.nn.sigmoid(gates_ab[..., H:])
    decay = -jnp.exp(decay_log) * jax.nn.softplus(gates_ab[..., :H] + dt_bias)
    mixed = lax.map(lane_mixer, (queries, keys_all, values, beta, decay, start_flags))
    mixed = mixed * valid[:, :, None, None]
    gated = rms_scale(mixed, o_gain) * jax.nn.silu(out_gate.reshape(lane_count, lane_len, H, DV))
    gated = low(gated.reshape(-1, HV))
    branch = low_back(matmul(gated, w_out))
    resid = lane_tokens.reshape(-1, D) + branch
    normed2 = low(rms_scale(resid, ffn_gain))
    gate_up = low_back(matmul(normed2, w_gu))
    hidden = low(jax.nn.silu(gate_up[:, :FF]) * gate_up[:, FF:])
    return resid + matmul(hidden, w_down)

def reference(tokens, cotangent, dealing, lengths, attn_gain, w_in, w_ab, conv_w, decay_log, dt_bias, o_gain, w_out, ffn_gain, w_gu, w_down):
    per_group = TOK_DEV // N_GROUP
    grid = dealing.reshape(N_GROUP, N_SEQ, N_WSHARD, TOK_DEV)
    one_hot = (grid[..., None] == jnp.arange(N_GROUP, dtype=jnp.int32)).astype(jnp.int32)
    ranks = lax.optimization_barrier(jnp.sum((jnp.cumsum(one_hot, axis=3) - 1) * one_hot, axis=4))
    source_group = jnp.arange(N_GROUP, dtype=jnp.int32)[:, None, None, None]
    seq_place = jnp.arange(N_SEQ, dtype=jnp.int32)[None, :, None, None]
    core_place = jnp.arange(N_WSHARD, dtype=jnp.int32)[None, None, :, None]
    target = (((grid * N_SEQ + seq_place) * N_WSHARD + core_place) * TOK_DEV + source_group * per_group + ranks).reshape(-1).astype(jnp.int32)

    def to_lanes(row_data):
        placed = jnp.zeros_like(row_data).at[target].set(row_data)
        placed = placed.reshape(N_GROUP, N_SEQ, N_WSHARD, TOK_DEV, -1).transpose(0, 2, 1, 3, 4)
        return placed.reshape(LANES, GROUP_TOK, -1)

    def from_lanes(row_data):
        placed = row_data.reshape(N_GROUP, N_WSHARD, N_SEQ, TOK_DEV, -1).transpose(0, 2, 1, 3, 4)
        return placed.reshape(TOKENS, -1)[target]
    lane_lengths = lengths.reshape(LANES, SEQS)
    ends = jnp.cumsum(lane_lengths, axis=1)
    bounds = jnp.concatenate([jnp.zeros((LANES, 1), jnp.int32), ends], axis=1)
    places = jnp.arange(GROUP_TOK, dtype=jnp.int32)
    start_flags = jnp.any(places[None, :, None] == bounds[:, None, :], axis=2).astype(jnp.int32)
    valid = (places[None, :] < ends[:, -1:]).astype(jnp.float32)

    def forward_fn(lane_tokens, attn_f, w_in_f, w_ab_f, conv_f, decay_f, dt_f, o_gain_f, w_out_f, ffn_f, w_gu_f, w_down_f):
        return block_forward(lane_tokens, attn_f, w_in_f, w_ab_f, conv_f, decay_f, dt_f, o_gain_f, w_out_f, ffn_f, w_gu_f, w_down_f, start_flags, valid)
    lane_tokens = to_lanes(tokens.astype(jnp.float32))
    lane_output, pull_back = jax.vjp(forward_fn, lane_tokens, attn_gain.astype(jnp.float32), w_in.astype(jnp.float32), w_ab.astype(jnp.float32), conv_w.astype(jnp.float32), decay_log.astype(jnp.float32), dt_bias.astype(jnp.float32), o_gain.astype(jnp.float32), w_out.astype(jnp.float32), ffn_gain.astype(jnp.float32), w_gu.astype(jnp.float32), w_down.astype(jnp.float32))
    lane_cot = to_lanes(cotangent.astype(jnp.float32)).reshape(-1, D)
    grads = pull_back(lane_cot)
    output = from_lanes(lane_output.reshape(LANES, GROUP_TOK, D)).astype(jnp.bfloat16)
    input_grad = from_lanes(grads[0]).astype(jnp.bfloat16)
    return (output, input_grad, grads[1], grads[2], grads[3], grads[4], grads[5], grads[6], grads[7], grads[8], grads[9], grads[10], grads[11])
```

```python
import functools

import jax
import jax.numpy as jnp
from jax import lax
from jax.experimental import pallas as pl
from jax.experimental.pallas import tpu as pltpu
from jax.sharding import PartitionSpec as P

H = 16
DK = 128
DV = 256
FF = 5632
CONV = 4
SPAN = 64
HK = 2048
HV = 4096
SIDE = 16

bf16 = jnp.bfloat16
f32 = jnp.float32
eps_norm = 1e-06


def mm(left, right, over=((1,), (0,))):
    return lax.dot_general(left, right, (over, ((), ())), preferred_element_type=f32)


def halves(value):
    high = value.astype(bf16)
    return high, (value - high.astype(f32)).astype(bf16)


def mm_right(left, right, over=((1,), (0,))):
    high, low = halves(right)
    return mm(left, high, over) + mm(left, low, over)


def mm_both(left, right, over=((1,), (0,))):
    left_high, left_low = halves(left)
    right_high, right_low = halves(right)
    return (
        mm(left_high, right_high, over)
        + mm(left_low, right_high, over)
        + mm(left_high, right_low, over)
    )


ROWS = ((1,), (1,))
COLS = ((0,), (0,))


def unit_lower_inverse(strict):
    parts = SPAN // 8
    places = lax.broadcasted_iota(jnp.int32, (8, SPAN), 0)
    columns = lax.broadcasted_iota(jnp.int32, (8, SPAN), 1)
    done = [(places + 8 * part == columns).astype(f32) for part in range(parts)]
    for row in range(SPAN - 1):
        first = row // 8
        line = done[first][row - 8 * first : row - 8 * first + 1, :]
        for part in range(first, parts):
            column = strict[8 * part : 8 * part + 8, row : row + 1]
            done[part] = done[part] - column * line
    return jnp.concatenate(done, axis=0)


def block_terms(head, heads, qkv, cols, rows):
    queries = qkv[:, head * DK : (head + 1) * DK]
    keys = qkv[:, (heads + head) * DK : (heads + head + 1) * DK]
    begin = 2 * heads * DK + head * DV
    values = qkv[:, begin : begin + DV]
    cum_c = cols[:, head : head + 1]
    beta_c = cols[:, heads + head : heads + head + 1]
    count_c = cols[:, 2 * heads : 2 * heads + 1]
    cum_r = rows[head : head + 1, :]
    count_r = rows[2 * heads : 2 * heads + 1, :]
    at_i = lax.broadcasted_iota(jnp.int32, (SPAN, SPAN), 0)
    at_j = lax.broadcasted_iota(jnp.int32, (SPAN, SPAN), 1)
    same = count_c == count_r
    lower_eq = same & (at_i >= at_j)
    lower_st = same & (at_i > at_j)
    fall = jnp.where(lower_eq, jnp.exp(jnp.where(lower_eq, cum_c - cum_r, 0.0)), 0.0)
    growth = jnp.where(count_c == 0.0, jnp.exp(cum_c), 0.0)
    last = SPAN - 1
    tail = jnp.where(
        count_c == count_c[last : last + 1, :], jnp.exp(cum_c[last : last + 1, :] - cum_c), 0.0
    )
    return queries, keys, values, beta_c, lower_st, fall, growth, tail, growth[last : last + 1, :]


def mixer_forward_kernel(heads, qkv_ref, cols_ref, rows_ref, mixed_ref, state_ref, inv_ref, solved_ref, carried):
    @pl.when(pl.program_id(0) == 0)
    def _():
        carried[...] = jnp.zeros_like(carried)

    qkv = qkv_ref[...]
    cols = cols_ref[...]
    rows = rows_ref[0]
    scale = DK ** (-0.5)
    for head in range(heads):
        queries, keys, values, beta_c, lower_st, fall, growth, tail, kept = block_terms(
            head, heads, qkv, cols, rows
        )
        state = carried[head]
        state_ref[0, head] = state
        key_prod = mm(keys, keys, ROWS)
        query_prod = mm(queries, keys, ROWS)
        strict = jnp.where(lower_st, beta_c * key_prod * fall, 0.0)
        inverse = unit_lower_inverse(strict)
        inv_ref[0, head] = inverse
        key_state = mm_right(keys, state)
        query_state = mm_right(queries, state)
        right_side = beta_c * (values.astype(f32) - growth * key_state)
        solved = mm_both(inverse, right_side)
        mixed = scale * (growth * query_state + mm_both(query_prod * fall, solved))
        mixed_ref[:, head * DV : (head + 1) * DV] = mixed
        solved_ref[:, head * DV : (head + 1) * DV] = solved
        carried[head] = kept * state + mm_both(tail * keys.astype(f32), solved, COLS)


def mixer_backward_kernel(
    heads, qkv_ref, cols_ref, rows_ref, state_ref, inv_ref, solved_ref, cot_ref, dqkv_ref, dcols_ref, carried
):
    @pl.when(pl.program_id(0) == 0)
    def _():
        carried[...] = jnp.zeros_like(carried)

    qkv = qkv_ref[...]
    cols = cols_ref[...]
    rows = rows_ref[0]
    scale = DK ** (-0.5)
    at_last = lax.broadcasted_iota(jnp.int32, (SPAN, 1), 0) == SPAN - 1
    d_betas, d_cums = [], []
    for head in range(heads):
        queries, keys, values, beta_c, lower_st, fall, growth, tail, kept = block_terms(
            head, heads, qkv, cols, rows
        )
        keys_f = keys.astype(f32)
        queries_f = queries.astype(f32)
        state = state_ref[0, head]
        inverse = inv_ref[0, head]
        solved = solved_ref[:, head * DV : (head + 1) * DV]
        d_mixed = scale * cot_ref[:, head * DV : (head + 1) * DV]
        d_state = carried[head]
        key_prod = mm(keys, keys, ROWS)
        query_prod = mm(queries, keys, ROWS)
        strict = jnp.where(lower_st, beta_c * key_prod * fall, 0.0)
        mixing = query_prod * fall
        key_state = mm_right(keys, state)
        query_state = mm_right(queries, state)
        d_solved = mm_both(mixing, d_mixed, COLS) + mm_both(tail * keys_f, d_state)
        d_right = mm_both(inverse, d_solved, COLS)
        d_mixing = mm_both(d_mixed, solved, ROWS)
        d_query_prod = d_mixing * fall
        d_strict = jnp.where(lower_st, -mm_both(d_right, solved, ROWS), 0.0)
        d_key_prod = d_strict * beta_c * fall
        d_key_state = -(beta_c * growth) * d_right
        d_query = mm_both(growth * d_mixed, state, ROWS) + mm_right(keys, d_query_prod, ((0,), (1,))).T
        both = d_key_prod + d_key_prod.T
        from_tail = mm_both(solved, d_state, ROWS)
        d_key = (
            mm_both(d_key_state, state, ROWS)
            + mm_both(both, keys_f)
            + mm_both(d_query_prod, queries_f, COLS)
            + tail * from_tail
        )
        residual = values.astype(f32) - growth * key_state
        d_betas.append(
            jnp.sum(d_right * residual, axis=1, keepdims=True)
            + jnp.sum(d_strict * key_prod * fall, axis=1, keepdims=True)
        )
        spread = d_strict * strict + d_mixing * mixing
        from_last = tail * jnp.sum(keys_f * from_tail, axis=1, keepdims=True)
        d_growth = jnp.sum(d_mixed * query_state, axis=1, keepdims=True) - beta_c * jnp.sum(
            d_right * key_state, axis=1, keepdims=True
        )
        at_end = jnp.sum(from_last, axis=0, keepdims=True) + kept * jnp.sum(
            jnp.sum(d_state * state, axis=1, keepdims=True), axis=0, keepdims=True
        )
        d_cums.append(
            jnp.sum(spread, axis=1, keepdims=True)
            - jnp.sum(spread.T, axis=1, keepdims=True)
            + growth * d_growth
            - from_last
            + jnp.where(at_last, at_end, 0.0)
        )
        dqkv_ref[:, head * DK : (head + 1) * DK] = d_query
        dqkv_ref[:, (heads + head) * DK : (heads + head + 1) * DK] = d_key
        begin = 2 * heads * DK + head * DV
        dqkv_ref[:, begin : begin + DV] = beta_c * d_right
        carried[head] = (
            kept * d_state
            + mm_both(growth * queries_f, d_mixed, COLS)
            + mm_right(keys, d_key_state, COLS)
        )
    dcols_ref[...] = jnp.concatenate(
        d_betas + d_cums + [jnp.zeros((SPAN, SIDE - 2 * heads), f32)], axis=1
    )


def side_arrays(beta_rows, decay_rows, starts):
    length, heads = beta_rows.shape
    blocks = length // SPAN
    lower = jnp.tril(jnp.ones((SPAN, SPAN), f32))
    running = jnp.einsum(
        "ij,bjh->bih", lower, decay_rows.reshape(blocks, SPAN, heads), precision=lax.Precision.HIGHEST
    )
    counted = jnp.einsum("ij,bj->bi", lower, starts.astype(f32).reshape(blocks, SPAN))
    cols = jnp.concatenate(
        [
            running,
            beta_rows.reshape(blocks, SPAN, heads),
            counted[..., None],
            jnp.zeros((blocks, SPAN, SIDE - 2 * heads - 1), f32),
        ],
        axis=2,
    )
    return cols.reshape(length, SIDE), cols.transpose(0, 2, 1)


def mixer_forward(qkv, cols, rows):
    length, width = qkv.shape
    heads = width // (2 * DK + DV)
    blocks = length // SPAN
    return pl.pallas_call(
        functools.partial(mixer_forward_kernel, heads),
        grid=(blocks,),
        in_specs=[
            pl.BlockSpec((SPAN, width), lambda i: (i, 0)),
            pl.BlockSpec((SPAN, SIDE), lambda i: (i, 0)),
            pl.BlockSpec((1, SIDE, SPAN), lambda i: (i, 0, 0)),
        ],
        out_specs=[
            pl.BlockSpec((SPAN, heads * DV), lambda i: (i, 0)),
            pl.BlockSpec((1, heads, DK, DV), lambda i: (i, 0, 0, 0)),
            pl.BlockSpec((1, heads, SPAN, SPAN), lambda i: (i, 0, 0, 0)),
            pl.BlockSpec((SPAN, heads * DV), lambda i: (i, 0)),
        ],
        out_shape=[
            jax.ShapeDtypeStruct((length, heads * DV), f32),
            jax.ShapeDtypeStruct((blocks, heads, DK, DV), f32),
            jax.ShapeDtypeStruct((blocks, heads, SPAN, SPAN), f32),
            jax.ShapeDtypeStruct((length, heads * DV), f32),
        ],
        scratch_shapes=[pltpu.VMEM((heads, DK, DV), f32)],
        compiler_params=pltpu.CompilerParams(vmem_limit_bytes=32 * 1024 * 1024),
        name="mixer_forward",
    )(qkv, cols, rows)


def mixer_backward(qkv, cols, rows, states, inverses, solved, d_mixed):
    length, width = qkv.shape
    heads = width // (2 * DK + DV)
    blocks = length // SPAN
    end = blocks - 1
    return pl.pallas_call(
        functools.partial(mixer_backward_kernel, heads),
        grid=(blocks,),
        in_specs=[
            pl.BlockSpec((SPAN, width), lambda i: (end - i, 0)),
            pl.BlockSpec((SPAN, SIDE), lambda i: (end - i, 0)),
            pl.BlockSpec((1, SIDE, SPAN), lambda i: (end - i, 0, 0)),
            pl.BlockSpec((1, heads, DK, DV), lambda i: (end - i, 0, 0, 0)),
            pl.BlockSpec((1, heads, SPAN, SPAN), lambda i: (end - i, 0, 0, 0)),
            pl.BlockSpec((SPAN, heads * DV), lambda i: (end - i, 0)),
            pl.BlockSpec((SPAN, heads * DV), lambda i: (end - i, 0)),
        ],
        out_specs=[
            pl.BlockSpec((SPAN, width), lambda i: (end - i, 0)),
            pl.BlockSpec((SPAN, SIDE), lambda i: (end - i, 0)),
        ],
        out_shape=[
            jax.ShapeDtypeStruct((length, width), f32),
            jax.ShapeDtypeStruct((length, SIDE), f32),
        ],
        scratch_shapes=[pltpu.VMEM((heads, DK, DV), f32)],
        compiler_params=pltpu.CompilerParams(vmem_limit_bytes=32 * 1024 * 1024),
        name="mixer_backward",
    )(qkv, cols, rows, states, inverses, solved, d_mixed)


def decay_back(d_cums):
    length, heads = d_cums.shape
    upper = jnp.triu(jnp.ones((SPAN, SPAN), f32))
    return jnp.einsum(
        "ij,bjh->bih",
        upper,
        d_cums.reshape(length // SPAN, SPAN, heads),
        precision=lax.Precision.HIGHEST,
    ).reshape(length, heads)


def rms_scale(values, gain):
    return values * lax.rsqrt(jnp.mean(values * values, axis=-1, keepdims=True) + eps_norm) * gain


def unit_rows(values):
    return values * lax.rsqrt(jnp.sum(values * values, axis=-1, keepdims=True) + eps_norm)


def short_conv(extended, conv_w, segment):
    rows_here = extended.shape[0] - (CONV - 1)
    own_seg = segment[CONV - 1 :]
    conv_sum = jnp.zeros((rows_here, extended.shape[1]), f32)
    for shift_by in range(CONV):
        begin = CONV - 1 - shift_by
        same = (segment[begin : begin + rows_here] == own_seg).astype(f32)
        conv_sum = conv_sum + conv_w[shift_by] * extended[begin : begin + rows_here] * same[:, None]
    return conv_sum


def mixer_inputs(heads, extended, conv_w, segment):
    rows_here = extended.shape[0] - (CONV - 1)
    act = jax.nn.silu(short_conv(extended, conv_w, segment))
    width = heads * DK
    queries = unit_rows(act[:, :width].reshape(rows_here, heads, DK)).reshape(rows_here, -1)
    keys_all = unit_rows(act[:, width : 2 * width].reshape(rows_here, heads, DK)).reshape(
        rows_here, -1
    )
    return jnp.concatenate([queries, keys_all, act[:, 2 * width :]], axis=1)


def decay_inputs(gates_ab, decay_log, dt_bias):
    heads = decay_log.shape[0]
    beta_rows = jax.nn.sigmoid(gates_ab[:, heads:])
    decay_rows = -jnp.exp(decay_log) * jax.nn.softplus(gates_ab[:, :heads] + dt_bias)
    return (beta_rows, decay_rows)


def gated_norm(mixed, out_gate, gain):
    rows_here = mixed.shape[0]
    per_head = mixed.reshape(rows_here, -1, DV)
    gated = rms_scale(per_head, gain) * jax.nn.silu(out_gate.reshape(per_head.shape))
    return gated.reshape(rows_here, -1)


def swiglu(gate_up):
    half = gate_up.shape[1] // 2
    return jax.nn.silu(gate_up[:, :half]) * gate_up[:, half:]


def dot(left, right):
    return jnp.dot(left, right, preferred_element_type=f32)


def dot_t(left, right):
    return lax.dot_general(left, right, (((0,), (0,)), ((), ())), preferred_element_type=f32)


def dot_back(left, right):
    return lax.dot_general(left, right, (((1,), (1,)), ((), ())), preferred_element_type=f32)


SHARDED = ("seq", "wshard")


class Place:
    def __init__(self, rows):
        self.group = lax.axis_size("group")
        self.seq = lax.axis_size("seq")
        self.cores = lax.axis_size("wshard")
        self.part = lax.axis_index("group")
        self.at_seq = lax.axis_index("seq")
        self.core = lax.axis_index("wshard")
        self.rows = rows
        self.per = rows // self.group
        self.subs = self.seq // self.group
        self.sources = self.seq // self.subs
        self.sub = self.at_seq % self.subs
        self.heads = H // self.group
        self.lane = self.seq * rows

    def deal(self, sorted_rows):
        width = sorted_rows.shape[1]
        if self.subs == 1:
            return lax.all_to_all(sorted_rows, "seq", split_axis=0, concat_axis=0, tiled=True)
        sent = jnp.zeros((self.group, self.subs, self.per, width), sorted_rows.dtype)
        sent = lax.dynamic_update_slice(
            sent,
            sorted_rows.reshape(self.group, 1, self.per, width),
            (0, self.at_seq // self.sources, 0, 0),
        )
        got = lax.all_to_all(
            sent.reshape(-1, width), "seq", split_axis=0, concat_axis=0, tiled=True
        )
        return lax.dynamic_slice(got, (self.sub * self.rows, 0), (self.rows, width))

    def undeal(self, rows):
        width = rows.shape[1]
        if self.subs == 1:
            return lax.all_to_all(rows, "seq", split_axis=0, concat_axis=0, tiled=True)
        sent = jnp.zeros((self.subs * self.rows, width), rows.dtype)
        sent = lax.dynamic_update_slice(sent, rows, (self.sub * self.rows, 0))
        got = lax.all_to_all(sent, "seq", split_axis=0, concat_axis=0, tiled=True)
        got = got.reshape(self.group, self.subs, self.per, width)
        got = lax.dynamic_slice(
            got, (0, self.at_seq // self.sources, 0, 0), (self.group, 1, self.per, width)
        )
        return got.reshape(self.rows, width)

    def swap(self, value, turn):
        if turn == 0:
            return value
        return lax.ppermute(value, "group", [(i, i ^ turn) for i in range(self.group)])

    def gather_any(self, rows):
        return jnp.concatenate([self.swap(rows, turn) for turn in range(self.group)], axis=0)

    def reduce_any(self, partial):
        total = partial[: self.rows]
        for turn in range(1, self.group):
            sent = partial[turn * self.rows : (turn + 1) * self.rows].astype(bf16)
            total = total + self.swap(sent, turn).astype(f32)
        return total

    def gather_places(self, rows):
        width = rows.shape[1]
        lane = jnp.zeros((self.sources, self.group, self.per, width), rows.dtype)
        for turn in range(self.group):
            got = self.swap(rows, turn).reshape(self.sources, 1, self.per, width)
            lane = lax.dynamic_update_slice(lane, got, (0, self.part ^ turn, 0, 0))
        return lane.reshape(-1, width)

    def reduce_places(self, partial):
        width = partial.shape[1]
        lane = partial.reshape(self.sources, self.group, self.per, width)
        total = None
        for turn in range(self.group):
            mine = lax.dynamic_slice(
                lane, (0, self.part ^ turn, 0, 0), (self.sources, 1, self.per, width)
            ).reshape(self.rows, width)
            if turn == 0:
                total = mine
            else:
                total = total + self.swap(mine.astype(bf16), turn).astype(f32)
        return total

    def gather_parts(self, value):
        parts = jnp.zeros((self.group,) + value.shape, value.dtype)
        for turn in range(self.group):
            parts = lax.dynamic_update_slice(
                parts, self.swap(value, turn)[None], (self.part ^ turn,) + (0,) * value.ndim
            )
        return parts

    def to_lane(self, rows):
        if self.subs == 1:
            return rows
        every = lax.all_gather(rows, "seq", axis=0, tiled=True)
        length = rows.shape[0] * self.subs
        return lax.dynamic_slice(
            every, ((self.at_seq // self.subs) * length, 0), (length, rows.shape[1])
        )

    def to_own(self, lane_rows):
        if self.subs == 1:
            return lane_rows
        length = lane_rows.shape[0] // self.subs
        return lax.dynamic_slice(lane_rows, (self.sub * length, 0), (length, lane_rows.shape[1]))

    def head_columns(self, array, sections):
        pieces = []
        for begin, width in sections:
            for turn in range(self.heads):
                pieces.append(
                    lax.dynamic_slice(
                        array,
                        (0, begin + (turn * self.group + self.part) * width),
                        (array.shape[0], width),
                    )
                )
        return jnp.concatenate(pieces, axis=1)

    def join_heads(self, parts, sections):
        group, rows = parts.shape[:2]
        out, begin = [], 0
        for _, width in sections:
            section = parts[:, :, begin : begin + self.heads * width]
            begin += self.heads * width
            section = section.reshape(group, rows, self.heads, width).transpose(1, 2, 0, 3)
            out.append(section.reshape(rows, self.heads * group * width))
        return jnp.concatenate(out, axis=1)

    def hidden_columns(self, array, unit_rows_here):
        rows = array.shape[0]
        blocks = self.seq * self.cores
        piece = unit_rows_here // self.group
        split = array.reshape(rows, 2 * blocks, self.group, piece)
        mine = lax.dynamic_slice(split, (0, 0, self.part, 0), (rows, 2 * blocks, 1, piece))
        return mine.reshape(rows, 2 * blocks * piece)

    def join_hidden(self, parts, unit_rows_here):
        group, rows = parts.shape[:2]
        blocks = self.seq * self.cores
        piece = unit_rows_here // group
        split = parts.reshape(group, rows, 2 * blocks, piece).transpose(1, 2, 0, 3)
        return split.reshape(rows, 2 * blocks * group * piece)

    def out_rows(self, w_out):
        width = w_out.shape[1]
        if self.subs == 1 and self.cores == 2:
            mine = lax.dynamic_slice(w_out, ((self.part % 2) * DV, 0), (DV, width))
            half = DV // 2
            kept = lax.dynamic_slice(mine, (self.core * half, 0), (half, width))
            other = lax.dynamic_slice(mine, ((1 - self.core) * half, 0), (half, width))
            got = lax.ppermute(other, "wshard", [(0, 1), (1, 0)])
            piece = jnp.where(self.core == self.part // 2, kept, got)
            return lax.all_gather(piece, SHARDED, axis=0, tiled=True)
        every = lax.all_gather(w_out, SHARDED, axis=0, tiled=True)
        every = every.reshape(self.heads, self.group, DV, width)
        return lax.dynamic_slice(
            every, (0, self.part, 0, 0), (self.heads, 1, DV, width)
        ).reshape(-1, width)

    def out_rows_back(self, grad):
        width = grad.shape[1]
        grad = grad.astype(bf16)
        if self.subs == 1 and self.cores == 2:
            half = lax.psum_scatter(grad, SHARDED, scatter_dimension=0, tiled=True)
            halves_all = self.gather_parts(half)
            here = lax.dynamic_slice(halves_all, (2 * self.core, 0, 0), (2, DV // 2, width))
            there = lax.dynamic_slice(halves_all, (2 - 2 * self.core, 0, 0), (2, DV // 2, width))
            got = lax.ppermute(there, "wshard", [(0, 1), (1, 0)])
            first = jnp.where(self.core == 0, here, got)
            second = jnp.where(self.core == 0, got, here)
            return jnp.stack([first, second], axis=1).reshape(2 * DV, width).astype(f32)
        every = jnp.zeros((self.heads, self.group, DV, width), bf16)
        every = lax.dynamic_update_slice(
            every, grad.reshape(self.heads, 1, DV, width), (0, self.part, 0, 0)
        )
        shard = lax.psum_scatter(every.reshape(-1, width), SHARDED, scatter_dimension=0, tiled=True)
        return lax.psum(shard, "group").astype(f32)


QKV = ((0, DK), (HK, DK), (2 * HK, DV))
GATE = ((2 * HK + HV, DV),)


def segment_info(lane_lengths, length):
    ends = jnp.cumsum(lane_lengths)
    bounds = jnp.concatenate([jnp.zeros((1,), jnp.int32), ends])
    places = jnp.arange(-(CONV - 1), length, dtype=jnp.int32)
    segment = jnp.sum((places[:, None] >= bounds[None, :]).astype(jnp.int32), axis=1)
    segment = jnp.where(places >= 0, segment, -1)
    own_places = places[CONV - 1 :]
    starts = jnp.any(own_places[:, None] == bounds[None, :], axis=1).astype(jnp.int32)
    valid = (own_places < ends[-1]).astype(f32)
    return (segment, starts, valid)


def shards(
    tokens,
    cotangent,
    dealing,
    lengths,
    attn_gain,
    w_in,
    w_ab,
    conv_w,
    decay_log,
    dt_bias,
    o_gain,
    w_out,
    ffn_gain,
    w_gu,
    w_down,
):
    rows, width = tokens.shape
    at = Place(rows)
    heads = at.heads
    device_rows = w_down.shape[0]
    devices = at.seq * at.cores

    small = (attn_gain, ffn_gain, o_gain, w_ab.reshape(-1), conv_w.reshape(-1))
    packed = lax.all_gather(jnp.concatenate(small), SHARDED, axis=0).reshape(devices, -1)
    full, begin = [], 0
    for array in small:
        full.append(packed[:, begin : begin + array.shape[0]])
        begin += array.shape[0]
    attn_f, ffn_f, o_f = (array.reshape(-1).astype(f32) for array in full[:3])
    ab_all = full[3].reshape(width, 2, heads, at.group)
    ab_mine = lax.dynamic_slice(ab_all, (0, 0, 0, at.part), (width, 2, heads, 1)).reshape(width, -1)
    conv_all = full[4].reshape(devices, CONV, -1).transpose(1, 0, 2).reshape(CONV, -1)
    conv_mine = at.head_columns(conv_all, QKV).astype(f32)

    def my_heads(values):
        return lax.dynamic_slice(values.reshape(heads, at.group), (0, at.part), (heads, 1)).reshape(-1)

    decay_mine, dt_mine = my_heads(decay_log), my_heads(dt_bias)

    in_qkv = lax.all_gather(at.head_columns(w_in, QKV), SHARDED, axis=0, tiled=True)
    in_gate = lax.all_gather(at.head_columns(w_in, GATE), SHARDED, axis=0, tiled=True)
    out_mine = at.out_rows(w_out)
    gu_mine = lax.all_gather(at.hidden_columns(w_gu, device_rows), SHARDED, axis=0, tiled=True)
    piece = device_rows // at.group
    down_mine = lax.all_gather(
        lax.dynamic_slice(w_down, (at.part * piece, 0), (piece, width)), SHARDED, axis=0, tiled=True
    )

    member = (dealing[:, None] == jnp.arange(at.group, dtype=jnp.int32)[None, :]).astype(jnp.int32)
    before = lax.dot_general(
        jnp.tril(jnp.ones((rows, rows), f32), -1).astype(bf16),
        member.astype(bf16),
        (((1,), (0,)), ((), ())),
        preferred_element_type=f32,
    ).astype(jnp.int32)
    target = jnp.sum((before + at.per * jnp.arange(at.group, dtype=jnp.int32)) * member, axis=1)
    sorting = (target[None, :] == jnp.arange(rows, dtype=jnp.int32)[:, None]).astype(bf16)
    dealt = at.deal(dot(sorting, jnp.concatenate([tokens, cotangent], axis=1)).astype(bf16))
    tokens_f = dealt[:, :width].astype(f32)
    cot_own = dealt[:, width:]
    cot_all = at.gather_any(cot_own)

    lane_lengths = lax.dynamic_index_in_dim(
        at.gather_parts(lengths.reshape(-1)), at.at_seq // at.subs, 0, keepdims=False
    )
    segment, starts, valid_lane = segment_info(lane_lengths, at.lane)
    valid = at.to_own(valid_lane[:, None])
    normed = rms_scale(tokens_f, attn_f).astype(bf16)
    normed_all = at.gather_places(normed)
    conv_in = dot(normed_all, in_qkv).astype(bf16)
    gates_ab = dot(normed_all, ab_mine)
    out_gate = dot(normed_all, in_gate)
    extended = jnp.pad(at.to_lane(conv_in), ((CONV - 1, 0), (0, 0))).astype(f32)
    qkv_f, pull_conv = jax.vjp(
        lambda extended_in, conv_in_w: mixer_inputs(heads, extended_in, conv_in_w, segment),
        extended,
        conv_mine,
    )
    qkv = qkv_f.astype(bf16)
    (beta_rows, decay_rows), pull_decay = jax.vjp(decay_inputs, gates_ab, decay_mine, dt_mine)
    cols, side_rows = side_arrays(at.to_lane(beta_rows), at.to_lane(decay_rows), starts)
    mixed_lane, states, inverses, solved = mixer_forward(qkv, cols, side_rows)
    mixed = at.to_own(mixed_lane) * valid
    gated_f, pull_gate = jax.vjp(gated_norm, mixed, out_gate, o_f)
    gated = gated_f.astype(bf16)
    branch = at.reduce_places(dot(gated, out_mine))
    resid = tokens_f + branch

    normed2_f, pull_norm2 = jax.vjp(rms_scale, resid, ffn_f)
    normed2_all = at.gather_any(normed2_f.astype(bf16))
    gate_up = dot(normed2_all, gu_mine)
    hidden_f, pull_ffn = jax.vjp(swiglu, gate_up)
    hidden = hidden_f.astype(bf16)
    output = (resid + at.reduce_any(dot(hidden, down_mine))).astype(bf16)

    d_hidden = dot_back(cot_all, down_mine)
    d_gate_up = pull_ffn(d_hidden)[0].astype(bf16)
    d_down = dot_t(hidden, cot_all)
    d_gu = dot_t(normed2_all, d_gate_up)
    d_normed2 = at.reduce_any(dot_back(d_gate_up, gu_mine))
    d_resid_norm, d_ffn_gain = pull_norm2(d_normed2)
    d_resid = cot_own.astype(f32) + d_resid_norm
    down_shard = lax.psum_scatter(d_down.astype(bf16), SHARDED, scatter_dimension=0, tiled=True)
    gu_shard = lax.psum_scatter(d_gu.astype(bf16), SHARDED, scatter_dimension=0, tiled=True)

    d_branch_all = at.gather_places(d_resid.astype(bf16))
    d_gated = dot_back(d_branch_all, out_mine)
    grad_w_out = at.out_rows_back(dot_t(gated, d_branch_all))
    d_mixed, d_out_gate, d_o_gain = pull_gate(d_gated)
    d_gate_cols = d_out_gate.astype(bf16)
    gate_shard = lax.psum_scatter(
        dot_t(normed_all, d_gate_cols).astype(bf16), SHARDED, scatter_dimension=0, tiled=True
    )
    d_qkv, d_cols = mixer_backward(
        qkv, cols, side_rows, states, inverses, solved, at.to_lane(d_mixed * valid)
    )
    d_beta = at.to_own(d_cols[:, :heads])
    d_decay = at.to_own(decay_back(d_cols[:, heads : 2 * heads]))
    d_extended, d_conv_w = pull_conv(d_qkv)
    d_conv_w = d_conv_w * (at.sub == 0).astype(f32)
    d_conv_in = at.to_own(d_extended[CONV - 1 :]).astype(bf16)
    d_gates_ab, d_decay_log, d_dt_bias = pull_decay((d_beta, d_decay))
    d_ab = d_gates_ab.astype(bf16)
    d_in = dot_t(normed_all, d_conv_in)
    d_w_ab = dot_t(normed_all, d_ab)
    d_normed = at.reduce_places(
        dot_back(d_conv_in, in_qkv) + dot_back(d_gate_cols, in_gate) + dot_back(d_ab, ab_mine)
    )
    value_norm, pull_norm = jax.vjp(rms_scale, tokens_f, attn_f)
    d_tokens_norm, d_attn_gain = pull_norm(d_normed)
    d_tokens = (d_resid + d_tokens_norm).astype(bf16)
    in_shard = lax.psum_scatter(d_in.astype(bf16), SHARDED, scatter_dimension=0, tiled=True)

    returned = at.undeal(jnp.concatenate([output, d_tokens], axis=1))
    returned = dot_t(sorting, returned).astype(bf16)

    grad_w_down = at.gather_parts(down_shard).reshape(device_rows, width).astype(f32)
    grad_w_gu = at.join_hidden(at.gather_parts(gu_shard), device_rows).astype(f32)
    grad_w_in = jnp.concatenate(
        [
            at.join_heads(at.gather_parts(in_shard), QKV),
            at.join_heads(at.gather_parts(gate_shard), GATE),
        ],
        axis=1,
    ).astype(f32)

    mine = (jnp.arange(at.group) == at.part).astype(f32)

    def own_columns(array, piece_width):
        count = array.shape[0]
        spread = array.reshape(count, heads, 1, piece_width) * mine[:, None]
        return spread.reshape(count, -1)

    conv_parts = [
        own_columns(d_conv_w[:, : heads * DK], DK),
        own_columns(d_conv_w[:, heads * DK : 2 * heads * DK], DK),
        own_columns(d_conv_w[:, 2 * heads * DK :], DV),
    ]
    totals = (
        d_attn_gain,
        d_ffn_gain,
        d_o_gain,
        jnp.concatenate(conv_parts, axis=1).reshape(-1),
        own_columns(d_w_ab.reshape(-1, heads), 1).reshape(-1),
        own_columns(d_decay_log[None], 1).reshape(-1),
        own_columns(d_dt_bias[None], 1).reshape(-1),
    )
    sizes = [array.shape[0] for array in totals]
    summed = lax.psum(jnp.concatenate(totals), ("group", "seq", "wshard"))
    parts, begin = [], 0
    for size in sizes:
        parts.append(summed[begin : begin + size])
        begin += size
    me = at.at_seq * at.cores + at.core

    def own_rows(array, axis=0):
        count = array.shape[axis] // devices
        return lax.dynamic_slice_in_dim(array, me * count, count, axis)

    return (
        returned[:, :width],
        returned[:, width:],
        own_rows(parts[0]),
        grad_w_in,
        own_rows(parts[4].reshape(width, 2 * H)),
        own_rows(parts[3].reshape(CONV, -1), 1),
        parts[5],
        parts[6],
        own_rows(parts[2]),
        grad_w_out,
        own_rows(parts[1]),
        grad_w_gu,
        grad_w_down,
    )


def solution(mesh):
    placed = (
        P(("group", "seq", "wshard"), None),
        P(("group", "seq", "wshard"), None),
        P(("group", "seq", "wshard")),
        P("group", "wshard", None),
        P(("seq", "wshard")),
        P(("seq", "wshard"), None),
        P(("seq", "wshard"), None),
        P(None, ("seq", "wshard")),
        P(),
        P(),
        P(("seq", "wshard")),
        P(("seq", "wshard"), None),
        P(("seq", "wshard")),
        P(("seq", "wshard"), None),
        P(("seq", "wshard"), None),
    )
    return jax.shard_map(
        shards,
        mesh=mesh,
        in_specs=placed,
        out_specs=(
            P(("group", "seq", "wshard"), None),
            P(("group", "seq", "wshard"), None),
            P(("seq", "wshard")),
            P(("seq", "wshard"), None),
            P(("seq", "wshard"), None),
            P(None, ("seq", "wshard")),
            P(),
            P(),
            P(("seq", "wshard")),
            P(("seq", "wshard"), None),
            P(("seq", "wshard")),
            P(("seq", "wshard"), None),
            P(("seq", "wshard"), None),
        ),
        check_vma=False,
    )
```

```python
import functools

import jax
import jax.numpy as jnp
from jax import lax
from jax.experimental import pallas as pl
from jax.experimental.pallas import tpu as pltpu
from jax.sharding import PartitionSpec as P

H = 16
DK = 128
DV = 256
FF = 5632
CONV = 4
SPAN = 64
HK = 2048
HV = 4096
SIDE = 16

bf16 = jnp.bfloat16
f32 = jnp.float32
eps_norm = 1e-06


def mm(left, right, over=((1,), (0,))):
    return lax.dot_general(left, right, (over, ((), ())), preferred_element_type=f32)


def halves(value):
    high = value.astype(bf16)
    return high, (value - high.astype(f32)).astype(bf16)


def mm_right(left, right, over=((1,), (0,))):
    high, low = halves(right)
    return mm(left, high, over) + mm(left, low, over)


def mm_both(left, right, over=((1,), (0,))):
    left_high, left_low = halves(left)
    right_high, right_low = halves(right)
    return (
        mm(left_high, right_high, over)
        + mm(left_low, right_high, over)
        + mm(left_high, right_low, over)
    )


ROWS = ((1,), (1,))
COLS = ((0,), (0,))


def unit_lower_inverse(strict):
    parts = SPAN // 8
    places = lax.broadcasted_iota(jnp.int32, (8, SPAN), 0)
    columns = lax.broadcasted_iota(jnp.int32, (8, SPAN), 1)
    done = [(places + 8 * part == columns).astype(f32) for part in range(parts)]
    for row in range(SPAN - 1):
        first = row // 8
        line = done[first][row - 8 * first : row - 8 * first + 1, :]
        for part in range(first, parts):
            column = strict[8 * part : 8 * part + 8, row : row + 1]
            done[part] = done[part] - column * line
    return jnp.concatenate(done, axis=0)


def silu_parts(value):
    rate = 1.0 / (1.0 + jnp.exp(-value))
    return value * rate, rate


def gate_terms(heads, gates, decay_log, dt_bias):
    shifted = gates[:, :heads] + dt_bias
    beta = 1.0 / (1.0 + jnp.exp(-gates[:, heads:]))
    soft = jnp.maximum(shifted, 0.0) + jnp.log1p(jnp.exp(-jnp.abs(shifted)))
    return shifted, beta, -jnp.exp(decay_log) * soft


def ones_left(ones, value):
    high, rest = halves(value)
    high_f = high.astype(f32)
    rest, low = halves(value - high_f)
    return mm(ones, high) + mm(ones, rest) + mm(ones, low)


def triangle(upper):
    at_i = lax.broadcasted_iota(jnp.int32, (SPAN, SPAN), 0)
    at_j = lax.broadcasted_iota(jnp.int32, (SPAN, SPAN), 1)
    return jnp.where(at_i <= at_j if upper else at_i >= at_j, 1.0, 0.0).astype(bf16)


def side_columns(heads, gates, side, decay_log, dt_bias):
    shifted, beta, decay = gate_terms(heads, gates, decay_log, dt_bias)
    running = ones_left(triangle(False), decay)
    cols = jnp.concatenate(
        [running, beta, side[:, :1], jnp.zeros((SPAN, 128 - 2 * heads - 1), f32)], axis=1
    )
    return cols, cols.T, shifted, beta, decay


def conv_forward(current, before, taps, side):
    extended = jnp.concatenate([before, current], axis=0)
    total = taps[0:1, :] * current
    for back in range(1, CONV):
        total = total + taps[back : back + 1, :] * (
            extended[8 - back : 8 - back + SPAN, :] * side[:, back : back + 1]
        )
    return total


def block_terms(head, heads, cols, rows):
    cum_c = cols[:, head : head + 1]
    beta_c = cols[:, heads + head : heads + head + 1]
    count_c = cols[:, 2 * heads : 2 * heads + 1]
    cum_r = rows[head : head + 1, :]
    count_r = rows[2 * heads : 2 * heads + 1, :]
    at_i = lax.broadcasted_iota(jnp.int32, (SPAN, SPAN), 0)
    at_j = lax.broadcasted_iota(jnp.int32, (SPAN, SPAN), 1)
    same = count_c == count_r
    lower_eq = same & (at_i >= at_j)
    lower_st = same & (at_i > at_j)
    fall = jnp.where(lower_eq, jnp.exp(jnp.where(lower_eq, cum_c - cum_r, 0.0)), 0.0)
    growth = jnp.where(count_c == 0.0, jnp.exp(cum_c), 0.0)
    last = SPAN - 1
    tail = jnp.where(
        count_c == count_c[last : last + 1, :], jnp.exp(cum_c[last : last + 1, :] - cum_c), 0.0
    )
    return beta_c, lower_st, fall, growth, tail, growth[last : last + 1, :]


def mixer_forward_kernel(
    heads,
    conv_ref,
    gate_ref,
    gates_ref,
    side_ref,
    taps_ref,
    gain_ref,
    log_ref,
    bias_ref,
    gated_ref,
    mixed_ref,
    qkv_ref,
    state_ref,
    inv_ref,
    solved_ref,
    carried,
    before,
):
    @pl.when(pl.program_id(0) == 0)
    def _():
        carried[...] = jnp.zeros_like(carried)
        before[...] = jnp.zeros_like(before)

    side = side_ref[...]
    current = conv_ref[...].astype(f32)
    act, _ = silu_parts(conv_forward(current, before[...], taps_ref[...], side))
    before[...] = current[SPAN - 8 :, :]
    cols, rows, _, _, _ = side_columns(heads, gates_ref[...], side, log_ref[...], bias_ref[...])
    valid = side[:, CONV : CONV + 1]
    gain = gain_ref[...]
    scale = DK ** (-0.5)
    for head in range(heads):
        beta_c, lower_st, fall, growth, tail, kept = block_terms(head, heads, cols, rows)
        unit = []
        for begin in (head * DK, (heads + head) * DK):
            row = act[:, begin : begin + DK]
            row = row * lax.rsqrt(jnp.sum(row * row, axis=1, keepdims=True) + eps_norm)
            row = row.astype(bf16)
            qkv_ref[:, begin : begin + DK] = row
            unit.append(row)
        queries, keys = unit
        begin = 2 * heads * DK + head * DV
        values = act[:, begin : begin + DV].astype(bf16)
        qkv_ref[:, begin : begin + DV] = values
        state = carried[head]
        state_ref[0, head] = state
        key_prod = mm(keys, keys, ROWS)
        query_prod = mm(queries, keys, ROWS)
        strict = jnp.where(lower_st, beta_c * key_prod * fall, 0.0)
        inverse = unit_lower_inverse(strict)
        inv_ref[0, head] = inverse
        key_state = mm_right(keys, state)
        query_state = mm_right(queries, state)
        right_side = beta_c * (values.astype(f32) - growth * key_state)
        solved = mm_both(inverse, right_side)
        mixed = scale * (growth * query_state + mm_both(query_prod * fall, solved)) * valid
        part = slice(head * DV, (head + 1) * DV)
        mixed_ref[:, part] = mixed
        solved_ref[:, part] = solved
        carried[head] = kept * state + mm_both(tail * keys.astype(f32), solved, COLS)
        shrink = lax.rsqrt(jnp.mean(mixed * mixed, axis=1, keepdims=True) + eps_norm)
        open_gate, _ = silu_parts(gate_ref[:, part])
        gated_ref[:, part] = (mixed * shrink * gain * open_gate).astype(bf16)


def mixer_backward_kernel(
    heads,
    conv_ref,
    ahead_ref,
    gate_ref,
    gates_ref,
    side_ref,
    taps_ref,
    gain_ref,
    log_ref,
    bias_ref,
    mixed_ref,
    qkv_ref,
    state_ref,
    inv_ref,
    solved_ref,
    cot_ref,
    dconv_ref,
    dgate_ref,
    dgates_ref,
    dtaps_ref,
    dgain_ref,
    dheads_ref,
    carried,
    after,
    after_side,
):
    @pl.when(pl.program_id(0) == 0)
    def _():
        carried[...] = jnp.zeros_like(carried)
        after[...] = jnp.zeros_like(after)
        after_side[...] = jnp.zeros_like(after_side)
        dtaps_ref[...] = jnp.zeros_like(dtaps_ref)
        dgain_ref[...] = jnp.zeros_like(dgain_ref)
        dheads_ref[...] = jnp.zeros_like(dheads_ref)

    side = side_ref[...]
    taps = taps_ref[...]
    gain = gain_ref[...]
    valid = side[:, CONV : CONV + 1]
    current = conv_ref[...].astype(f32)
    ahead = ahead_ref[8:, :].astype(f32)
    conv_out = conv_forward(current, ahead, taps, side)
    act, rate = silu_parts(conv_out)
    slope = rate * (1.0 + conv_out * (1.0 - rate))
    cols, rows, shifted, beta_all, decay_all = side_columns(
        heads, gates_ref[...], side, log_ref[...], bias_ref[...]
    )
    scale = DK ** (-0.5)
    at_last = lax.broadcasted_iota(jnp.int32, (SPAN, 1), 0) == SPAN - 1
    d_betas, d_cums = [], []
    d_queries, d_keys, d_values = [], [], []
    d_gain = jnp.zeros((1, DV), f32)
    for head in range(heads):
        beta_c, lower_st, fall, growth, tail, kept = block_terms(head, heads, cols, rows)
        part = slice(head * DV, (head + 1) * DV)
        mixed = mixed_ref[:, part]
        gate = gate_ref[:, part]
        d_gated = cot_ref[:, part]
        shrink = lax.rsqrt(jnp.mean(mixed * mixed, axis=1, keepdims=True) + eps_norm)
        normal = mixed * shrink
        open_gate, gate_rate = silu_parts(gate)
        with_normal = d_gated * normal
        d_gain = d_gain + jnp.sum(with_normal * open_gate, axis=0, keepdims=True)
        dgate_ref[:, part] = (
            with_normal * gain * (gate_rate * (1.0 + gate * (1.0 - gate_rate)))
        ).astype(bf16)
        d_normal = d_gated * gain * open_gate
        d_mixed = shrink * (d_normal - normal * jnp.mean(d_normal * normal, axis=1, keepdims=True))
        d_mixed = (scale * valid) * d_mixed
        queries = qkv_ref[:, head * DK : (head + 1) * DK]
        keys = qkv_ref[:, (heads + head) * DK : (heads + head + 1) * DK]
        begin = 2 * heads * DK + head * DV
        values = qkv_ref[:, begin : begin + DV]
        keys_f = keys.astype(f32)
        queries_f = queries.astype(f32)
        state = state_ref[0, head]
        inverse = inv_ref[0, head]
        solved = solved_ref[:, part]
        d_state = carried[head]
        key_prod = mm(keys, keys, ROWS)
        query_prod = mm(queries, keys, ROWS)
        strict = jnp.where(lower_st, beta_c * key_prod * fall, 0.0)
        mixing = query_prod * fall
        key_state = mm_right(keys, state)
        query_state = mm_right(queries, state)
        d_solved = mm_both(mixing, d_mixed, COLS) + mm_both(tail * keys_f, d_state)
        d_right = mm_both(inverse, d_solved, COLS)
        d_mixing = mm_both(d_mixed, solved, ROWS)
        d_query_prod = d_mixing * fall
        d_strict = jnp.where(lower_st, -mm_both(d_right, solved, ROWS), 0.0)
        d_key_prod = d_strict * beta_c * fall
        d_key_state = -(beta_c * growth) * d_right
        d_query = mm_both(growth * d_mixed, state, ROWS) + mm_both(d_query_prod, keys_f)
        both = d_key_prod + d_key_prod.T
        from_tail = mm_both(solved, d_state, ROWS)
        d_key = (
            mm_both(d_key_state, state, ROWS)
            + mm_both(both, keys_f)
            + mm_both(d_query_prod, queries_f, COLS)
            + tail * from_tail
        )
        residual = values.astype(f32) - growth * key_state
        d_betas.append(
            jnp.sum(d_right * residual, axis=1, keepdims=True)
            + jnp.sum(d_strict * key_prod * fall, axis=1, keepdims=True)
        )
        spread = d_strict * strict + d_mixing * mixing
        from_last = tail * jnp.sum(keys_f * from_tail, axis=1, keepdims=True)
        d_growth = jnp.sum(d_mixed * query_state, axis=1, keepdims=True) - beta_c * jnp.sum(
            d_right * key_state, axis=1, keepdims=True
        )
        at_end = jnp.sum(from_last, axis=0, keepdims=True) + kept * jnp.sum(
            jnp.sum(d_state * state, axis=1, keepdims=True), axis=0, keepdims=True
        )
        d_cums.append(
            jnp.sum(spread, axis=1, keepdims=True)
            - jnp.sum(spread.T, axis=1, keepdims=True)
            + growth * d_growth
            - from_last
            + jnp.where(at_last, at_end, 0.0)
        )
        carried[head] = (
            kept * d_state
            + mm_both(growth * queries_f, d_mixed, COLS)
            + mm_right(keys, d_key_state, COLS)
        )
        for grads, grad, start in ((d_queries, d_query, head * DK), (d_keys, d_key, (heads + head) * DK)):
            row = act[:, start : start + DK]
            small = lax.rsqrt(jnp.sum(row * row, axis=1, keepdims=True) + eps_norm)
            along = jnp.sum(row * grad, axis=1, keepdims=True) * small * small
            grads.append(small * (grad - row * along))
        d_values.append(beta_c * d_right)
    dgain_ref[...] += d_gain
    d_conv = jnp.concatenate(d_queries + d_keys + d_values, axis=1) * slope
    extended = jnp.concatenate([ahead, current], axis=0)
    later, later_side = after[...], after_side[...]
    d_in = taps[0:1, :] * d_conv
    d_taps = [jnp.sum(d_conv * current, axis=0, keepdims=True)]
    for back in range(1, CONV):
        masked = d_conv * side[:, back : back + 1]
        d_taps.append(
            jnp.sum(masked * extended[8 - back : 8 - back + SPAN, :], axis=0, keepdims=True)
        )
        reach = jnp.concatenate([masked, later * later_side[:, back : back + 1]], axis=0)
        d_in = d_in + taps[back : back + 1, :] * reach[back : back + SPAN, :]
    dtaps_ref[...] += jnp.concatenate(d_taps, axis=0)
    dconv_ref[...] = d_in.astype(bf16)
    after[...] = d_conv[:8, :]
    after_side[...] = side[:8, :]
    d_decay = ones_left(triangle(True), jnp.concatenate(d_cums, axis=1))
    d_beta = jnp.concatenate(d_betas, axis=1)
    d_shifted = -d_decay * jnp.exp(log_ref[...]) / (1.0 + jnp.exp(-shifted))
    dgates_ref[...] = jnp.concatenate([d_shifted, d_beta * beta_all * (1.0 - beta_all)], axis=1)
    dheads_ref[...] += jnp.concatenate(
        [
            jnp.sum(d_decay * decay_all, axis=0, keepdims=True),
            jnp.sum(d_shifted, axis=0, keepdims=True),
        ],
        axis=1,
    )


def whole_block(shape):
    return pl.BlockSpec(shape, lambda i: (0,) * len(shape))


MIXER_PARAMS = pltpu.CompilerParams(vmem_limit_bytes=48 * 1024 * 1024)


def mixer_forward(conv_in, out_gate, gates, side, taps, gain, decay_log, dt_bias):
    length, width = conv_in.shape
    heads = decay_log.shape[1]
    blocks = length // SPAN
    return pl.pallas_call(
        functools.partial(mixer_forward_kernel, heads),
        grid=(blocks,),
        in_specs=[
            pl.BlockSpec((SPAN, width), lambda i: (i, 0)),
            pl.BlockSpec((SPAN, heads * DV), lambda i: (i, 0)),
            pl.BlockSpec((SPAN, 2 * heads), lambda i: (i, 0)),
            pl.BlockSpec((SPAN, SIDE), lambda i: (i, 0)),
            whole_block((CONV, width)),
            whole_block((1, DV)),
            whole_block((1, heads)),
            whole_block((1, heads)),
        ],
        out_specs=[
            pl.BlockSpec((SPAN, heads * DV), lambda i: (i, 0)),
            pl.BlockSpec((SPAN, heads * DV), lambda i: (i, 0)),
            pl.BlockSpec((SPAN, width), lambda i: (i, 0)),
            pl.BlockSpec((1, heads, DK, DV), lambda i: (i, 0, 0, 0)),
            pl.BlockSpec((1, heads, SPAN, SPAN), lambda i: (i, 0, 0, 0)),
            pl.BlockSpec((SPAN, heads * DV), lambda i: (i, 0)),
        ],
        out_shape=[
            jax.ShapeDtypeStruct((length, heads * DV), bf16),
            jax.ShapeDtypeStruct((length, heads * DV), f32),
            jax.ShapeDtypeStruct((length, width), bf16),
            jax.ShapeDtypeStruct((blocks, heads, DK, DV), f32),
            jax.ShapeDtypeStruct((blocks, heads, SPAN, SPAN), f32),
            jax.ShapeDtypeStruct((length, heads * DV), f32),
        ],
        scratch_shapes=[pltpu.VMEM((heads, DK, DV), f32), pltpu.VMEM((8, width), f32)],
        compiler_params=MIXER_PARAMS,
        name="mixer_forward",
    )(conv_in, out_gate, gates, side, taps, gain, decay_log, dt_bias)


def mixer_backward(conv_in, out_gate, gates, side, taps, gain, decay_log, dt_bias, kept, d_gated):
    length, width = conv_in.shape
    heads = decay_log.shape[1]
    blocks = length // SPAN
    end = blocks - 1
    ahead_rows = 16
    per = SPAN // ahead_rows
    return pl.pallas_call(
        functools.partial(mixer_backward_kernel, heads),
        grid=(blocks,),
        in_specs=[
            pl.BlockSpec((SPAN, width), lambda i: (end - i, 0)),
            pl.BlockSpec((ahead_rows, width), lambda i: (jnp.maximum((end - i) * per - 1, 0), 0)),
            pl.BlockSpec((SPAN, heads * DV), lambda i: (end - i, 0)),
            pl.BlockSpec((SPAN, 2 * heads), lambda i: (end - i, 0)),
            pl.BlockSpec((SPAN, SIDE), lambda i: (end - i, 0)),
            whole_block((CONV, width)),
            whole_block((1, DV)),
            whole_block((1, heads)),
            whole_block((1, heads)),
            pl.BlockSpec((SPAN, heads * DV), lambda i: (end - i, 0)),
            pl.BlockSpec((SPAN, width), lambda i: (end - i, 0)),
            pl.BlockSpec((1, heads, DK, DV), lambda i: (end - i, 0, 0, 0)),
            pl.BlockSpec((1, heads, SPAN, SPAN), lambda i: (end - i, 0, 0, 0)),
            pl.BlockSpec((SPAN, heads * DV), lambda i: (end - i, 0)),
            pl.BlockSpec((SPAN, heads * DV), lambda i: (end - i, 0)),
        ],
        out_specs=[
            pl.BlockSpec((SPAN, width), lambda i: (end - i, 0)),
            pl.BlockSpec((SPAN, heads * DV), lambda i: (end - i, 0)),
            pl.BlockSpec((SPAN, 2 * heads), lambda i: (end - i, 0)),
            whole_block((CONV, width)),
            whole_block((1, DV)),
            whole_block((1, 2 * heads)),
        ],
        out_shape=[
            jax.ShapeDtypeStruct((length, width), bf16),
            jax.ShapeDtypeStruct((length, heads * DV), bf16),
            jax.ShapeDtypeStruct((length, 2 * heads), f32),
            jax.ShapeDtypeStruct((CONV, width), f32),
            jax.ShapeDtypeStruct((1, DV), f32),
            jax.ShapeDtypeStruct((1, 2 * heads), f32),
        ],
        scratch_shapes=[
            pltpu.VMEM((heads, DK, DV), f32),
            pltpu.VMEM((8, width), f32),
            pltpu.VMEM((8, SIDE), f32),
        ],
        compiler_params=MIXER_PARAMS,
        name="mixer_backward",
    )(conv_in, conv_in, out_gate, gates, side, taps, gain, decay_log, dt_bias, *kept, d_gated)


MESH = pl.DeviceIdType.MESH


def column_peers(seq, cores):
    count = seq * cores
    me = lax.axis_index("seq") * cores + lax.axis_index("wshard")
    peers = []
    for step in range(1, count):
        place = lax.rem(me + step, count)
        peers.append((place, {"seq": place // cores, "wshard": lax.rem(place, cores)}))
    return me, peers


def greet(ids):
    barrier = pltpu.get_barrier_semaphore()
    for device in ids:
        pl.semaphore_signal(barrier, inc=1, device_id=device, device_id_type=MESH)
    pl.semaphore_wait(barrier, len(ids))


def small_gather_kernel(seq, cores, in_ref, out_ref, send_sem, recv_sem):
    me, peers = column_peers(seq, cores)
    greet([device for _, device in peers])
    copies = []
    for at, (_, device) in enumerate(peers):
        copies.append(
            pltpu.make_async_remote_copy(
                src_ref=in_ref,
                dst_ref=out_ref.at[me],
                send_sem=send_sem.at[at],
                recv_sem=recv_sem.at[at],
                device_id=device,
                device_id_type=MESH,
            )
        )
        copies[-1].start()
    out_ref[me] = in_ref[...]
    for copy in copies:
        copy.wait()


def small_gather(values, seq, cores):
    count = seq * cores
    return pl.pallas_call(
        functools.partial(small_gather_kernel, seq, cores),
        out_shape=jax.ShapeDtypeStruct((count,) + values.shape, values.dtype),
        in_specs=[pl.BlockSpec(memory_space=pltpu.VMEM)],
        out_specs=pl.BlockSpec(memory_space=pltpu.VMEM),
        scratch_shapes=[pltpu.SemaphoreType.DMA((count - 1,)), pltpu.SemaphoreType.DMA((count - 1,))],
        compiler_params=pltpu.CompilerParams(collective_id=0, has_side_effects=True),
        name="small_gather",
    )(values)


def small_sum_kernel(seq, cores, group, in_ref, out_ref, landed, send_sem, recv_sem, plane_send, plane_recv):
    me, peers = column_peers(seq, cores)
    part = lax.axis_index("group")
    plane = [{"group": lax.rem(part + step, group)} for step in range(1, group)]
    greet([device for _, device in peers] + plane)
    copies = []
    for at, (place, device) in enumerate(peers):
        copies.append(
            pltpu.make_async_remote_copy(
                src_ref=in_ref.at[place],
                dst_ref=landed.at[at],
                send_sem=send_sem.at[at],
                recv_sem=recv_sem.at[at],
                device_id=device,
                device_id_type=MESH,
            )
        )
        copies[-1].start()
    total = in_ref[me]
    for at, copy in enumerate(copies):
        copy.wait()
        total = total + landed[at]
    out_ref[part] = total
    copies = []
    for at, device in enumerate(plane):
        copies.append(
            pltpu.make_async_remote_copy(
                src_ref=out_ref.at[part],
                dst_ref=out_ref.at[part],
                send_sem=plane_send.at[at],
                recv_sem=plane_recv.at[at],
                device_id=device,
                device_id_type=MESH,
            )
        )
        copies[-1].start()
    for copy in copies:
        copy.wait()


def small_sum(values, seq, cores, group):
    count = seq * cores
    shape = values.shape[1:]
    return pl.pallas_call(
        functools.partial(small_sum_kernel, seq, cores, group),
        out_shape=jax.ShapeDtypeStruct((group,) + shape, values.dtype),
        in_specs=[pl.BlockSpec(memory_space=pltpu.VMEM)],
        out_specs=pl.BlockSpec(memory_space=pltpu.VMEM),
        scratch_shapes=[
            pltpu.VMEM((count - 1,) + shape, values.dtype),
            pltpu.SemaphoreType.DMA((count - 1,)),
            pltpu.SemaphoreType.DMA((count - 1,)),
            pltpu.SemaphoreType.DMA((group - 1,)),
            pltpu.SemaphoreType.DMA((group - 1,)),
        ],
        compiler_params=pltpu.CompilerParams(collective_id=1, has_side_effects=True),
        name="small_sum",
    )(values)


def rms_scale(values, gain):
    return values * lax.rsqrt(jnp.mean(values * values, axis=-1, keepdims=True) + eps_norm) * gain


def swiglu(gate_up):
    half = gate_up.shape[1] // 2
    return jax.nn.silu(gate_up[:, :half]) * gate_up[:, half:]


def dot(left, right):
    return jnp.dot(left, right, preferred_element_type=f32)


def dot_t(left, right):
    return lax.dot_general(left, right, (((0,), (0,)), ((), ())), preferred_element_type=f32)


def dot_back(left, right):
    return lax.dot_general(left, right, (((1,), (1,)), ((), ())), preferred_element_type=f32)


SHARDED = ("seq", "wshard")


class Place:
    def __init__(self, rows):
        self.group = lax.axis_size("group")
        self.seq = lax.axis_size("seq")
        self.cores = lax.axis_size("wshard")
        self.part = lax.axis_index("group")
        self.at_seq = lax.axis_index("seq")
        self.core = lax.axis_index("wshard")
        self.rows = rows
        self.per = rows // self.group
        self.subs = self.seq // self.group
        self.sources = self.seq // self.subs
        self.sub = self.at_seq % self.subs
        self.heads = H // self.group
        self.lane = self.seq * rows

    def deal(self, sorted_rows):
        width = sorted_rows.shape[1]
        if self.subs == 1:
            return lax.all_to_all(sorted_rows, "seq", split_axis=0, concat_axis=0, tiled=True)
        sent = jnp.zeros((self.group, self.subs, self.per, width), sorted_rows.dtype)
        sent = lax.dynamic_update_slice(
            sent,
            sorted_rows.reshape(self.group, 1, self.per, width),
            (0, self.at_seq // self.sources, 0, 0),
        )
        got = lax.all_to_all(
            sent.reshape(-1, width), "seq", split_axis=0, concat_axis=0, tiled=True
        )
        return lax.dynamic_slice(got, (self.sub * self.rows, 0), (self.rows, width))

    def undeal(self, rows):
        width = rows.shape[1]
        if self.subs == 1:
            return lax.all_to_all(rows, "seq", split_axis=0, concat_axis=0, tiled=True)
        sent = jnp.zeros((self.subs * self.rows, width), rows.dtype)
        sent = lax.dynamic_update_slice(sent, rows, (self.sub * self.rows, 0))
        got = lax.all_to_all(sent, "seq", split_axis=0, concat_axis=0, tiled=True)
        got = got.reshape(self.group, self.subs, self.per, width)
        got = lax.dynamic_slice(
            got, (0, self.at_seq // self.sources, 0, 0), (self.group, 1, self.per, width)
        )
        return got.reshape(self.rows, width)

    def swap(self, value, turn):
        if turn == 0:
            return value
        return lax.ppermute(value, "group", [(i, i ^ turn) for i in range(self.group)])

    def gather_any(self, rows):
        return jnp.concatenate([self.swap(rows, turn) for turn in range(self.group)], axis=0)

    def reduce_any(self, partial):
        total = partial[: self.rows]
        for turn in range(1, self.group):
            sent = partial[turn * self.rows : (turn + 1) * self.rows].astype(bf16)
            total = total + self.swap(sent, turn).astype(f32)
        return total

    def gather_places(self, rows):
        width = rows.shape[1]
        lane = jnp.zeros((self.sources, self.group, self.per, width), rows.dtype)
        for turn in range(self.group):
            got = self.swap(rows, turn).reshape(self.sources, 1, self.per, width)
            lane = lax.dynamic_update_slice(lane, got, (0, self.part ^ turn, 0, 0))
        return lane.reshape(-1, width)

    def reduce_places(self, partial):
        width = partial.shape[1]
        lane = partial.reshape(self.sources, self.group, self.per, width)
        total = None
        for turn in range(self.group):
            mine = lax.dynamic_slice(
                lane, (0, self.part ^ turn, 0, 0), (self.sources, 1, self.per, width)
            ).reshape(self.rows, width)
            if turn == 0:
                total = mine
            else:
                total = total + self.swap(mine.astype(bf16), turn).astype(f32)
        return total

    def gather_parts(self, value):
        parts = jnp.zeros((self.group,) + value.shape, value.dtype)
        for turn in range(self.group):
            parts = lax.dynamic_update_slice(
                parts, self.swap(value, turn)[None], (self.part ^ turn,) + (0,) * value.ndim
            )
        return parts

    def to_lane(self, rows):
        if self.subs == 1:
            return rows
        every = lax.all_gather(rows, "seq", axis=0, tiled=True)
        length = rows.shape[0] * self.subs
        return lax.dynamic_slice(
            every, ((self.at_seq // self.subs) * length, 0), (length, rows.shape[1])
        )

    def to_own(self, lane_rows):
        if self.subs == 1:
            return lane_rows
        length = lane_rows.shape[0] // self.subs
        return lax.dynamic_slice(lane_rows, (self.sub * length, 0), (length, lane_rows.shape[1]))

    def head_columns(self, array, sections):
        pieces = []
        for begin, width in sections:
            for turn in range(self.heads):
                pieces.append(
                    lax.dynamic_slice(
                        array,
                        (0, begin + (turn * self.group + self.part) * width),
                        (array.shape[0], width),
                    )
                )
        return jnp.concatenate(pieces, axis=1)

    def join_heads(self, parts, sections):
        group, rows = parts.shape[:2]
        out, begin = [], 0
        for _, width in sections:
            section = parts[:, :, begin : begin + self.heads * width]
            begin += self.heads * width
            section = section.reshape(group, rows, self.heads, width).transpose(1, 2, 0, 3)
            out.append(section.reshape(rows, self.heads * group * width))
        return jnp.concatenate(out, axis=1)

    def hidden_columns(self, array, unit_rows_here):
        rows = array.shape[0]
        blocks = self.seq * self.cores
        piece = unit_rows_here // self.group
        split = array.reshape(rows, 2 * blocks, self.group, piece)
        mine = lax.dynamic_slice(split, (0, 0, self.part, 0), (rows, 2 * blocks, 1, piece))
        return mine.reshape(rows, 2 * blocks * piece)

    def join_hidden(self, parts, unit_rows_here):
        group, rows = parts.shape[:2]
        blocks = self.seq * self.cores
        piece = unit_rows_here // group
        split = parts.reshape(group, rows, 2 * blocks, piece).transpose(1, 2, 0, 3)
        return split.reshape(rows, 2 * blocks * group * piece)

    def out_rows(self, w_out):
        width = w_out.shape[1]
        if self.subs == 1 and self.cores == 2:
            mine = lax.dynamic_slice(w_out, ((self.part % 2) * DV, 0), (DV, width))
            half = DV // 2
            kept = lax.dynamic_slice(mine, (self.core * half, 0), (half, width))
            other = lax.dynamic_slice(mine, ((1 - self.core) * half, 0), (half, width))
            got = lax.ppermute(other, "wshard", [(0, 1), (1, 0)])
            piece = jnp.where(self.core == self.part // 2, kept, got)
            return lax.all_gather(piece, SHARDED, axis=0, tiled=True)
        every = lax.all_gather(w_out, SHARDED, axis=0, tiled=True)
        every = every.reshape(self.heads, self.group, DV, width)
        return lax.dynamic_slice(
            every, (0, self.part, 0, 0), (self.heads, 1, DV, width)
        ).reshape(-1, width)

    def out_rows_scatter(self, grad):
        if self.subs == 1 and self.cores == 2:
            return lax.psum_scatter(grad, SHARDED, scatter_dimension=0, tiled=True)
        width = grad.shape[1]
        every = jnp.zeros((self.heads, self.group, DV, width), bf16)
        every = lax.dynamic_update_slice(
            every, grad.reshape(self.heads, 1, DV, width), (0, self.part, 0, 0)
        )
        return lax.psum_scatter(every.reshape(-1, width), SHARDED, scatter_dimension=0, tiled=True)

    def out_rows_join(self, shard):
        width = shard.shape[1]
        if self.subs == 1 and self.cores == 2:
            halves_all = self.gather_parts(shard)
            here = lax.dynamic_slice(halves_all, (2 * self.core, 0, 0), (2, DV // 2, width))
            there = lax.dynamic_slice(halves_all, (2 - 2 * self.core, 0, 0), (2, DV // 2, width))
            got = lax.ppermute(there, "wshard", [(0, 1), (1, 0)])
            first = jnp.where(self.core == 0, here, got)
            second = jnp.where(self.core == 0, got, here)
            return jnp.stack([first, second], axis=1).reshape(2 * DV, width).astype(f32)
        return lax.psum(shard, "group").astype(f32)

    def conv_pieces(self, conv_w):
        if self.subs > 1:
            return conv_w
        columns = conv_w.shape[1]
        wide = lax.dynamic_slice(conv_w, (0, self.part * DV), (CONV, DV))
        narrow = self.head_columns_of(conv_w, DK)
        return jnp.where(self.at_seq * self.cores + self.core >= 2 * HK // columns, wide, narrow)

    def head_columns_of(self, array, head_width):
        count = array.shape[1] // (self.group * head_width)
        return jnp.concatenate(
            [
                lax.dynamic_slice(
                    array,
                    (0, (turn * self.group + self.part) * head_width),
                    (array.shape[0], head_width),
                )
                for turn in range(count)
            ],
            axis=1,
        )

    def join_conv(self, pieces):
        pieces = pieces.reshape(self.seq * self.cores, CONV, -1).transpose(1, 0, 2)
        pieces = pieces.reshape(CONV, -1)
        return self.head_columns(pieces, QKV) if self.subs > 1 else pieces

    def split_conv(self, grad):
        devices = self.seq * self.cores
        if self.subs > 1:
            pieces, begin = [], 0
            mine = (jnp.arange(self.group) == self.part).astype(f32)[:, None]
            for _, head_width in QKV:
                end = begin + self.heads * head_width
                section = grad[:, begin:end].reshape(CONV, self.heads, 1, head_width) * mine
                pieces.append(section.reshape(CONV, -1))
                begin = end
            grad = jnp.concatenate(pieces, axis=1)
        return grad.reshape(CONV, devices, -1).transpose(1, 0, 2).reshape(devices, -1)

    def join_own_conv(self, parts):
        parts = parts.reshape(self.group, CONV, -1)
        if self.subs > 1:
            return jnp.sum(parts, axis=0)
        columns = parts.shape[2] * self.group
        wide = parts.transpose(1, 0, 2).reshape(CONV, columns)
        narrow = parts.reshape(self.group, CONV, -1, DK).transpose(1, 2, 0, 3).reshape(CONV, columns)
        return jnp.where(self.at_seq * self.cores + self.core >= 2 * HK // columns, wide, narrow)


QKV = ((0, DK), (HK, DK), (2 * HK, DV))
GATE = ((2 * HK + HV, DV),)


def side_array(lane_lengths, length):
    ends = jnp.cumsum(lane_lengths)
    bounds = jnp.concatenate([jnp.zeros((1,), jnp.int32), ends])
    places = jnp.arange(length, dtype=jnp.int32)
    crossed = places[:, None] >= bounds[None, :]
    block_begin = (places // SPAN) * SPAN
    counted = jnp.sum((crossed & (bounds[None, :] >= block_begin[:, None])).astype(jnp.int32), axis=1)
    segment = jnp.sum(crossed.astype(jnp.int32), axis=1)
    columns = [counted.astype(f32)]
    for back in range(1, CONV):
        earlier = jnp.sum((places[:, None] - back >= bounds[None, :]).astype(jnp.int32), axis=1)
        columns.append(((earlier == segment) & (places >= back)).astype(f32))
    columns.append((places < ends[-1]).astype(f32))
    columns += [jnp.zeros((length,), f32)] * (SIDE - len(columns))
    return jnp.stack(columns, axis=1)


def shards(
    tokens,
    cotangent,
    dealing,
    lengths,
    attn_gain,
    w_in,
    w_ab,
    conv_w,
    decay_log,
    dt_bias,
    o_gain,
    w_out,
    ffn_gain,
    w_gu,
    w_down,
):
    rows, width = tokens.shape
    at = Place(rows)
    heads = at.heads
    device_rows = w_down.shape[0]
    devices = at.seq * at.cores

    at_device = at.at_seq * at.cores + at.core

    ab_shard = at.head_columns(w_ab, ((0, 1), (H, 1)))
    conv_pieces = at.conv_pieces(conv_w)
    small = (attn_gain, ffn_gain, o_gain, ab_shard.reshape(-1), conv_pieces.reshape(-1))
    lengths_small = [array.shape[0] for array in small]
    filled = sum(lengths_small)
    rows_small = -(-filled // (16 * 128)) * 16
    packed = jnp.concatenate(small + (jnp.zeros((rows_small * 128 - filled,), bf16),))
    packed = small_gather(packed.reshape(rows_small, 128), at.seq, at.cores).reshape(devices, -1)
    full, begin = [], 0
    for count in lengths_small:
        full.append(packed[:, begin : begin + count])
        begin += count
    attn_f, ffn_f, o_f = (array.reshape(-1).astype(f32) for array in full[:3])
    ab_mine = full[3].reshape(width, 2 * heads)
    conv_mine = at.join_conv(full[4]).astype(f32)

    def my_heads(values):
        return lax.dynamic_slice(values.reshape(heads, at.group), (0, at.part), (heads, 1)).reshape(1, -1)

    decay_mine, dt_mine = my_heads(decay_log), my_heads(dt_bias)

    in_qkv = lax.all_gather(at.head_columns(w_in, QKV), SHARDED, axis=0, tiled=True)
    in_gate = lax.all_gather(at.head_columns(w_in, GATE), SHARDED, axis=0, tiled=True)
    out_mine = at.out_rows(w_out)
    gu_mine = lax.all_gather(at.hidden_columns(w_gu, device_rows), SHARDED, axis=0, tiled=True)
    piece = device_rows // at.group
    down_mine = lax.all_gather(
        lax.dynamic_slice(w_down, (at.part * piece, 0), (piece, width)), SHARDED, axis=0, tiled=True
    )

    member = (dealing[:, None] == jnp.arange(at.group, dtype=jnp.int32)[None, :]).astype(jnp.int32)
    before = dot(jnp.tril(jnp.ones((rows, rows), f32), -1).astype(bf16), member.astype(bf16))
    before = before.astype(jnp.int32)
    target = jnp.sum((before + at.per * jnp.arange(at.group, dtype=jnp.int32)) * member, axis=1)
    sorting = (target[None, :] == jnp.arange(rows, dtype=jnp.int32)[:, None]).astype(bf16)
    dealt = at.deal(dot(sorting, jnp.concatenate([tokens, cotangent], axis=1)).astype(bf16))
    tokens_f = dealt[:, :width].astype(f32)
    cot_own = dealt[:, width:]

    lane_lengths = lax.dynamic_index_in_dim(
        at.gather_parts(lengths.reshape(-1)), at.at_seq // at.subs, 0, keepdims=False
    )
    side = side_array(lane_lengths, at.lane)
    normed = rms_scale(tokens_f, attn_f).astype(bf16)
    normed_all = at.gather_places(normed)
    conv_in = at.to_lane(dot(normed_all, in_qkv).astype(bf16))
    gates_ab = at.to_lane(dot(normed_all, ab_mine))
    out_gate = at.to_lane(dot(normed_all, in_gate))
    mixer_args = (conv_in, out_gate, gates_ab, side, conv_mine, o_f[None], decay_mine, dt_mine)
    gated_lane, *kept = mixer_forward(*mixer_args)
    gated = at.to_own(gated_lane)
    branch = at.reduce_places(dot(gated, out_mine))
    resid = tokens_f + branch

    normed2_f, pull_norm2 = jax.vjp(rms_scale, resid, ffn_f)
    normed2_all = at.gather_any(normed2_f.astype(bf16))
    cot_all = at.gather_any(cot_own)
    gate_up = dot(normed2_all, gu_mine)
    hidden_f, pull_ffn = jax.vjp(swiglu, gate_up)
    hidden = hidden_f.astype(bf16)

    d_hidden = dot_back(cot_all, down_mine)
    d_gate_up = pull_ffn(d_hidden)[0].astype(bf16)
    d_normed2_parts = dot_back(d_gate_up, gu_mine)
    d_gu = dot_t(normed2_all, d_gate_up).astype(bf16)
    d_down = dot_t(hidden, cot_all).astype(bf16)
    d_normed2_parts, d_gu, d_down = lax.optimization_barrier((d_normed2_parts, d_gu, d_down))
    gu_shard = lax.psum_scatter(d_gu, SHARDED, scatter_dimension=0, tiled=True)
    down_shard = lax.psum_scatter(d_down, SHARDED, scatter_dimension=0, tiled=True)
    d_normed2 = at.reduce_any(d_normed2_parts)
    output_parts = dot(hidden, down_mine)
    d_resid_norm, d_ffn_gain = pull_norm2(d_normed2)
    d_resid = cot_own.astype(f32) + d_resid_norm

    d_branch_all = at.gather_places(d_resid.astype(bf16))
    d_gated = dot_back(d_branch_all, out_mine)
    d_out = dot_t(gated, d_branch_all).astype(bf16)
    d_gated, d_out, output_parts = lax.optimization_barrier((d_gated, d_out, output_parts))
    output = (resid + at.reduce_any(output_parts)).astype(bf16)
    out_shard = at.out_rows_scatter(d_out)
    d_conv_lane, d_gate_lane, d_gates_lane, d_conv_w, d_o_gain, d_heads = mixer_backward(
        *mixer_args, tuple(kept), at.to_lane(d_gated)
    )
    once = (at.sub == 0).astype(f32)
    d_conv_w, d_o_gain, d_heads = d_conv_w * once, d_o_gain * once, d_heads * once
    d_conv_in = at.to_own(d_conv_lane)
    d_gate = at.to_own(d_gate_lane)
    d_ab = at.to_own(d_gates_lane).astype(bf16)
    d_in_gate = dot_t(normed_all, d_gate).astype(bf16)
    d_in = dot_t(normed_all, d_conv_in).astype(bf16)
    d_in, d_in_gate, d_conv_in, d_gate, d_ab = lax.optimization_barrier(
        (d_in, d_in_gate, d_conv_in, d_gate, d_ab)
    )
    in_shard = lax.psum_scatter(d_in, SHARDED, scatter_dimension=0, tiled=True)
    gate_shard = lax.psum_scatter(d_in_gate, SHARDED, scatter_dimension=0, tiled=True)
    d_w_ab = dot_t(normed_all, d_ab)
    d_normed = at.reduce_places(
        dot_back(d_conv_in, in_qkv) + dot_back(d_gate, in_gate) + dot_back(d_ab, ab_mine)
    )
    value_norm, pull_norm = jax.vjp(rms_scale, tokens_f, attn_f)
    d_tokens_norm, d_attn_gain = pull_norm(d_normed)
    d_tokens = (d_resid + d_tokens_norm).astype(bf16)

    returned = at.undeal(jnp.concatenate([output, d_tokens], axis=1))
    returned = dot_t(sorting, returned).astype(bf16)

    grad_w_gu = at.join_hidden(at.gather_parts(gu_shard), device_rows).astype(f32)
    grad_w_down = at.gather_parts(down_shard).reshape(device_rows, width).astype(f32)
    grad_w_out = at.out_rows_join(out_shard)
    grad_w_in = jnp.concatenate(
        [
            at.join_heads(at.gather_parts(in_shard), QKV),
            at.join_heads(at.gather_parts(gate_shard), GATE),
        ],
        axis=1,
    ).astype(f32)

    def to_blocks(array):
        return array.reshape(devices, -1)

    blocks = (
        to_blocks(d_attn_gain),
        to_blocks(d_ffn_gain),
        to_blocks(d_o_gain),
        to_blocks(d_w_ab),
        at.split_conv(d_conv_w),
        jnp.broadcast_to(d_heads, (devices, 2 * heads)),
    )
    sizes = [array.shape[1] for array in blocks]
    filled = sum(sizes)
    rows_small = -(-filled // 1024) * 8
    packed = jnp.concatenate(
        blocks + (jnp.zeros((devices, rows_small * 128 - filled), f32),), axis=1
    )
    summed = small_sum(packed.reshape(devices, rows_small, 128), at.seq, at.cores, at.group)
    summed = summed.reshape(at.group, -1)
    parts, begin = [], 0
    for size in sizes:
        parts.append(summed[:, begin : begin + size])
        begin += size
    grad_w_ab = parts[3].reshape(at.group, width // devices, 2, heads).transpose(1, 2, 3, 0)
    grad_heads = parts[5].reshape(at.group, 2, heads).transpose(1, 2, 0).reshape(2, H)
    return (
        returned[:, :width],
        returned[:, width:],
        jnp.sum(parts[0], axis=0),
        grad_w_in,
        grad_w_ab.reshape(width // devices, 2 * H),
        at.join_own_conv(parts[4]),
        grad_heads[0],
        grad_heads[1],
        jnp.sum(parts[2], axis=0),
        grad_w_out,
        jnp.sum(parts[1], axis=0),
        grad_w_gu,
        grad_w_down,
    )


def solution(mesh):
    placed = (
        P(("group", "seq", "wshard"), None),
        P(("group", "seq", "wshard"), None),
        P(("group", "seq", "wshard")),
        P("group", "wshard", None),
        P(("seq", "wshard")),
        P(("seq", "wshard"), None),
        P(("seq", "wshard"), None),
        P(None, ("seq", "wshard")),
        P(),
        P(),
        P(("seq", "wshard")),
        P(("seq", "wshard"), None),
        P(("seq", "wshard")),
        P(("seq", "wshard"), None),
        P(("seq", "wshard"), None),
    )
    return jax.shard_map(
        shards,
        mesh=mesh,
        in_specs=placed,
        out_specs=(
            P(("group", "seq", "wshard"), None),
            P(("group", "seq", "wshard"), None),
            P(("seq", "wshard")),
            P(("seq", "wshard"), None),
            P(("seq", "wshard"), None),
            P(None, ("seq", "wshard")),
            P(),
            P(),
            P(("seq", "wshard")),
            P(("seq", "wshard"), None),
            P(("seq", "wshard")),
            P(("seq", "wshard"), None),
            P(("seq", "wshard"), None),
        ),
        check_vma=False,
    )
```

```python
import functools

import jax
import jax.numpy as jnp
from jax import lax
from jax.experimental import pallas as pl
from jax.experimental.pallas import tpu as pltpu
from jax.sharding import PartitionSpec as P

H = 16
DK = 128
DV = 256
FF = 5632
CONV = 4
SPAN = 64
HK = 2048
HV = 4096
SIDE = 16
EDGE = 32

bf16 = jnp.bfloat16
f32 = jnp.float32
eps_norm = 1e-06


def mm(left, right, over=((1,), (0,))):
    return lax.dot_general(left, right, (over, ((), ())), preferred_element_type=f32)


def halves(value):
    high = value.astype(bf16)
    return high, (value - high.astype(f32)).astype(bf16)


def mm_fine(left, right):
    left_high, left_low = halves(left)
    right_high, right_low = halves(right)
    return mm(left_high, right_high) + mm(left_low, right_high) + mm(left_high, right_low)


def mm_right(left, right, over=((1,), (0,))):
    return mm(left, right.astype(bf16), over)


def mm_both(left, right, over=((1,), (0,))):
    return mm(left.astype(bf16), right.astype(bf16), over)


ROWS = ((1,), (1,))
COLS = ((0,), (0,))


def unit_lower_inverses(stricts):
    groups = EDGE // 8
    count = SPAN // EDGE
    places = lax.broadcasted_iota(jnp.int32, (8, EDGE), 0)
    columns = lax.broadcasted_iota(jnp.int32, (8, EDGE), 1)
    blocks = {}
    for at, strict in enumerate(stricts):
        for block in range(count):
            begin = block * EDGE
            blocks[at, block] = (
                strict[begin : begin + EDGE, begin : begin + EDGE],
                [(places + 8 * part == columns).astype(f32) for part in range(groups)],
            )
    for row in range(EDGE - 1):
        first = row // 8
        for own, done in blocks.values():
            line = done[first][row - 8 * first : row - 8 * first + 1, :]
            for part in range(first, groups):
                column = own[8 * part : 8 * part + 8, row : row + 1]
                done[part] = done[part] - column * line
    inverses = []
    for at, strict in enumerate(stricts):
        parts = [jnp.concatenate(blocks[at, block][1], axis=0) for block in range(count)]
        size = EDGE
        while size < SPAN:
            joined = []
            for pair in range(0, len(parts), 2):
                begin = pair * size
                below = strict[begin + size : begin + 2 * size, begin : begin + size]
                upper, lower = parts[pair], parts[pair + 1]
                corner = mm_fine(mm_fine(lower, below), upper)
                joined.append(
                    jnp.concatenate(
                        [
                            jnp.concatenate([upper, jnp.zeros((size, size), f32)], axis=1),
                            jnp.concatenate([-corner, lower], axis=1),
                        ],
                        axis=0,
                    )
                )
            parts = joined
            size *= 2
        inverses.append(parts[0])
    return inverses


def silu_parts(value):
    rate = 1.0 / (1.0 + jnp.exp(-value))
    return value * rate, rate


def gate_terms(heads, gates, decay_log, dt_bias):
    shifted = gates[:, :heads] + dt_bias
    beta = 1.0 / (1.0 + jnp.exp(-gates[:, heads:]))
    soft = jnp.maximum(shifted, 0.0) + jnp.log1p(jnp.exp(-jnp.abs(shifted)))
    return shifted, beta, -jnp.exp(decay_log) * soft


def ones_left(ones, value):
    high, rest = halves(value)
    high_f = high.astype(f32)
    rest, low = halves(value - high_f)
    return mm(ones, high) + mm(ones, rest) + mm(ones, low)


def triangle(upper):
    at_i = lax.broadcasted_iota(jnp.int32, (SPAN, SPAN), 0)
    at_j = lax.broadcasted_iota(jnp.int32, (SPAN, SPAN), 1)
    return jnp.where(at_i <= at_j if upper else at_i >= at_j, 1.0, 0.0).astype(bf16)


def side_columns(heads, gates, side, decay_log, dt_bias):
    shifted, beta, decay = gate_terms(heads, gates, decay_log, dt_bias)
    running = ones_left(triangle(False), decay)
    cols = jnp.concatenate(
        [running, beta, side[:, :1], jnp.zeros((SPAN, 128 - 2 * heads - 1), f32)], axis=1
    )
    return cols, cols.T, shifted, beta, decay


def conv_forward(current, before, taps, side):
    extended = jnp.concatenate([before, current], axis=0)
    total = taps[0:1, :] * current
    for back in range(1, CONV):
        total = total + taps[back : back + 1, :] * (
            extended[8 - back : 8 - back + SPAN, :] * side[:, back : back + 1]
        )
    return total


def block_terms(head, heads, cols, rows):
    cum_c = cols[:, head : head + 1]
    beta_c = cols[:, heads + head : heads + head + 1]
    count_c = cols[:, 2 * heads : 2 * heads + 1]
    cum_r = rows[head : head + 1, :]
    count_r = rows[2 * heads : 2 * heads + 1, :]
    at_i = lax.broadcasted_iota(jnp.int32, (SPAN, SPAN), 0)
    at_j = lax.broadcasted_iota(jnp.int32, (SPAN, SPAN), 1)
    same = count_c == count_r
    lower_eq = same & (at_i >= at_j)
    lower_st = same & (at_i > at_j)
    fall = jnp.where(lower_eq, jnp.exp(jnp.where(lower_eq, cum_c - cum_r, 0.0)), 0.0)
    growth = jnp.where(count_c == 0.0, jnp.exp(cum_c), 0.0)
    last = SPAN - 1
    tail = jnp.where(
        count_c == count_c[last : last + 1, :], jnp.exp(cum_c[last : last + 1, :] - cum_c), 0.0
    )
    return beta_c, lower_st, fall, growth, tail, growth[last : last + 1, :]


def mixer_forward_kernel(
    heads,
    conv_ref,
    gate_ref,
    gates_ref,
    side_ref,
    taps_ref,
    gain_ref,
    log_ref,
    bias_ref,
    gated_ref,
    mixed_ref,
    qkv_ref,
    state_ref,
    inv_ref,
    solved_ref,
    carried,
    before,
):
    @pl.when(pl.program_id(0) == 0)
    def _():
        carried[...] = jnp.zeros_like(carried)
        before[...] = jnp.zeros_like(before)

    side = side_ref[...]
    current = conv_ref[...].astype(bf16).astype(f32)
    act, _ = silu_parts(conv_forward(current, before[...], taps_ref[...], side))
    before[...] = current[SPAN - 8 :, :]
    cols, rows, _, _, _ = side_columns(heads, gates_ref[...], side, log_ref[...], bias_ref[...])
    valid = side[:, CONV : CONV + 1]
    gain = gain_ref[...]
    scale = DK ** (-0.5)
    terms, units, stricts = [], [], []
    for head in range(heads):
        terms.append(block_terms(head, heads, cols, rows))
        beta_c, lower_st, fall = terms[-1][:3]
        unit = []
        for begin in (head * DK, (heads + head) * DK):
            row = act[:, begin : begin + DK]
            row = row * lax.rsqrt(jnp.sum(row * row, axis=1, keepdims=True) + eps_norm)
            row = row.astype(bf16)
            qkv_ref[:, begin : begin + DK] = row
            unit.append(row)
        units.append(unit)
        stricts.append(jnp.where(lower_st, beta_c * mm(unit[1], unit[1], ROWS) * fall, 0.0))
    inverses = unit_lower_inverses(stricts)
    for head in range(heads):
        beta_c, lower_st, fall, growth, tail, kept = terms[head]
        queries, keys = units[head]
        inverse = inverses[head]
        inv_ref[0, head] = inverse
        begin = 2 * heads * DK + head * DV
        values = act[:, begin : begin + DV].astype(bf16)
        qkv_ref[:, begin : begin + DV] = values
        state = carried[head]
        state_ref[0, head] = state
        query_prod = mm(queries, keys, ROWS)
        key_state = mm_right(keys, state)
        query_state = mm_right(queries, state)
        right_side = beta_c * (values.astype(f32) - growth * key_state)
        solved = mm_both(inverse, right_side)
        mixed = scale * (growth * query_state + mm_both(query_prod * fall, solved)) * valid
        part = slice(head * DV, (head + 1) * DV)
        mixed_ref[:, part] = mixed
        solved_ref[:, part] = solved
        carried[head] = kept * state + mm_both(tail * keys.astype(f32), solved, COLS)
        shrink = lax.rsqrt(jnp.mean(mixed * mixed, axis=1, keepdims=True) + eps_norm)
        open_gate, _ = silu_parts(gate_ref[:, part])
        gated_ref[:, part] = (mixed * shrink * gain * open_gate).astype(bf16)


def mixer_backward_kernel(
    heads,
    conv_ref,
    ahead_ref,
    gate_ref,
    gates_ref,
    side_ref,
    taps_ref,
    gain_ref,
    log_ref,
    bias_ref,
    mixed_ref,
    qkv_ref,
    state_ref,
    inv_ref,
    solved_ref,
    cot_ref,
    dproj_ref,
    dgates_ref,
    dtaps_ref,
    dgain_ref,
    dheads_ref,
    carried,
    after,
    after_side,
):
    @pl.when(pl.program_id(0) == 0)
    def _():
        carried[...] = jnp.zeros_like(carried)
        after[...] = jnp.zeros_like(after)
        after_side[...] = jnp.zeros_like(after_side)
        dtaps_ref[...] = jnp.zeros_like(dtaps_ref)
        dgain_ref[...] = jnp.zeros_like(dgain_ref)
        dheads_ref[...] = jnp.zeros_like(dheads_ref)

    side = side_ref[...]
    taps = taps_ref[...]
    gain = gain_ref[...]
    valid = side[:, CONV : CONV + 1]
    current = conv_ref[...].astype(bf16).astype(f32)
    ahead = ahead_ref[...].astype(bf16).astype(f32)
    conv_out = conv_forward(current, ahead, taps, side)
    act, rate = silu_parts(conv_out)
    slope = rate * (1.0 + conv_out * (1.0 - rate))
    cols, rows, shifted, beta_all, decay_all = side_columns(
        heads, gates_ref[...], side, log_ref[...], bias_ref[...]
    )
    scale = DK ** (-0.5)
    at_last = lax.broadcasted_iota(jnp.int32, (SPAN, 1), 0) == SPAN - 1
    d_betas, d_cums = [], []
    d_queries, d_keys, d_values = [], [], []
    d_gain = jnp.zeros((1, DV), f32)
    for head in range(heads):
        beta_c, lower_st, fall, growth, tail, kept = block_terms(head, heads, cols, rows)
        part = slice(head * DV, (head + 1) * DV)
        mixed = mixed_ref[:, part]
        gate = gate_ref[:, part]
        d_gated = cot_ref[:, part]
        shrink = lax.rsqrt(jnp.mean(mixed * mixed, axis=1, keepdims=True) + eps_norm)
        normal = mixed * shrink
        open_gate, gate_rate = silu_parts(gate)
        with_normal = d_gated * normal
        d_gain = d_gain + jnp.sum(with_normal * open_gate, axis=0, keepdims=True)
        begin = 2 * heads * DK + (heads + head) * DV
        dproj_ref[:, begin : begin + DV] = (
            with_normal * gain * (gate_rate * (1.0 + gate * (1.0 - gate_rate)))
        ).astype(bf16)
        d_normal = d_gated * gain * open_gate
        d_mixed = shrink * (d_normal - normal * jnp.mean(d_normal * normal, axis=1, keepdims=True))
        d_mixed = (scale * valid) * d_mixed
        queries = qkv_ref[:, head * DK : (head + 1) * DK]
        keys = qkv_ref[:, (heads + head) * DK : (heads + head + 1) * DK]
        begin = 2 * heads * DK + head * DV
        values = qkv_ref[:, begin : begin + DV]
        keys_f = keys.astype(f32)
        queries_f = queries.astype(f32)
        state = state_ref[0, head]
        inverse = inv_ref[0, head]
        solved = solved_ref[:, part]
        d_state = carried[head]
        key_prod = mm(keys, keys, ROWS)
        query_prod = mm(queries, keys, ROWS)
        strict = jnp.where(lower_st, beta_c * key_prod * fall, 0.0)
        mixing = query_prod * fall
        key_state = mm_right(keys, state)
        query_state = mm_right(queries, state)
        d_solved = mm_both(mixing, d_mixed, COLS) + mm_both(tail * keys_f, d_state)
        d_right = mm_both(inverse, d_solved, COLS)
        d_mixing = mm_both(d_mixed, solved, ROWS)
        d_query_prod = d_mixing * fall
        d_strict = jnp.where(lower_st, -mm_both(d_right, solved, ROWS), 0.0)
        d_key_prod = d_strict * beta_c * fall
        d_key_state = -(beta_c * growth) * d_right
        d_query = mm_both(growth * d_mixed, state, ROWS) + mm_both(d_query_prod, keys_f)
        both = d_key_prod + d_key_prod.T
        from_tail = mm_both(solved, d_state, ROWS)
        d_key = (
            mm_both(d_key_state, state, ROWS)
            + mm_both(both, keys_f)
            + mm_both(d_query_prod, queries_f, COLS)
            + tail * from_tail
        )
        residual = values.astype(f32) - growth * key_state
        d_betas.append(
            jnp.sum(d_right * residual, axis=1, keepdims=True)
            + jnp.sum(d_strict * key_prod * fall, axis=1, keepdims=True)
        )
        spread = d_strict * strict + d_mixing * mixing
        from_last = tail * jnp.sum(keys_f * from_tail, axis=1, keepdims=True)
        d_growth = jnp.sum(d_mixed * query_state, axis=1, keepdims=True) - beta_c * jnp.sum(
            d_right * key_state, axis=1, keepdims=True
        )
        at_end = jnp.sum(from_last, axis=0, keepdims=True) + kept * jnp.sum(
            jnp.sum(d_state * state, axis=1, keepdims=True), axis=0, keepdims=True
        )
        d_cums.append(
            jnp.sum(spread, axis=1, keepdims=True)
            - jnp.sum(spread.T, axis=1, keepdims=True)
            + growth * d_growth
            - from_last
            + jnp.where(at_last, at_end, 0.0)
        )
        carried[head] = (
            kept * d_state
            + mm_both(growth * queries_f, d_mixed, COLS)
            + mm_right(keys, d_key_state, COLS)
        )
        for grads, grad, start in ((d_queries, d_query, head * DK), (d_keys, d_key, (heads + head) * DK)):
            row = act[:, start : start + DK]
            small = lax.rsqrt(jnp.sum(row * row, axis=1, keepdims=True) + eps_norm)
            along = jnp.sum(row * grad, axis=1, keepdims=True) * small * small
            grads.append(small * (grad - row * along))
        d_values.append(beta_c * d_right)
    dgain_ref[...] += d_gain
    d_conv = jnp.concatenate(d_queries + d_keys + d_values, axis=1) * slope
    extended = jnp.concatenate([ahead, current], axis=0)
    later, later_side = after[...], after_side[...]
    d_in = taps[0:1, :] * d_conv
    d_taps = [jnp.sum(d_conv * current, axis=0, keepdims=True)]
    for back in range(1, CONV):
        masked = d_conv * side[:, back : back + 1]
        d_taps.append(
            jnp.sum(masked * extended[8 - back : 8 - back + SPAN, :], axis=0, keepdims=True)
        )
        reach = jnp.concatenate([masked, later * later_side[:, back : back + 1]], axis=0)
        d_in = d_in + taps[back : back + 1, :] * reach[back : back + SPAN, :]
    dtaps_ref[...] += jnp.concatenate(d_taps, axis=0)
    dproj_ref[:, : heads * (2 * DK + DV)] = d_in.astype(bf16)
    after[...] = d_conv[:8, :]
    after_side[...] = side[:8, :]
    d_decay = ones_left(triangle(True), jnp.concatenate(d_cums, axis=1))
    d_beta = jnp.concatenate(d_betas, axis=1)
    d_shifted = -d_decay * jnp.exp(log_ref[...]) / (1.0 + jnp.exp(-shifted))
    dgates_ref[...] = jnp.concatenate([d_shifted, d_beta * beta_all * (1.0 - beta_all)], axis=1)
    dheads_ref[...] += jnp.concatenate(
        [
            jnp.sum(d_decay * decay_all, axis=0, keepdims=True),
            jnp.sum(d_shifted, axis=0, keepdims=True),
        ],
        axis=1,
    )


def whole_block(shape):
    return pl.BlockSpec(shape, lambda i: (0,) * len(shape))


MIXER_PARAMS = pltpu.CompilerParams(vmem_limit_bytes=48 * 1024 * 1024)


def mixer_forward(proj, gates, side, taps, gain, decay_log, dt_bias):
    length = proj.shape[0]
    width = taps.shape[1]
    heads = decay_log.shape[1]
    gate_at = width // (heads * DV)
    blocks = length // SPAN
    return pl.pallas_call(
        functools.partial(mixer_forward_kernel, heads),
        grid=(blocks,),
        in_specs=[
            pl.BlockSpec((SPAN, width), lambda i: (i, 0)),
            pl.BlockSpec((SPAN, heads * DV), lambda i: (i, gate_at)),
            pl.BlockSpec((SPAN, 2 * heads), lambda i: (i, 0)),
            pl.BlockSpec((SPAN, SIDE), lambda i: (i, 0)),
            whole_block((CONV, width)),
            whole_block((1, DV)),
            whole_block((1, heads)),
            whole_block((1, heads)),
        ],
        out_specs=[
            pl.BlockSpec((SPAN, heads * DV), lambda i: (i, 0)),
            pl.BlockSpec((SPAN, heads * DV), lambda i: (i, 0)),
            pl.BlockSpec((SPAN, width), lambda i: (i, 0)),
            pl.BlockSpec((1, heads, DK, DV), lambda i: (i, 0, 0, 0)),
            pl.BlockSpec((1, heads, SPAN, SPAN), lambda i: (i, 0, 0, 0)),
            pl.BlockSpec((SPAN, heads * DV), lambda i: (i, 0)),
        ],
        out_shape=[
            jax.ShapeDtypeStruct((length, heads * DV), bf16),
            jax.ShapeDtypeStruct((length, heads * DV), f32),
            jax.ShapeDtypeStruct((length, width), bf16),
            jax.ShapeDtypeStruct((blocks, heads, DK, DV), f32),
            jax.ShapeDtypeStruct((blocks, heads, SPAN, SPAN), f32),
            jax.ShapeDtypeStruct((length, heads * DV), f32),
        ],
        scratch_shapes=[pltpu.VMEM((heads, DK, DV), f32), pltpu.VMEM((8, width), f32)],
        compiler_params=MIXER_PARAMS,
        cost_estimate=pl.CostEstimate(
            flops=length * heads * 10**7, bytes_accessed=length * heads * 10**4, transcendentals=0
        ),
        name="mixer_forward",
    )(proj, proj, gates, side, taps, gain, decay_log, dt_bias)


def mixer_backward(proj, gates, side, taps, gain, decay_log, dt_bias, kept, d_gated):
    length = proj.shape[0]
    width = taps.shape[1]
    heads = decay_log.shape[1]
    gate_at = width // (heads * DV)
    blocks = length // SPAN
    end = blocks - 1
    ahead_rows = 8
    per = SPAN // ahead_rows
    return pl.pallas_call(
        functools.partial(mixer_backward_kernel, heads),
        grid=(blocks,),
        in_specs=[
            pl.BlockSpec((SPAN, width), lambda i: (end - i, 0)),
            pl.BlockSpec((ahead_rows, width), lambda i: (jnp.maximum((end - i) * per - 1, 0), 0)),
            pl.BlockSpec((SPAN, heads * DV), lambda i: (end - i, gate_at)),
            pl.BlockSpec((SPAN, 2 * heads), lambda i: (end - i, 0)),
            pl.BlockSpec((SPAN, SIDE), lambda i: (end - i, 0)),
            whole_block((CONV, width)),
            whole_block((1, DV)),
            whole_block((1, heads)),
            whole_block((1, heads)),
            pl.BlockSpec((SPAN, heads * DV), lambda i: (end - i, 0)),
            pl.BlockSpec((SPAN, width), lambda i: (end - i, 0)),
            pl.BlockSpec((1, heads, DK, DV), lambda i: (end - i, 0, 0, 0)),
            pl.BlockSpec((1, heads, SPAN, SPAN), lambda i: (end - i, 0, 0, 0)),
            pl.BlockSpec((SPAN, heads * DV), lambda i: (end - i, 0)),
            pl.BlockSpec((SPAN, heads * DV), lambda i: (end - i, 0)),
        ],
        out_specs=[
            pl.BlockSpec((SPAN, width + heads * DV), lambda i: (end - i, 0)),
            pl.BlockSpec((SPAN, 2 * heads), lambda i: (end - i, 0)),
            whole_block((CONV, width)),
            whole_block((1, DV)),
            whole_block((1, 2 * heads)),
        ],
        out_shape=[
            jax.ShapeDtypeStruct((length, width + heads * DV), bf16),
            jax.ShapeDtypeStruct((length, 2 * heads), f32),
            jax.ShapeDtypeStruct((CONV, width), f32),
            jax.ShapeDtypeStruct((1, DV), f32),
            jax.ShapeDtypeStruct((1, 2 * heads), f32),
        ],
        scratch_shapes=[
            pltpu.VMEM((heads, DK, DV), f32),
            pltpu.VMEM((8, width), f32),
            pltpu.VMEM((8, SIDE), f32),
        ],
        compiler_params=MIXER_PARAMS,
        cost_estimate=pl.CostEstimate(
            flops=length * heads * 10**7, bytes_accessed=length * heads * 10**4, transcendentals=0
        ),
        name="mixer_backward",
    )(proj, proj, proj, gates, side, taps, gain, decay_log, dt_bias, *kept, d_gated)


MESH = pl.DeviceIdType.MESH


def column_peers(seq, cores):
    count = seq * cores
    me = lax.axis_index("seq") * cores + lax.axis_index("wshard")
    peers = []
    for step in range(1, count):
        place = lax.rem(me + step, count)
        peers.append((place, {"seq": place // cores, "wshard": lax.rem(place, cores)}))
    return me, peers


def greet(ids):
    barrier = pltpu.get_barrier_semaphore()
    for device in ids:
        pl.semaphore_signal(barrier, inc=1, device_id=device, device_id_type=MESH)
    pl.semaphore_wait(barrier, len(ids))


def small_gather_kernel(seq, cores, in_ref, out_ref, send_sem, recv_sem):
    me, peers = column_peers(seq, cores)
    greet([device for _, device in peers])
    copies = []
    for at, (_, device) in enumerate(peers):
        copies.append(
            pltpu.make_async_remote_copy(
                src_ref=in_ref,
                dst_ref=out_ref.at[me],
                send_sem=send_sem.at[at],
                recv_sem=recv_sem.at[at],
                device_id=device,
                device_id_type=MESH,
            )
        )
        copies[-1].start()
    out_ref[me] = in_ref[...]
    for copy in copies:
        copy.wait()


def small_gather(values, seq, cores):
    count = seq * cores
    return pl.pallas_call(
        functools.partial(small_gather_kernel, seq, cores),
        out_shape=jax.ShapeDtypeStruct((count,) + values.shape, values.dtype),
        in_specs=[pl.BlockSpec(memory_space=pltpu.VMEM)],
        out_specs=pl.BlockSpec(memory_space=pltpu.VMEM),
        scratch_shapes=[pltpu.SemaphoreType.DMA((count - 1,)), pltpu.SemaphoreType.DMA((count - 1,))],
        compiler_params=pltpu.CompilerParams(collective_id=0, has_side_effects=True),
        name="small_gather",
    )(values)


def small_sum_kernel(seq, cores, group, in_ref, out_ref, landed, send_sem, recv_sem, plane_send, plane_recv):
    me, peers = column_peers(seq, cores)
    part = lax.axis_index("group")
    plane = [{"group": lax.rem(part + step, group)} for step in range(1, group)]
    greet([device for _, device in peers] + plane)
    copies = []
    for at, (place, device) in enumerate(peers):
        copies.append(
            pltpu.make_async_remote_copy(
                src_ref=in_ref.at[place],
                dst_ref=landed.at[at],
                send_sem=send_sem.at[at],
                recv_sem=recv_sem.at[at],
                device_id=device,
                device_id_type=MESH,
            )
        )
        copies[-1].start()
    total = in_ref[me]
    for at, copy in enumerate(copies):
        copy.wait()
        total = total + landed[at]
    out_ref[part] = total
    copies = []
    for at, device in enumerate(plane):
        copies.append(
            pltpu.make_async_remote_copy(
                src_ref=out_ref.at[part],
                dst_ref=out_ref.at[part],
                send_sem=plane_send.at[at],
                recv_sem=plane_recv.at[at],
                device_id=device,
                device_id_type=MESH,
            )
        )
        copies[-1].start()
    for copy in copies:
        copy.wait()


def small_sum(values, seq, cores, group):
    count = seq * cores
    shape = values.shape[1:]
    return pl.pallas_call(
        functools.partial(small_sum_kernel, seq, cores, group),
        out_shape=jax.ShapeDtypeStruct((group,) + shape, values.dtype),
        in_specs=[pl.BlockSpec(memory_space=pltpu.VMEM)],
        out_specs=pl.BlockSpec(memory_space=pltpu.VMEM),
        scratch_shapes=[
            pltpu.VMEM((count - 1,) + shape, values.dtype),
            pltpu.SemaphoreType.DMA((count - 1,)),
            pltpu.SemaphoreType.DMA((count - 1,)),
            pltpu.SemaphoreType.DMA((group - 1,)),
            pltpu.SemaphoreType.DMA((group - 1,)),
        ],
        compiler_params=pltpu.CompilerParams(collective_id=1, has_side_effects=True),
        name="small_sum",
    )(values)


def pick_columns_kernel(pieces, group, array_ref, out_ref):
    part = lax.axis_index("group")
    for own in range(group):

        @pl.when(part == own)
        def _():
            out_ref[...] = jnp.concatenate(
                [
                    array_ref[:, first + own * width : first + (own + 1) * width]
                    for first, width in pieces
                ],
                axis=1,
            )


def pick_columns(array, pieces, group):
    rows, columns = array.shape
    step = min(rows, 64)
    picked = sum(width for _, width in pieces)
    return pl.pallas_call(
        functools.partial(pick_columns_kernel, pieces, group),
        grid=(rows // step,),
        in_specs=[pl.BlockSpec((step, columns), lambda i: (i, 0))],
        out_specs=pl.BlockSpec((step, picked), lambda i: (i, 0)),
        out_shape=jax.ShapeDtypeStruct((rows, picked), array.dtype),
        compiler_params=MIXER_PARAMS,
        name="pick_columns",
    )(array)


def join_columns_kernel(group, runs, parts_ref, out_ref):
    source, target = 0, 0
    for width, count in runs:
        pack = 1
        while pack < count and (pack * group * width) % 128:
            pack *= 2
        for first in range(0, count, pack):
            pieces = []
            for run in range(first, first + pack):
                for part in range(group):
                    begin = source + run * width
                    pieces.append(parts_ref[part, :, begin : begin + width].astype(f32))
            size = pack * group * width
            out_ref[:, target : target + size] = jnp.concatenate(pieces, axis=1)
            target += size
        source += count * width


def join_columns(parts, runs):
    group, rows, columns = parts.shape
    step = min(rows, 32)
    return pl.pallas_call(
        functools.partial(join_columns_kernel, group, runs),
        grid=(rows // step,),
        in_specs=[pl.BlockSpec((group, step, columns), lambda i: (0, i, 0))],
        out_specs=pl.BlockSpec((step, group * columns), lambda i: (i, 0)),
        out_shape=jax.ShapeDtypeStruct((rows, group * columns), f32),
        compiler_params=MIXER_PARAMS,
        name="join_columns",
    )(parts)


def rms_scale(values, gain):
    return values * lax.rsqrt(jnp.mean(values * values, axis=-1, keepdims=True) + eps_norm) * gain


def swiglu(gate_up):
    half = gate_up.shape[1] // 2
    return jax.nn.silu(gate_up[:, :half]) * gate_up[:, half:]


def dot(left, right):
    return jnp.dot(left, right, preferred_element_type=f32)


def dot_t(left, right):
    return lax.dot_general(left, right, (((0,), (0,)), ((), ())), preferred_element_type=f32)


def dot_back(left, right):
    return lax.dot_general(left, right, (((1,), (1,)), ((), ())), preferred_element_type=f32)


SHARDED = ("seq", "wshard")


class Place:
    def __init__(self, rows):
        self.group = lax.axis_size("group")
        self.seq = lax.axis_size("seq")
        self.cores = lax.axis_size("wshard")
        self.part = lax.axis_index("group")
        self.at_seq = lax.axis_index("seq")
        self.core = lax.axis_index("wshard")
        self.rows = rows
        self.per = rows // self.group
        self.subs = self.seq // self.group
        self.sources = self.seq // self.subs
        self.sub = self.at_seq % self.subs
        self.heads = H // self.group
        self.lane = self.seq * rows

    def deal(self, sorted_rows):
        width = sorted_rows.shape[1]
        if self.subs == 1:
            return lax.all_to_all(sorted_rows, "seq", split_axis=0, concat_axis=0, tiled=True)
        sent = jnp.zeros((self.group, self.subs, self.per, width), sorted_rows.dtype)
        sent = lax.dynamic_update_slice(
            sent,
            sorted_rows.reshape(self.group, 1, self.per, width),
            (0, self.at_seq // self.sources, 0, 0),
        )
        got = lax.all_to_all(
            sent.reshape(-1, width), "seq", split_axis=0, concat_axis=0, tiled=True
        )
        return lax.dynamic_slice(got, (self.sub * self.rows, 0), (self.rows, width))

    def undeal(self, rows):
        width = rows.shape[1]
        if self.subs == 1:
            return lax.all_to_all(rows, "seq", split_axis=0, concat_axis=0, tiled=True)
        sent = jnp.zeros((self.subs * self.rows, width), rows.dtype)
        sent = lax.dynamic_update_slice(sent, rows, (self.sub * self.rows, 0))
        got = lax.all_to_all(sent, "seq", split_axis=0, concat_axis=0, tiled=True)
        got = got.reshape(self.group, self.subs, self.per, width)
        got = lax.dynamic_slice(
            got, (0, self.at_seq // self.sources, 0, 0), (self.group, 1, self.per, width)
        )
        return got.reshape(self.rows, width)

    def swap(self, value, turn):
        if turn == 0:
            return value
        return lax.ppermute(value, "group", [(i, i ^ turn) for i in range(self.group)])

    def gather_any(self, rows):
        return jnp.concatenate([self.swap(rows, turn) for turn in range(self.group)], axis=0)

    def reduce_any(self, partial, beside=()):
        got = []
        for turn in range(1, self.group):
            sent = partial[turn * self.rows : (turn + 1) * self.rows].astype(bf16)
            got.append(self.swap(sent, turn))
        got, beside = lax.optimization_barrier((got, beside))
        total = partial[: self.rows]
        for part in got:
            total = total + part.astype(f32)
        return total, beside

    def gather_places(self, rows, beside=()):
        width = rows.shape[1]
        got = [self.swap(rows, turn) for turn in range(1, self.group)]
        got, beside = lax.optimization_barrier((got, beside))
        lane = jnp.zeros((self.sources, self.group, self.per, width), rows.dtype)
        for turn, part in enumerate([rows] + got):
            part = part.reshape(self.sources, 1, self.per, width)
            lane = lax.dynamic_update_slice(lane, part, (0, self.part ^ turn, 0, 0))
        return lane.reshape(-1, width), beside

    def reduce_places(self, partial, beside=()):
        width = partial.shape[1]
        lane = partial.reshape(self.sources, self.group, self.per, width)
        parts = [
            lax.dynamic_slice(
                lane, (0, self.part ^ turn, 0, 0), (self.sources, 1, self.per, width)
            ).reshape(self.rows, width)
            for turn in range(self.group)
        ]
        got = [self.swap(parts[turn].astype(bf16), turn) for turn in range(1, self.group)]
        got, beside = lax.optimization_barrier((got, beside))
        total = parts[0]
        for part in got:
            total = total + part.astype(f32)
        return total, beside

    def gather_parts(self, value):
        if self.group == 4 and value.ndim == 2 and value.shape[0] % 2 == 0:
            rows = value.shape[0] // 2
            one, two = self.swap(value, 1), self.swap(value, 2)
            three = jnp.concatenate([self.swap(two[:rows], 1), self.swap(one[rows:], 2)], axis=0)
            turns = (value, one, two, three)
        else:
            turns = tuple(self.swap(value, turn) for turn in range(self.group))
        parts = jnp.zeros((self.group,) + value.shape, value.dtype)
        for turn in range(self.group):
            parts = lax.dynamic_update_slice(
                parts, turns[turn][None], (self.part ^ turn,) + (0,) * value.ndim
            )
        return parts

    def to_lane(self, rows):
        if self.subs == 1:
            return rows
        every = lax.all_gather(rows, "seq", axis=0, tiled=True)
        length = rows.shape[0] * self.subs
        return lax.dynamic_slice(
            every, ((self.at_seq // self.subs) * length, 0), (length, rows.shape[1])
        )

    def to_own(self, lane_rows):
        if self.subs == 1:
            return lane_rows
        length = lane_rows.shape[0] // self.subs
        return lax.dynamic_slice(lane_rows, (self.sub * length, 0), (length, lane_rows.shape[1]))

    def head_columns(self, array, sections):
        pieces = []
        for begin, width in sections:
            for turn in range(self.heads):
                pieces.append(
                    lax.dynamic_slice(
                        array,
                        (0, begin + (turn * self.group + self.part) * width),
                        (array.shape[0], width),
                    )
                )
        return jnp.concatenate(pieces, axis=1)

    def core_rows(self, array, core):
        split = array.reshape(self.seq, self.cores, -1, array.shape[1])
        return lax.dynamic_index_in_dim(split, core, 1, keepdims=False).reshape(-1, array.shape[1])

    def core_sum(self, grad):
        if self.cores != 2:
            return grad
        got = lax.ppermute(self.core_rows(grad, 1 - self.core), "wshard", [(0, 1), (1, 0)])
        return (self.core_rows(grad, self.core).astype(f32) + got.astype(f32)).astype(bf16)

    def core_columns(self, array):
        if self.cores != 2:
            return (array,)
        rows, columns = array.shape
        run = columns // (self.seq * 2)
        picked = []
        for core in (1 - self.core, self.core):
            picked.append(
                jnp.concatenate(
                    [
                        lax.dynamic_slice(array, (0, (2 * place + core) * run), (rows, run))
                        for place in range(self.seq)
                    ],
                    axis=1,
                )
            )
        return tuple(picked)

    def weight_grad(self, lefts, right):
        if self.cores != 2:
            return dot_t(lefts[0], right).astype(bf16)
        got = lax.ppermute(dot_t(lefts[0], right).astype(bf16), "wshard", [(0, 1), (1, 0)])
        return (dot_t(lefts[1], right) + got.astype(f32)).astype(bf16)

    def scatter(self, grad):
        axes = "seq" if self.cores == 2 else SHARDED
        return lax.psum_scatter(grad, axes, scatter_dimension=0, tiled=True)

    def out_rows(self, w_out):
        width = w_out.shape[1]
        if self.subs == 1 and self.cores == 2:
            mine = lax.dynamic_slice(w_out, ((self.part % 2) * DV, 0), (DV, width))
            half = DV // 2
            kept = lax.dynamic_slice(mine, (self.core * half, 0), (half, width))
            other = lax.dynamic_slice(mine, ((1 - self.core) * half, 0), (half, width))
            got = lax.ppermute(other, "wshard", [(0, 1), (1, 0)])
            piece = jnp.where(self.core == self.part // 2, kept, got)
            return lax.all_gather(piece, SHARDED, axis=0, tiled=True)
        every = lax.all_gather(w_out, SHARDED, axis=0, tiled=True)
        every = every.reshape(self.heads, self.group, DV, width)
        return lax.dynamic_slice(
            every, (0, self.part, 0, 0), (self.heads, 1, DV, width)
        ).reshape(-1, width)

    def out_grad(self, gated, d_branch):
        if self.subs == 1 and self.cores == 2:
            return self.weight_grad(self.core_columns(gated), d_branch)
        width = d_branch.shape[1]
        grad = dot_t(gated, d_branch).astype(bf16)
        every = jnp.zeros((self.heads, self.group, DV, width), bf16)
        every = lax.dynamic_update_slice(
            every, grad.reshape(self.heads, 1, DV, width), (0, self.part, 0, 0)
        ).reshape(-1, width)
        return self.core_sum(every)

    def out_rows_join(self, shard):
        width = shard.shape[1]
        if self.subs == 1 and self.cores == 2:
            halves_all = self.gather_parts(shard)
            here = lax.dynamic_slice(halves_all, (2 * self.core, 0, 0), (2, DV // 2, width))
            there = lax.dynamic_slice(halves_all, (2 - 2 * self.core, 0, 0), (2, DV // 2, width))
            got = lax.ppermute(there, "wshard", [(0, 1), (1, 0)])
            first = jnp.where(self.core == 0, here, got)
            second = jnp.where(self.core == 0, got, here)
            return jnp.stack([first, second], axis=1).reshape(2 * DV, width).astype(f32)
        return lax.psum(shard, "group").astype(f32)

    def conv_pieces(self, conv_w):
        if self.subs > 1:
            return conv_w
        columns = conv_w.shape[1]
        wide = lax.dynamic_slice(conv_w, (0, self.part * DV), (CONV, DV))
        narrow = self.head_columns_of(conv_w, DK)
        return jnp.where(self.at_seq * self.cores + self.core >= 2 * HK // columns, wide, narrow)

    def head_columns_of(self, array, head_width):
        count = array.shape[1] // (self.group * head_width)
        return jnp.concatenate(
            [
                lax.dynamic_slice(
                    array,
                    (0, (turn * self.group + self.part) * head_width),
                    (array.shape[0], head_width),
                )
                for turn in range(count)
            ],
            axis=1,
        )

    def join_conv(self, pieces):
        pieces = pieces.reshape(self.seq * self.cores, CONV, -1).transpose(1, 0, 2)
        pieces = pieces.reshape(CONV, -1)
        return self.head_columns(pieces, QKV) if self.subs > 1 else pieces

    def split_conv(self, grad):
        devices = self.seq * self.cores
        if self.subs > 1:
            pieces, begin = [], 0
            mine = (jnp.arange(self.group) == self.part).astype(f32)[:, None]
            for _, head_width in QKV:
                end = begin + self.heads * head_width
                section = grad[:, begin:end].reshape(CONV, self.heads, 1, head_width) * mine
                pieces.append(section.reshape(CONV, -1))
                begin = end
            grad = jnp.concatenate(pieces, axis=1)
        return grad.reshape(CONV, devices, -1).transpose(1, 0, 2).reshape(devices, -1)

    def join_own_conv(self, parts):
        parts = parts.reshape(self.group, CONV, -1)
        if self.subs > 1:
            return jnp.sum(parts, axis=0)
        columns = parts.shape[2] * self.group
        wide = parts.transpose(1, 0, 2).reshape(CONV, columns)
        narrow = parts.reshape(self.group, CONV, -1, DK).transpose(1, 2, 0, 3).reshape(CONV, columns)
        return jnp.where(self.at_seq * self.cores + self.core >= 2 * HK // columns, wide, narrow)


QKV = ((0, DK), (HK, DK), (2 * HK, DV))
GATE = ((2 * HK + HV, DV),)


def side_array(lane_lengths, length):
    ends = jnp.cumsum(lane_lengths)
    bounds = jnp.concatenate([jnp.zeros((1,), jnp.int32), ends])
    places = jnp.arange(length, dtype=jnp.int32)
    crossed = places[:, None] >= bounds[None, :]
    block_begin = (places // SPAN) * SPAN
    counted = jnp.sum((crossed & (bounds[None, :] >= block_begin[:, None])).astype(jnp.int32), axis=1)
    segment = jnp.sum(crossed.astype(jnp.int32), axis=1)
    columns = [counted.astype(f32)]
    for back in range(1, CONV):
        earlier = jnp.sum((places[:, None] - back >= bounds[None, :]).astype(jnp.int32), axis=1)
        columns.append(((earlier == segment) & (places >= back)).astype(f32))
    columns.append((places < ends[-1]).astype(f32))
    columns += [jnp.zeros((length,), f32)] * (SIDE - len(columns))
    return jnp.stack(columns, axis=1)


def shards(
    tokens,
    cotangent,
    dealing,
    lengths,
    attn_gain,
    w_in,
    w_ab,
    conv_w,
    decay_log,
    dt_bias,
    o_gain,
    w_out,
    ffn_gain,
    w_gu,
    w_down,
):
    rows, width = tokens.shape
    at = Place(rows)
    heads = at.heads
    device_rows = w_down.shape[0]
    devices = at.seq * at.cores

    at_device = at.at_seq * at.cores + at.core

    pieces = []
    for begin, piece_width in QKV + GATE:
        pieces += [
            (begin + turn * at.group * piece_width, piece_width) for turn in range(heads)
        ]
    in_piece = pick_columns(w_in, tuple(pieces), at.group)

    ab_shard = at.head_columns(w_ab, ((0, 1), (H, 1)))
    conv_pieces = at.conv_pieces(conv_w)
    small = (attn_gain, ffn_gain, o_gain, ab_shard.reshape(-1), conv_pieces.reshape(-1))
    lengths_small = [array.shape[0] for array in small]
    filled = sum(lengths_small)
    rows_small = -(-filled // (16 * 128)) * 16
    packed = jnp.concatenate(small + (jnp.zeros((rows_small * 128 - filled,), bf16),))
    packed, in_piece = lax.optimization_barrier((packed, in_piece))
    in_mine = lax.all_gather(in_piece, SHARDED, axis=0, tiled=True)
    packed = small_gather(packed.reshape(rows_small, 128), at.seq, at.cores)
    packed, tokens, cotangent = lax.optimization_barrier((packed, tokens, cotangent))
    packed = packed.reshape(devices, -1)
    full, begin = [], 0
    for count in lengths_small:
        full.append(packed[:, begin : begin + count])
        begin += count
    attn_f, ffn_f, o_f = (array.reshape(-1).astype(f32) for array in full[:3])
    ab_mine = full[3].reshape(width, 2 * heads)
    conv_mine = at.join_conv(full[4]).astype(f32)

    def my_heads(values):
        return lax.dynamic_slice(values.reshape(heads, at.group), (0, at.part), (heads, 1)).reshape(1, -1)

    decay_mine, dt_mine = my_heads(decay_log), my_heads(dt_bias)

    member = (dealing[:, None] == jnp.arange(at.group, dtype=jnp.int32)[None, :]).astype(jnp.int32)
    before = dot(jnp.tril(jnp.ones((rows, rows), f32), -1).astype(bf16), member.astype(bf16))
    before = before.astype(jnp.int32)
    target = jnp.sum((before + at.per * jnp.arange(at.group, dtype=jnp.int32)) * member, axis=1)
    sorting = (target[None, :] == jnp.arange(rows, dtype=jnp.int32)[:, None]).astype(bf16)
    tokens_f = at.deal(dot(sorting, tokens).astype(bf16)).astype(f32)
    normed = rms_scale(tokens_f, attn_f).astype(bf16)
    normed, cotangent, w_out, w_gu, w_down = lax.optimization_barrier(
        (normed, cotangent, w_out, w_gu, w_down)
    )
    normed_all, _ = at.gather_places(normed)
    normed_all, normed_cores = lax.optimization_barrier(
        (normed_all, at.core_columns(normed_all))
    )

    out_mine = at.out_rows(w_out)
    piece = device_rows // at.group
    gu_pieces = tuple((block * device_rows, piece) for block in range(2 * devices))
    gu_mine = lax.all_gather(
        pick_columns(w_gu, gu_pieces, at.group), SHARDED, axis=0, tiled=True
    )
    down_mine = lax.all_gather(
        lax.dynamic_slice(w_down, (at.part * piece, 0), (piece, width)), SHARDED, axis=0, tiled=True
    )
    cot_own = at.deal(dot(sorting, cotangent).astype(bf16))
    normed_all, cot_own = lax.optimization_barrier((normed_all, cot_own))

    lane_lengths = lax.dynamic_index_in_dim(
        at.gather_parts(lengths.reshape(-1)), at.at_seq // at.subs, 0, keepdims=False
    )
    side = side_array(lane_lengths, at.lane)
    gates_ab = at.to_lane(dot(normed_all, ab_mine))
    proj, cot_own = lax.optimization_barrier((dot(normed_all, in_mine), cot_own))
    cot_all = at.gather_any(cot_own)
    proj = at.to_lane(proj)
    mixer_args = (proj, gates_ab, side, conv_mine, o_f[None], decay_mine, dt_mine)
    gated_lane, *kept = mixer_forward(*mixer_args)
    gated_lane, cot_all = lax.optimization_barrier((gated_lane, cot_all))
    gated = at.to_own(gated_lane)
    branch, _ = at.reduce_places(dot(gated, out_mine))
    resid = tokens_f + branch

    normed2_f, pull_norm2 = jax.vjp(rms_scale, resid, ffn_f)
    normed2_all = at.gather_any(normed2_f.astype(bf16))
    normed2_all, normed2_cores = lax.optimization_barrier(
        (normed2_all, at.core_columns(normed2_all))
    )
    gate_up = dot(normed2_all, gu_mine)
    hidden_f, pull_ffn = jax.vjp(swiglu, gate_up)
    hidden = hidden_f.astype(bf16)

    d_down = at.core_sum(dot_t(hidden, cot_all).astype(bf16))
    d_down, hidden, cot_back = lax.optimization_barrier((d_down, hidden, cot_all))
    down_shard = at.scatter(d_down)
    d_hidden = dot_back(cot_back, down_mine)
    d_gate_up = pull_ffn(d_hidden)[0].astype(bf16)
    d_normed2_parts = dot_back(d_gate_up, gu_mine)
    d_normed2_parts, d_gate_up = lax.optimization_barrier((d_normed2_parts, d_gate_up))
    d_gu = at.weight_grad(normed2_cores, d_gate_up)
    d_normed2, d_gu = at.reduce_any(d_normed2_parts, d_gu)
    d_gu, down_shard = lax.optimization_barrier((d_gu, down_shard))
    gu_shard = at.scatter(d_gu)
    d_resid_norm, d_ffn_gain = pull_norm2(d_normed2)
    d_resid = cot_own.astype(f32) + d_resid_norm

    d_branch_all, output_parts = at.gather_places(d_resid.astype(bf16), dot(hidden, down_mine))
    d_gated = dot_back(d_branch_all, out_mine)
    d_gated, output_parts, down_shard = lax.optimization_barrier(
        (d_gated, output_parts, down_shard)
    )
    output_sum, _ = at.reduce_any(output_parts)
    down_parts = at.gather_parts(down_shard)
    d_proj_lane, d_gates_lane, d_conv_w, d_o_gain, d_heads = mixer_backward(
        *mixer_args, tuple(kept), at.to_lane(d_gated)
    )
    d_proj_lane, output_sum, down_parts = lax.optimization_barrier(
        (d_proj_lane, output_sum, down_parts)
    )
    once = (at.sub == 0).astype(f32)
    d_conv_w, d_o_gain, d_heads = d_conv_w * once, d_o_gain * once, d_heads * once
    d_proj = at.to_own(d_proj_lane)
    d_ab = at.to_own(d_gates_lane).astype(bf16)
    d_in = at.weight_grad(normed_cores, d_proj)
    d_in, d_proj, d_ab, d_branch_all, output_sum, gu_shard = lax.optimization_barrier(
        (d_in, d_proj, d_ab, d_branch_all, output_sum, gu_shard)
    )
    in_shard = at.scatter(d_in)
    output = at.undeal((resid + output_sum).astype(bf16))
    d_normed_parts = dot_back(d_proj, in_mine) + dot_back(d_ab, ab_mine)
    d_normed_parts, d_branch_all, d_ab = lax.optimization_barrier(
        (d_normed_parts, d_branch_all, d_ab)
    )
    d_normed, (d_out, d_w_ab) = at.reduce_places(
        d_normed_parts, (at.out_grad(gated, d_branch_all), dot_t(normed_all, d_ab))
    )
    d_normed, gu_shard, output = lax.optimization_barrier((d_normed, gu_shard, output))
    value_norm, pull_norm = jax.vjp(rms_scale, tokens_f, attn_f)
    d_tokens_norm, d_attn_gain = pull_norm(d_normed)
    d_tokens = (d_resid + d_tokens_norm).astype(bf16)

    input_grad = dot_t(sorting, at.undeal(d_tokens)).astype(bf16)
    output = dot_t(sorting, output).astype(bf16)

    def to_blocks(array):
        return array.reshape(devices, -1)

    blocks = (
        to_blocks(d_attn_gain),
        to_blocks(d_ffn_gain),
        to_blocks(d_o_gain),
        to_blocks(d_w_ab),
        at.split_conv(d_conv_w),
        jnp.broadcast_to(d_heads, (devices, 2 * heads)),
    )
    sizes = [array.shape[1] for array in blocks]
    filled = sum(sizes)
    rows_small = -(-filled // 1024) * 8
    packed = jnp.concatenate(
        blocks + (jnp.zeros((devices, rows_small * 128 - filled), f32),), axis=1
    )
    summed = small_sum(packed.reshape(devices, rows_small, 128), at.seq, at.cores, at.group)

    grad_w_gu = join_columns(at.gather_parts(gu_shard), ((piece, 2 * devices),))
    grad_w_down = down_parts.reshape(device_rows, width).astype(f32)
    in_shard, summed, input_grad, d_out = lax.optimization_barrier(
        (in_shard, summed, input_grad, d_out)
    )
    out_shard = at.scatter(d_out)
    grad_w_in = join_columns(
        at.gather_parts(in_shard), tuple((piece_width, heads) for _, piece_width in QKV + GATE)
    )
    grad_w_out = at.out_rows_join(out_shard)

    summed = summed.reshape(at.group, -1)
    parts, begin = [], 0
    for size in sizes:
        parts.append(summed[:, begin : begin + size])
        begin += size
    grad_w_ab = parts[3].reshape(at.group, width // devices, 2, heads).transpose(1, 2, 3, 0)
    grad_heads = parts[5].reshape(at.group, 2, heads).transpose(1, 2, 0).reshape(2, H)
    return (
        output,
        input_grad,
        jnp.sum(parts[0], axis=0),
        grad_w_in,
        grad_w_ab.reshape(width // devices, 2 * H),
        at.join_own_conv(parts[4]),
        grad_heads[0],
        grad_heads[1],
        jnp.sum(parts[2], axis=0),
        grad_w_out,
        jnp.sum(parts[1], axis=0),
        grad_w_gu,
        grad_w_down,
    )


def solution(mesh):
    placed = (
        P(("group", "seq", "wshard"), None),
        P(("group", "seq", "wshard"), None),
        P(("group", "seq", "wshard")),
        P("group", "wshard", None),
        P(("seq", "wshard")),
        P(("seq", "wshard"), None),
        P(("seq", "wshard"), None),
        P(None, ("seq", "wshard")),
        P(),
        P(),
        P(("seq", "wshard")),
        P(("seq", "wshard"), None),
        P(("seq", "wshard")),
        P(("seq", "wshard"), None),
        P(("seq", "wshard"), None),
    )
    return jax.shard_map(
        shards,
        mesh=mesh,
        in_specs=placed,
        out_specs=(
            P(("group", "seq", "wshard"), None),
            P(("group", "seq", "wshard"), None),
            P(("seq", "wshard")),
            P(("seq", "wshard"), None),
            P(("seq", "wshard"), None),
            P(None, ("seq", "wshard")),
            P(),
            P(),
            P(("seq", "wshard")),
            P(("seq", "wshard"), None),
            P(("seq", "wshard")),
            P(("seq", "wshard"), None),
            P(("seq", "wshard"), None),
        ),
        check_vma=False,
    )
```

```python
import functools

import jax
import jax.numpy as jnp
from jax import lax
from jax.experimental import pallas as pl
from jax.experimental.pallas import tpu as pltpu
from jax.sharding import PartitionSpec as P

H = 16
DK = 128
DV = 256
FF = 5632
CONV = 4
SPAN = 64
HK = 2048
HV = 4096
SIDE = 16
EDGE = 32

bf16 = jnp.bfloat16
f32 = jnp.float32
eps_norm = 1e-06


def mm(left, right, over=((1,), (0,))):
    return lax.dot_general(left, right, (over, ((), ())), preferred_element_type=f32)


def halves(value):
    high = value.astype(bf16)
    return high, (value - high.astype(f32)).astype(bf16)


def mm_fine(left, right):
    left_high, left_low = halves(left)
    right_high, right_low = halves(right)
    return mm(left_high, right_high) + mm(left_low, right_high) + mm(left_high, right_low)


def mm_right(left, right, over=((1,), (0,))):
    return mm(left, right.astype(bf16), over)


def mm_both(left, right, over=((1,), (0,))):
    return mm(left.astype(bf16), right.astype(bf16), over)


ROWS = ((1,), (1,))
COLS = ((0,), (0,))


def unit_lower_inverses(stricts):
    groups = EDGE // 8
    count = SPAN // EDGE
    places = lax.broadcasted_iota(jnp.int32, (8, EDGE), 0)
    columns = lax.broadcasted_iota(jnp.int32, (8, EDGE), 1)
    blocks = {}
    for at, strict in enumerate(stricts):
        for block in range(count):
            begin = block * EDGE
            blocks[at, block] = (
                strict[begin : begin + EDGE, begin : begin + EDGE],
                [(places + 8 * part == columns).astype(f32) for part in range(groups)],
            )
    for row in range(EDGE - 1):
        first = row // 8
        for own, done in blocks.values():
            line = done[first][row - 8 * first : row - 8 * first + 1, :]
            for part in range(first, groups):
                column = own[8 * part : 8 * part + 8, row : row + 1]
                done[part] = done[part] - column * line
    inverses = []
    for at, strict in enumerate(stricts):
        parts = [jnp.concatenate(blocks[at, block][1], axis=0) for block in range(count)]
        size = EDGE
        while size < SPAN:
            joined = []
            for pair in range(0, len(parts), 2):
                begin = pair * size
                below = strict[begin + size : begin + 2 * size, begin : begin + size]
                upper, lower = parts[pair], parts[pair + 1]
                corner = mm_fine(mm_fine(lower, below), upper)
                joined.append(
                    jnp.concatenate(
                        [
                            jnp.concatenate([upper, jnp.zeros((size, size), f32)], axis=1),
                            jnp.concatenate([-corner, lower], axis=1),
                        ],
                        axis=0,
                    )
                )
            parts = joined
            size *= 2
        inverses.append(parts[0])
    return inverses


def in_turns(workers):
    workers = list(workers)
    while workers:
        for worker in list(workers):
            if next(worker, workers) is workers:
                workers.remove(worker)


def silu_parts(value):
    rate = 1.0 / (1.0 + jnp.exp(-value))
    return value * rate, rate


def gate_terms(heads, gates, decay_log, dt_bias):
    shifted = gates[:, :heads] + dt_bias
    beta = 1.0 / (1.0 + jnp.exp(-gates[:, heads:]))
    soft = jnp.maximum(shifted, 0.0) + jnp.log1p(jnp.exp(-jnp.abs(shifted)))
    return shifted, beta, -jnp.exp(decay_log) * soft


def ones_left(ones, value):
    high, rest = halves(value)
    high_f = high.astype(f32)
    rest, low = halves(value - high_f)
    return mm(ones, high) + mm(ones, rest) + mm(ones, low)


def triangle(upper):
    at_i = lax.broadcasted_iota(jnp.int32, (SPAN, SPAN), 0)
    at_j = lax.broadcasted_iota(jnp.int32, (SPAN, SPAN), 1)
    return jnp.where(at_i <= at_j if upper else at_i >= at_j, 1.0, 0.0).astype(bf16)


def side_columns(heads, gates, side, decay_log, dt_bias):
    shifted, beta, decay = gate_terms(heads, gates, decay_log, dt_bias)
    running = ones_left(triangle(False), decay)
    cols = jnp.concatenate(
        [running, beta, side[:, :CONV], jnp.zeros((SPAN, 128 - 2 * heads - CONV), f32)], axis=1
    )
    return cols, cols.T, shifted, beta, decay


EDGE_ROWS = 16


def shifted_rows(current, before, side):
    at_i = lax.broadcasted_iota(jnp.int32, (SPAN, SPAN + EDGE_ROWS), 0)
    at_j = lax.broadcasted_iota(jnp.int32, (SPAN, SPAN + EDGE_ROWS), 1)
    moves = [
        jnp.where(at_j == at_i + (EDGE_ROWS - back), side[:, back : back + 1], 0.0).astype(bf16)
        for back in range(1, CONV)
    ]
    moved = mm(jnp.concatenate(moves, axis=0), jnp.concatenate([before, current], axis=0))
    return [moved[(back - 1) * SPAN : back * SPAN, :] for back in range(1, CONV)]


def shifted_back(d_conv, later, same_rows, later_rows):
    at_i = lax.broadcasted_iota(jnp.int32, (SPAN, SPAN + EDGE_ROWS), 0)
    at_j = lax.broadcasted_iota(jnp.int32, (SPAN, SPAN + EDGE_ROWS), 1)
    moves = []
    for back in range(1, CONV):
        same = jnp.concatenate(
            [same_rows[back : back + 1, :], later_rows[back : back + 1, :EDGE_ROWS]], axis=1
        )
        moves.append(jnp.where(at_j == at_i + back, same, 0.0).astype(bf16))
    moved = mm(jnp.concatenate(moves, axis=0), jnp.concatenate([d_conv, later], axis=0))
    return [moved[(back - 1) * SPAN : back * SPAN, :] for back in range(1, CONV)]


def conv_forward(current, moved, taps):
    total = taps[0:1, :] * current
    for back in range(1, CONV):
        total = total + taps[back : back + 1, :] * moved[back - 1]
    return total


def block_terms(head, heads, cols, rows):
    cum_c = cols[:, head : head + 1]
    beta_c = cols[:, heads + head : heads + head + 1]
    count_c = cols[:, 2 * heads : 2 * heads + 1]
    cum_r = rows[head : head + 1, :]
    count_r = rows[2 * heads : 2 * heads + 1, :]
    at_i = lax.broadcasted_iota(jnp.int32, (SPAN, SPAN), 0)
    at_j = lax.broadcasted_iota(jnp.int32, (SPAN, SPAN), 1)
    same = count_c == count_r
    lower_eq = same & (at_i >= at_j)
    lower_st = same & (at_i > at_j)
    fall = jnp.where(lower_eq, jnp.exp(jnp.where(lower_eq, cum_c - cum_r, 0.0)), 0.0)
    growth = jnp.where(count_c == 0.0, jnp.exp(cum_c), 0.0)
    last = SPAN - 1
    tail = jnp.where(
        count_c == count_c[last : last + 1, :], jnp.exp(cum_c[last : last + 1, :] - cum_c), 0.0
    )
    return beta_c, lower_st, fall, growth, tail, growth[last : last + 1, :]


def mixer_forward_kernel(
    heads,
    conv_ref,
    gate_ref,
    gates_ref,
    side_ref,
    taps_ref,
    gain_ref,
    log_ref,
    bias_ref,
    gated_ref,
    mixed_ref,
    qkv_ref,
    state_ref,
    inv_ref,
    solved_ref,
    carried,
    before,
):
    @pl.when(pl.program_id(0) == 0)
    def _():
        carried[...] = jnp.zeros_like(carried)
        before[...] = jnp.zeros_like(before)

    side = side_ref[...]
    current = conv_ref[...].astype(bf16)
    moved = shifted_rows(current, before[...], side)
    act, _ = silu_parts(conv_forward(current.astype(f32), moved, taps_ref[...]))
    before[...] = current[SPAN - EDGE_ROWS :, :]
    cols, rows, _, _, _ = side_columns(heads, gates_ref[...], side, log_ref[...], bias_ref[...])
    valid = side[:, CONV : CONV + 1]
    gain = gain_ref[...]
    scale = DK ** (-0.5)
    terms, units, stricts = [], [], []
    for head in range(heads):
        terms.append(block_terms(head, heads, cols, rows))
        beta_c, lower_st, fall = terms[-1][:3]
        unit = []
        for begin in (head * DK, (heads + head) * DK):
            row = act[:, begin : begin + DK]
            row = row * lax.rsqrt(jnp.sum(row * row, axis=1, keepdims=True) + eps_norm)
            row = row.astype(bf16)
            qkv_ref[:, begin : begin + DK] = row
            unit.append(row)
        units.append(unit)
        stricts.append(jnp.where(lower_st, beta_c * mm(unit[1], unit[1], ROWS) * fall, 0.0))
    inverses = unit_lower_inverses(stricts)

    def one_head(head):
        beta_c, lower_st, fall, growth, tail, kept = terms[head]
        queries, keys = units[head]
        inverse = inverses[head]
        inv_ref[0, head] = inverse
        begin = 2 * heads * DK + head * DV
        values = act[:, begin : begin + DV].astype(bf16)
        qkv_ref[:, begin : begin + DV] = values
        state = carried[head]
        state_ref[0, head] = state
        query_prod = mm(queries, keys, ROWS)
        key_state = mm_right(keys, state)
        query_state = mm_right(queries, state)
        yield
        right_side = beta_c * (values.astype(f32) - growth * key_state)
        yield
        solved = mm_both(inverse, right_side)
        yield
        part = slice(head * DV, (head + 1) * DV)
        solved_ref[:, part] = solved
        inner = mm_both(query_prod * fall, solved)
        yield
        carried[head] = kept * state + mm_both(tail * keys.astype(f32), solved, COLS)
        yield
        mixed = scale * (growth * query_state + inner) * valid
        mixed_ref[:, part] = mixed
        shrink = lax.rsqrt(jnp.mean(mixed * mixed, axis=1, keepdims=True) + eps_norm)
        open_gate, _ = silu_parts(gate_ref[:, part])
        gated_ref[:, part] = (mixed * shrink * gain * open_gate).astype(bf16)
        yield

    in_turns([one_head(head) for head in range(heads)])


def mixer_backward_kernel(
    heads,
    conv_ref,
    ahead_ref,
    gate_ref,
    gates_ref,
    side_ref,
    taps_ref,
    gain_ref,
    log_ref,
    bias_ref,
    mixed_ref,
    qkv_ref,
    state_ref,
    inv_ref,
    solved_ref,
    cot_ref,
    dproj_ref,
    dgates_ref,
    dtaps_ref,
    dgain_ref,
    dheads_ref,
    carried,
    after,
    after_side,
):
    @pl.when(pl.program_id(0) == 0)
    def _():
        carried[...] = jnp.zeros_like(carried)
        after[...] = jnp.zeros_like(after)
        after_side[...] = jnp.zeros_like(after_side)
        dtaps_ref[...] = jnp.zeros_like(dtaps_ref)
        dgain_ref[...] = jnp.zeros_like(dgain_ref)
        dheads_ref[...] = jnp.zeros_like(dheads_ref)

    side = side_ref[...]
    taps = taps_ref[...]
    gain = gain_ref[...]
    valid = side[:, CONV : CONV + 1]
    current = conv_ref[...].astype(bf16)
    moved = shifted_rows(current, ahead_ref[...].astype(bf16), side)
    current = current.astype(f32)
    conv_out = conv_forward(current, moved, taps)
    act, rate = silu_parts(conv_out)
    slope = rate * (1.0 + conv_out * (1.0 - rate))
    cols, rows, shifted, beta_all, decay_all = side_columns(
        heads, gates_ref[...], side, log_ref[...], bias_ref[...]
    )
    scale = DK ** (-0.5)
    at_last = lax.broadcasted_iota(jnp.int32, (SPAN, 1), 0) == SPAN - 1
    d_betas, d_cums, d_gains = [None] * heads, [None] * heads, [None] * heads
    d_queries, d_keys, d_values = [None] * heads, [None] * heads, [None] * heads

    def one_head(head):
        beta_c, lower_st, fall, growth, tail, kept = block_terms(head, heads, cols, rows)
        part = slice(head * DV, (head + 1) * DV)
        mixed = mixed_ref[:, part]
        gate = gate_ref[:, part]
        d_gated = cot_ref[:, part]
        shrink = lax.rsqrt(jnp.mean(mixed * mixed, axis=1, keepdims=True) + eps_norm)
        normal = mixed * shrink
        open_gate, gate_rate = silu_parts(gate)
        with_normal = d_gated * normal
        d_gains[head] = jnp.sum(with_normal * open_gate, axis=0, keepdims=True)
        begin = 2 * heads * DK + (heads + head) * DV
        dproj_ref[:, begin : begin + DV] = (
            with_normal * gain * (gate_rate * (1.0 + gate * (1.0 - gate_rate)))
        ).astype(bf16)
        d_normal = d_gated * gain * open_gate
        d_mixed = shrink * (d_normal - normal * jnp.mean(d_normal * normal, axis=1, keepdims=True))
        d_mixed = (scale * valid) * d_mixed
        yield
        queries = qkv_ref[:, head * DK : (head + 1) * DK]
        keys = qkv_ref[:, (heads + head) * DK : (heads + head + 1) * DK]
        begin = 2 * heads * DK + head * DV
        values = qkv_ref[:, begin : begin + DV]
        keys_f = keys.astype(f32)
        queries_f = queries.astype(f32)
        state = state_ref[0, head]
        inverse = inv_ref[0, head]
        solved = solved_ref[:, part]
        d_state = carried[head]
        key_prod = mm(keys, keys, ROWS)
        query_prod = mm(queries, keys, ROWS)
        strict = jnp.where(lower_st, beta_c * key_prod * fall, 0.0)
        mixing = query_prod * fall
        key_state = mm_right(keys, state)
        query_state = mm_right(queries, state)
        yield
        d_solved = mm_both(mixing, d_mixed, COLS) + mm_both(tail * keys_f, d_state)
        d_mixing = mm_both(d_mixed, solved, ROWS)
        yield
        d_right = mm_both(inverse, d_solved, COLS)
        yield
        d_query_prod = d_mixing * fall
        d_strict = jnp.where(lower_st, -mm_both(d_right, solved, ROWS), 0.0)
        d_key_prod = d_strict * beta_c * fall
        d_key_state = -(beta_c * growth) * d_right
        yield
        carried[head] = (
            kept * d_state
            + mm_both(growth * queries_f, d_mixed, COLS)
            + mm_right(keys, d_key_state, COLS)
        )
        yield
        d_query = mm_both(growth * d_mixed, state, ROWS) + mm_both(d_query_prod, keys_f)
        yield
        both = d_key_prod + d_key_prod.T
        from_tail = mm_both(solved, d_state, ROWS)
        d_key = (
            mm_both(d_key_state, state, ROWS)
            + mm_both(both, keys_f)
            + mm_both(d_query_prod, queries_f, COLS)
            + tail * from_tail
        )
        yield
        residual = values.astype(f32) - growth * key_state
        d_betas[head] = jnp.sum(d_right * residual, axis=1, keepdims=True) + jnp.sum(
            d_strict * key_prod * fall, axis=1, keepdims=True
        )
        spread = d_strict * strict + d_mixing * mixing
        from_last = tail * jnp.sum(keys_f * from_tail, axis=1, keepdims=True)
        d_growth = jnp.sum(d_mixed * query_state, axis=1, keepdims=True) - beta_c * jnp.sum(
            d_right * key_state, axis=1, keepdims=True
        )
        at_end = jnp.sum(from_last, axis=0, keepdims=True) + kept * jnp.sum(
            jnp.sum(d_state * state, axis=1, keepdims=True), axis=0, keepdims=True
        )
        yield
        d_cums[head] = (
            jnp.sum(spread, axis=1, keepdims=True)
            - jnp.sum(spread.T, axis=1, keepdims=True)
            + growth * d_growth
            - from_last
            + jnp.where(at_last, at_end, 0.0)
        )
        yield
        for grads, grad, start in ((d_queries, d_query, head * DK), (d_keys, d_key, (heads + head) * DK)):
            row = act[:, start : start + DK]
            small = lax.rsqrt(jnp.sum(row * row, axis=1, keepdims=True) + eps_norm)
            along = jnp.sum(row * grad, axis=1, keepdims=True) * small * small
            grads[head] = small * (grad - row * along)
        d_values[head] = beta_c * d_right
        yield

    in_turns([one_head(head) for head in range(heads)])
    dgain_ref[...] += sum(d_gains)
    d_conv = jnp.concatenate(d_queries + d_keys + d_values, axis=1) * slope
    d_low = d_conv.astype(bf16)
    same_rows = rows[2 * heads : 2 * heads + CONV, :]
    back_rows = shifted_back(d_low, after[...], same_rows, after_side[...])
    d_in = taps[0:1, :] * d_conv
    d_taps = [jnp.sum(d_conv * current, axis=0, keepdims=True)]
    for back in range(1, CONV):
        d_taps.append(jnp.sum(d_conv * moved[back - 1], axis=0, keepdims=True))
        d_in = d_in + taps[back : back + 1, :] * back_rows[back - 1]
    dtaps_ref[...] += jnp.concatenate(d_taps, axis=0)
    dproj_ref[:, : heads * (2 * DK + DV)] = d_in.astype(bf16)
    after[...] = d_low[:EDGE_ROWS, :]
    after_side[...] = same_rows
    d_decay = ones_left(triangle(True), jnp.concatenate(d_cums, axis=1))
    d_beta = jnp.concatenate(d_betas, axis=1)
    d_shifted = -d_decay * jnp.exp(log_ref[...]) / (1.0 + jnp.exp(-shifted))
    dgates_ref[...] = jnp.concatenate([d_shifted, d_beta * beta_all * (1.0 - beta_all)], axis=1)
    dheads_ref[...] += jnp.concatenate(
        [
            jnp.sum(d_decay * decay_all, axis=0, keepdims=True),
            jnp.sum(d_shifted, axis=0, keepdims=True),
        ],
        axis=1,
    )


def whole_block(shape):
    return pl.BlockSpec(shape, lambda i: (0,) * len(shape))


MIXER_PARAMS = pltpu.CompilerParams(vmem_limit_bytes=48 * 1024 * 1024)


def mixer_forward(proj, gates, side, taps, gain, decay_log, dt_bias):
    length = proj.shape[0]
    width = taps.shape[1]
    heads = decay_log.shape[1]
    gate_at = width // (heads * DV)
    blocks = length // SPAN
    return pl.pallas_call(
        functools.partial(mixer_forward_kernel, heads),
        grid=(blocks,),
        in_specs=[
            pl.BlockSpec((SPAN, width), lambda i: (i, 0)),
            pl.BlockSpec((SPAN, heads * DV), lambda i: (i, gate_at)),
            pl.BlockSpec((SPAN, 2 * heads), lambda i: (i, 0)),
            pl.BlockSpec((SPAN, SIDE), lambda i: (i, 0)),
            whole_block((CONV, width)),
            whole_block((1, DV)),
            whole_block((1, heads)),
            whole_block((1, heads)),
        ],
        out_specs=[
            pl.BlockSpec((SPAN, heads * DV), lambda i: (i, 0)),
            pl.BlockSpec((SPAN, heads * DV), lambda i: (i, 0)),
            pl.BlockSpec((SPAN, width), lambda i: (i, 0)),
            pl.BlockSpec((1, heads, DK, DV), lambda i: (i, 0, 0, 0)),
            pl.BlockSpec((1, heads, SPAN, SPAN), lambda i: (i, 0, 0, 0)),
            pl.BlockSpec((SPAN, heads * DV), lambda i: (i, 0)),
        ],
        out_shape=[
            jax.ShapeDtypeStruct((length, heads * DV), bf16),
            jax.ShapeDtypeStruct((length, heads * DV), f32),
            jax.ShapeDtypeStruct((length, width), bf16),
            jax.ShapeDtypeStruct((blocks, heads, DK, DV), f32),
            jax.ShapeDtypeStruct((blocks, heads, SPAN, SPAN), f32),
            jax.ShapeDtypeStruct((length, heads * DV), f32),
        ],
        scratch_shapes=[pltpu.VMEM((heads, DK, DV), f32), pltpu.VMEM((EDGE_ROWS, width), bf16)],
        compiler_params=MIXER_PARAMS,
        cost_estimate=pl.CostEstimate(
            flops=length, bytes_accessed=length, transcendentals=0
        ),
        name="mixer_forward",
    )(proj, proj, gates, side, taps, gain, decay_log, dt_bias)


def mixer_backward(proj, gates, side, taps, gain, decay_log, dt_bias, kept, d_gated):
    length = proj.shape[0]
    width = taps.shape[1]
    heads = decay_log.shape[1]
    gate_at = width // (heads * DV)
    blocks = length // SPAN
    end = blocks - 1
    ahead_rows = EDGE_ROWS
    per = SPAN // ahead_rows
    return pl.pallas_call(
        functools.partial(mixer_backward_kernel, heads),
        grid=(blocks,),
        in_specs=[
            pl.BlockSpec((SPAN, width), lambda i: (end - i, 0)),
            pl.BlockSpec((ahead_rows, width), lambda i: (jnp.maximum((end - i) * per - 1, 0), 0)),
            pl.BlockSpec((SPAN, heads * DV), lambda i: (end - i, gate_at)),
            pl.BlockSpec((SPAN, 2 * heads), lambda i: (end - i, 0)),
            pl.BlockSpec((SPAN, SIDE), lambda i: (end - i, 0)),
            whole_block((CONV, width)),
            whole_block((1, DV)),
            whole_block((1, heads)),
            whole_block((1, heads)),
            pl.BlockSpec((SPAN, heads * DV), lambda i: (end - i, 0)),
            pl.BlockSpec((SPAN, width), lambda i: (end - i, 0)),
            pl.BlockSpec((1, heads, DK, DV), lambda i: (end - i, 0, 0, 0)),
            pl.BlockSpec((1, heads, SPAN, SPAN), lambda i: (end - i, 0, 0, 0)),
            pl.BlockSpec((SPAN, heads * DV), lambda i: (end - i, 0)),
            pl.BlockSpec((SPAN, heads * DV), lambda i: (end - i, 0)),
        ],
        out_specs=[
            pl.BlockSpec((SPAN, width + heads * DV), lambda i: (end - i, 0)),
            pl.BlockSpec((SPAN, 2 * heads), lambda i: (end - i, 0)),
            whole_block((CONV, width)),
            whole_block((1, DV)),
            whole_block((1, 2 * heads)),
        ],
        out_shape=[
            jax.ShapeDtypeStruct((length, width + heads * DV), bf16),
            jax.ShapeDtypeStruct((length, 2 * heads), f32),
            jax.ShapeDtypeStruct((CONV, width), f32),
            jax.ShapeDtypeStruct((1, DV), f32),
            jax.ShapeDtypeStruct((1, 2 * heads), f32),
        ],
        scratch_shapes=[
            pltpu.VMEM((heads, DK, DV), f32),
            pltpu.VMEM((EDGE_ROWS, width), bf16),
            pltpu.VMEM((CONV, SPAN), f32),
        ],
        compiler_params=MIXER_PARAMS,
        cost_estimate=pl.CostEstimate(
            flops=length, bytes_accessed=length, transcendentals=0
        ),
        name="mixer_backward",
    )(proj, proj, proj, gates, side, taps, gain, decay_log, dt_bias, *kept, d_gated)


MESH = pl.DeviceIdType.MESH


def column_peers(seq, cores):
    count = seq * cores
    me = lax.axis_index("seq") * cores + lax.axis_index("wshard")
    peers = []
    for step in range(1, count):
        place = lax.rem(me + step, count)
        peers.append((place, {"seq": place // cores, "wshard": lax.rem(place, cores)}))
    return me, peers


def greet(ids):
    barrier = pltpu.get_barrier_semaphore()
    for device in ids:
        pl.semaphore_signal(barrier, inc=1, device_id=device, device_id_type=MESH)
    pl.semaphore_wait(barrier, len(ids))


def small_gather_kernel(seq, cores, in_ref, out_ref, send_sem, recv_sem):
    me, peers = column_peers(seq, cores)
    greet([device for _, device in peers])
    copies = []
    for at, (_, device) in enumerate(peers):
        copies.append(
            pltpu.make_async_remote_copy(
                src_ref=in_ref,
                dst_ref=out_ref.at[me],
                send_sem=send_sem.at[at],
                recv_sem=recv_sem.at[at],
                device_id=device,
                device_id_type=MESH,
            )
        )
        copies[-1].start()
    out_ref[me] = in_ref[...]
    for copy in copies:
        copy.wait()


def small_gather(values, seq, cores):
    count = seq * cores
    return pl.pallas_call(
        functools.partial(small_gather_kernel, seq, cores),
        out_shape=jax.ShapeDtypeStruct((count,) + values.shape, values.dtype),
        in_specs=[pl.BlockSpec(memory_space=pltpu.VMEM)],
        out_specs=pl.BlockSpec(memory_space=pltpu.VMEM),
        scratch_shapes=[pltpu.SemaphoreType.DMA((count - 1,)), pltpu.SemaphoreType.DMA((count - 1,))],
        compiler_params=pltpu.CompilerParams(collective_id=0, has_side_effects=True),
        name="small_gather",
    )(values)


def small_sum_kernel(seq, cores, group, in_ref, out_ref, landed, send_sem, recv_sem, plane_send, plane_recv):
    me, peers = column_peers(seq, cores)
    part = lax.axis_index("group")
    plane = [{"group": lax.rem(part + step, group)} for step in range(1, group)]
    greet([device for _, device in peers] + plane)
    copies = []
    for at, (place, device) in enumerate(peers):
        copies.append(
            pltpu.make_async_remote_copy(
                src_ref=in_ref.at[place],
                dst_ref=landed.at[at],
                send_sem=send_sem.at[at],
                recv_sem=recv_sem.at[at],
                device_id=device,
                device_id_type=MESH,
            )
        )
        copies[-1].start()
    total = in_ref[me]
    for at, copy in enumerate(copies):
        copy.wait()
        total = total + landed[at]
    out_ref[part] = total
    copies = []
    for at, device in enumerate(plane):
        copies.append(
            pltpu.make_async_remote_copy(
                src_ref=out_ref.at[part],
                dst_ref=out_ref.at[part],
                send_sem=plane_send.at[at],
                recv_sem=plane_recv.at[at],
                device_id=device,
                device_id_type=MESH,
            )
        )
        copies[-1].start()
    for copy in copies:
        copy.wait()


def small_sum(values, seq, cores, group):
    count = seq * cores
    shape = values.shape[1:]
    return pl.pallas_call(
        functools.partial(small_sum_kernel, seq, cores, group),
        out_shape=jax.ShapeDtypeStruct((group,) + shape, values.dtype),
        in_specs=[pl.BlockSpec(memory_space=pltpu.VMEM)],
        out_specs=pl.BlockSpec(memory_space=pltpu.VMEM),
        scratch_shapes=[
            pltpu.VMEM((count - 1,) + shape, values.dtype),
            pltpu.SemaphoreType.DMA((count - 1,)),
            pltpu.SemaphoreType.DMA((count - 1,)),
            pltpu.SemaphoreType.DMA((group - 1,)),
            pltpu.SemaphoreType.DMA((group - 1,)),
        ],
        compiler_params=pltpu.CompilerParams(collective_id=1, has_side_effects=True),
        name="small_sum",
    )(values)


def plane_gather_kernel(in_ref, out_ref, done, send_sem, recv_sem):
    part = lax.axis_index("group")
    near = part + 1 - 2 * lax.rem(part, 2)
    far = lax.rem(part + 2, 4)
    half = in_ref.shape[0] // 2
    first, second = pl.ds(0, half), pl.ds(half, half)
    greet([{"group": near}, {"group": far}])

    def send(source, block, rows, target, at):
        copy = pltpu.make_async_remote_copy(
            src_ref=source,
            dst_ref=out_ref.at[block, rows],
            send_sem=send_sem.at[at],
            recv_sem=recv_sem.at[at],
            device_id={"group": target},
            device_id_type=MESH,
        )
        copy.start()
        return copy

    copies = [
        send(in_ref.at[second], part, second, near, 0),
        send(in_ref.at[first], part, first, far, 1),
        send(in_ref.at[first], part, first, near, 2),
        send(in_ref.at[second], part, second, far, 3),
    ]
    own = pltpu.make_async_copy(in_ref, out_ref.at[part], done)
    own.start()
    copies[1].wait_recv()
    copies.append(send(out_ref.at[far, first], far, first, near, 4))
    copies[0].wait_recv()
    copies.append(send(out_ref.at[near, second], near, second, far, 5))
    for at, copy in enumerate(copies):
        copy.wait_send()
        if at >= 2:
            copy.wait_recv()
    own.wait()


def plane_gather(value):
    return pl.pallas_call(
        plane_gather_kernel,
        out_shape=jax.ShapeDtypeStruct((4,) + value.shape, value.dtype),
        in_specs=[pl.BlockSpec(memory_space=pltpu.VMEM)],
        out_specs=pl.BlockSpec(memory_space=pltpu.VMEM),
        scratch_shapes=[
            pltpu.SemaphoreType.DMA,
            pltpu.SemaphoreType.DMA((6,)),
            pltpu.SemaphoreType.DMA((6,)),
        ],
        compiler_params=pltpu.CompilerParams(
            collective_id=2, has_side_effects=True, vmem_limit_bytes=32 * 1024 * 1024
        ),
        name="plane_gather",
    )(value)


def pick_columns_kernel(pieces, group, array_ref, out_ref):
    part = lax.axis_index("group")
    for own in range(group):

        @pl.when(part == own)
        def _():
            out_ref[...] = jnp.concatenate(
                [
                    array_ref[:, first + own * width : first + (own + 1) * width]
                    for first, width in pieces
                ],
                axis=1,
            )


def pick_columns(array, pieces, group):
    rows, columns = array.shape
    step = min(rows, 64)
    picked = sum(width for _, width in pieces)
    return pl.pallas_call(
        functools.partial(pick_columns_kernel, pieces, group),
        grid=(rows // step,),
        in_specs=[pl.BlockSpec((step, columns), lambda i: (i, 0))],
        out_specs=pl.BlockSpec((step, picked), lambda i: (i, 0)),
        out_shape=jax.ShapeDtypeStruct((rows, picked), array.dtype),
        compiler_params=MIXER_PARAMS,
        name="pick_columns",
    )(array)


def join_columns_kernel(group, runs, parts_ref, *refs):
    out_ref = refs[-1]
    source, target = 0, 0
    for width, count in runs:
        pack = 1
        while pack < count and (pack * group * width) % 128:
            pack *= 2
        for first in range(0, count, pack):
            pieces = []
            for run in range(first, first + pack):
                for part in range(group):
                    begin = source + run * width
                    pieces.append(parts_ref[part, :, begin : begin + width].astype(f32))
            size = pack * group * width
            out_ref[:, target : target + size] = jnp.concatenate(pieces, axis=1)
            target += size
        source += count * width


def join_columns(parts, runs, total_rows=None, into=None):
    group, rows, columns = parts.shape
    step = min(rows, 32)
    total_rows = into.shape[0] if into is not None else total_rows or rows
    first = (total_rows - rows) // step if into is not None else 0
    args, specs, aliases = (parts,), [pl.BlockSpec((group, step, columns), lambda i: (0, i, 0))], {}
    if into is not None:
        args, aliases = (parts, into), {1: 0}
        specs.append(pl.BlockSpec(memory_space=pl.ANY))
    return pl.pallas_call(
        functools.partial(join_columns_kernel, group, runs),
        grid=(rows // step,),
        in_specs=specs,
        out_specs=pl.BlockSpec((step, group * columns), lambda i: (first + i, 0)),
        out_shape=jax.ShapeDtypeStruct((total_rows, group * columns), f32),
        input_output_aliases=aliases,
        compiler_params=MIXER_PARAMS,
        name="join_columns",
    )(*args)


def rms_scale(values, gain):
    return values * lax.rsqrt(jnp.mean(values * values, axis=-1, keepdims=True) + eps_norm) * gain


def swiglu(gate_up):
    half = gate_up.shape[1] // 2
    return jax.nn.silu(gate_up[:, :half]) * gate_up[:, half:]


def sum_parts(own, others):
    total = own.astype(f32)
    for part in others:
        total = total + part.astype(f32)
    return total


def dot(left, right):
    return jnp.dot(left, right, preferred_element_type=f32)


def dot_t(left, right):
    return lax.dot_general(left, right, (((0,), (0,)), ((), ())), preferred_element_type=f32)


def dot_back(left, right):
    return lax.dot_general(left, right, (((1,), (1,)), ((), ())), preferred_element_type=f32)


SHARDED = ("seq", "wshard")


class Place:
    def __init__(self, rows):
        self.group = lax.axis_size("group")
        self.seq = lax.axis_size("seq")
        self.cores = lax.axis_size("wshard")
        self.part = lax.axis_index("group")
        self.at_seq = lax.axis_index("seq")
        self.core = lax.axis_index("wshard")
        self.rows = rows
        self.per = rows // self.group
        self.subs = self.seq // self.group
        self.sources = self.seq // self.subs
        self.sub = self.at_seq % self.subs
        self.heads = H // self.group
        self.lane = self.seq * rows

    def deal(self, sorted_rows):
        width = sorted_rows.shape[1]
        if self.subs == 1:
            return lax.all_to_all(sorted_rows, "seq", split_axis=0, concat_axis=0, tiled=True)
        sent = jnp.zeros((self.group, self.subs, self.per, width), sorted_rows.dtype)
        sent = lax.dynamic_update_slice(
            sent,
            sorted_rows.reshape(self.group, 1, self.per, width),
            (0, self.at_seq // self.sources, 0, 0),
        )
        got = lax.all_to_all(
            sent.reshape(-1, width), "seq", split_axis=0, concat_axis=0, tiled=True
        )
        return lax.dynamic_slice(got, (self.sub * self.rows, 0), (self.rows, width))

    def undeal(self, rows):
        width = rows.shape[1]
        if self.subs == 1:
            return lax.all_to_all(rows, "seq", split_axis=0, concat_axis=0, tiled=True)
        sent = jnp.zeros((self.subs * self.rows, width), rows.dtype)
        sent = lax.dynamic_update_slice(sent, rows, (self.sub * self.rows, 0))
        got = lax.all_to_all(sent, "seq", split_axis=0, concat_axis=0, tiled=True)
        got = got.reshape(self.group, self.subs, self.per, width)
        got = lax.dynamic_slice(
            got, (0, self.at_seq // self.sources, 0, 0), (self.group, 1, self.per, width)
        )
        return got.reshape(self.rows, width)

    def swap(self, value, turn):
        if turn == 0:
            return value
        return lax.ppermute(value, "group", [(i, i ^ turn) for i in range(self.group)])

    def gather_any(self, rows):
        return jnp.concatenate([self.swap(rows, turn) for turn in range(self.group)], axis=0)

    def send_any(self, partial):
        own = partial[: self.rows]
        got = [
            self.swap(partial[turn * self.rows : (turn + 1) * self.rows], turn)
            for turn in range(1, self.group)
        ]
        return own, got

    def gather_places(self, rows, beside=()):
        width = rows.shape[1]
        got = [self.swap(rows, turn) for turn in range(1, self.group)]
        got, beside = lax.optimization_barrier((got, beside))
        lane = jnp.zeros((self.sources, self.group, self.per, width), rows.dtype)
        for turn, part in enumerate([rows] + got):
            part = part.reshape(self.sources, 1, self.per, width)
            lane = lax.dynamic_update_slice(lane, part, (0, self.part ^ turn, 0, 0))
        return lane.reshape(-1, width), beside

    def send_places(self, partial):
        width = partial.shape[1]
        lane = partial.reshape(self.sources, self.group, self.per, width)
        parts = [
            lax.dynamic_slice(
                lane, (0, self.part ^ turn, 0, 0), (self.sources, 1, self.per, width)
            ).reshape(self.rows, width)
            for turn in range(self.group)
        ]
        return parts[0], [self.swap(parts[turn], turn) for turn in range(1, self.group)]

    def near_turns(self, value):
        return (value, self.swap(value, 1), self.swap(value, 2))

    def far_turn(self, near):
        rows = near[0].shape[0] // 2
        return near + ((self.swap(near[2][:rows], 1), self.swap(near[1][rows:], 2)),)

    def turns_of(self, value):
        if self.group == 4 and value.ndim == 2 and value.shape[0] % 2 == 0:
            return self.far_turn(self.near_turns(value))
        return tuple(self.swap(value, turn) for turn in range(self.group))

    def by_owner(self, turns):
        value = turns[0]
        parts = jnp.zeros((self.group,) + value.shape, value.dtype)
        for turn, got in enumerate(turns):
            owner, begin = self.part ^ turn, 0
            for piece in got if isinstance(got, tuple) else (got,):
                parts = lax.dynamic_update_slice(
                    parts, piece[None], (owner, begin) + (0,) * (value.ndim - 1)
                )
                begin += piece.shape[0]
        return parts

    def gather_parts(self, value):
        return self.by_owner(self.turns_of(value))

    def to_lane(self, rows):
        if self.subs == 1:
            return rows
        every = lax.all_gather(rows, "seq", axis=0, tiled=True)
        length = rows.shape[0] * self.subs
        return lax.dynamic_slice(
            every, ((self.at_seq // self.subs) * length, 0), (length, rows.shape[1])
        )

    def to_own(self, lane_rows):
        if self.subs == 1:
            return lane_rows
        length = lane_rows.shape[0] // self.subs
        return lax.dynamic_slice(lane_rows, (self.sub * length, 0), (length, lane_rows.shape[1]))

    def head_columns(self, array, sections):
        pieces = []
        for begin, width in sections:
            for turn in range(self.heads):
                pieces.append(
                    lax.dynamic_slice(
                        array,
                        (0, begin + (turn * self.group + self.part) * width),
                        (array.shape[0], width),
                    )
                )
        return jnp.concatenate(pieces, axis=1)

    def core_rows(self, array, core):
        split = array.reshape(self.seq, self.cores, -1, array.shape[1])
        return lax.dynamic_index_in_dim(split, core, 1, keepdims=False).reshape(-1, array.shape[1])

    def core_sum(self, grad):
        if self.cores != 2:
            return grad
        got = lax.ppermute(self.core_rows(grad, 1 - self.core), "wshard", [(0, 1), (1, 0)])
        return (self.core_rows(grad, self.core).astype(f32) + got.astype(f32)).astype(bf16)

    def core_columns(self, array, halves_of=1):
        rows, columns = array.shape
        run = columns // (self.seq * self.cores)
        size = run // halves_of
        out = []
        for half in range(halves_of):
            picked = []
            for core in (1 - self.core, self.core) if self.cores == 2 else range(self.cores):
                picked.append(
                    [
                        lax.dynamic_slice(
                            array,
                            (0, (place * self.cores + core) * run + half * size),
                            (rows, size),
                        )
                        for place in range(self.seq)
                    ]
                )
            if self.cores == 2:
                out.append(tuple(jnp.concatenate(pieces, axis=1) for pieces in picked))
            else:
                every = [pieces[place] for place in range(self.seq) for pieces in picked]
                out.append((jnp.concatenate(every, axis=1),))
        return out

    def other_grad(self, lefts, right):
        if self.cores != 2:
            return None
        return lax.ppermute(dot_t(lefts[0], right).astype(bf16), "wshard", [(0, 1), (1, 0)])

    def own_grad(self, lefts, right, got):
        own = dot_t(lefts[-1], right)
        return (own if got is None else own + got.astype(f32)).astype(bf16)

    def scatter(self, grad):
        axes = "seq" if self.cores == 2 else SHARDED
        return lax.psum_scatter(grad, axes, scatter_dimension=0, tiled=True)

    def out_rows(self, w_out):
        width = w_out.shape[1]
        if self.subs == 1 and self.cores == 2:
            mine = lax.dynamic_slice(w_out, ((self.part % 2) * DV, 0), (DV, width))
            half = DV // 2
            kept = lax.dynamic_slice(mine, (self.core * half, 0), (half, width))
            other = lax.dynamic_slice(mine, ((1 - self.core) * half, 0), (half, width))
            got = lax.ppermute(other, "wshard", [(0, 1), (1, 0)])
            piece = jnp.where(self.core == self.part // 2, kept, got)
            return lax.all_gather(piece, SHARDED, axis=0, tiled=True)
        every = lax.all_gather(w_out, SHARDED, axis=0, tiled=True)
        every = every.reshape(self.heads, self.group, DV, width)
        return lax.dynamic_slice(
            every, (0, self.part, 0, 0), (self.heads, 1, DV, width)
        ).reshape(-1, width)

    def out_grad(self, gated, d_branch):
        if self.subs == 1 and self.cores == 2:
            lefts = self.core_columns(gated)[0]
            return self.own_grad(lefts, d_branch, self.other_grad(lefts, d_branch))
        width = d_branch.shape[1]
        grad = dot_t(gated, d_branch).astype(bf16)
        every = jnp.zeros((self.heads, self.group, DV, width), bf16)
        every = lax.dynamic_update_slice(
            every, grad.reshape(self.heads, 1, DV, width), (0, self.part, 0, 0)
        ).reshape(-1, width)
        return self.core_sum(every)

    def out_rows_join(self, shard):
        width = shard.shape[1]
        if self.subs == 1 and self.cores == 2:
            halves_all = self.gather_parts(shard)
            here = lax.dynamic_slice(halves_all, (2 * self.core, 0, 0), (2, DV // 2, width))
            there = lax.dynamic_slice(halves_all, (2 - 2 * self.core, 0, 0), (2, DV // 2, width))
            got = lax.ppermute(there, "wshard", [(0, 1), (1, 0)])
            first = jnp.where(self.core == 0, here, got)
            second = jnp.where(self.core == 0, got, here)
            return jnp.stack([first, second], axis=1).reshape(2 * DV, width).astype(f32)
        return lax.psum(shard, "group").astype(f32)

    def conv_pieces(self, conv_w):
        if self.subs > 1:
            return conv_w
        columns = conv_w.shape[1]
        wide = lax.dynamic_slice(conv_w, (0, self.part * DV), (CONV, DV))
        narrow = self.head_columns_of(conv_w, DK)
        return jnp.where(self.at_seq * self.cores + self.core >= 2 * HK // columns, wide, narrow)

    def head_columns_of(self, array, head_width):
        count = array.shape[1] // (self.group * head_width)
        return jnp.concatenate(
            [
                lax.dynamic_slice(
                    array,
                    (0, (turn * self.group + self.part) * head_width),
                    (array.shape[0], head_width),
                )
                for turn in range(count)
            ],
            axis=1,
        )

    def join_conv(self, pieces):
        pieces = pieces.reshape(self.seq * self.cores, CONV, -1).transpose(1, 0, 2)
        pieces = pieces.reshape(CONV, -1)
        return self.head_columns(pieces, QKV) if self.subs > 1 else pieces

    def split_conv(self, grad):
        devices = self.seq * self.cores
        if self.subs > 1:
            pieces, begin = [], 0
            mine = (jnp.arange(self.group) == self.part).astype(f32)[:, None]
            for _, head_width in QKV:
                end = begin + self.heads * head_width
                section = grad[:, begin:end].reshape(CONV, self.heads, 1, head_width) * mine
                pieces.append(section.reshape(CONV, -1))
                begin = end
            grad = jnp.concatenate(pieces, axis=1)
        return grad.reshape(CONV, devices, -1).transpose(1, 0, 2).reshape(devices, -1)

    def join_own_conv(self, parts):
        parts = parts.reshape(self.group, CONV, -1)
        if self.subs > 1:
            return jnp.sum(parts, axis=0)
        columns = parts.shape[2] * self.group
        wide = parts.transpose(1, 0, 2).reshape(CONV, columns)
        narrow = parts.reshape(self.group, CONV, -1, DK).transpose(1, 2, 0, 3).reshape(CONV, columns)
        return jnp.where(self.at_seq * self.cores + self.core >= 2 * HK // columns, wide, narrow)


QKV = ((0, DK), (HK, DK), (2 * HK, DV))
GATE = ((2 * HK + HV, DV),)


def side_array(lane_lengths, length):
    ends = jnp.cumsum(lane_lengths)
    bounds = jnp.concatenate([jnp.zeros((1,), jnp.int32), ends])
    places = jnp.arange(length, dtype=jnp.int32)
    crossed = places[:, None] >= bounds[None, :]
    block_begin = (places // SPAN) * SPAN
    counted = jnp.sum((crossed & (bounds[None, :] >= block_begin[:, None])).astype(jnp.int32), axis=1)
    segment = jnp.sum(crossed.astype(jnp.int32), axis=1)
    columns = [counted.astype(f32)]
    for back in range(1, CONV):
        earlier = jnp.sum((places[:, None] - back >= bounds[None, :]).astype(jnp.int32), axis=1)
        columns.append(((earlier == segment) & (places >= back)).astype(f32))
    columns.append((places < ends[-1]).astype(f32))
    columns += [jnp.zeros((length,), f32)] * (SIDE - len(columns))
    return jnp.stack(columns, axis=1)


def shards(
    tokens,
    cotangent,
    dealing,
    lengths,
    attn_gain,
    w_in,
    w_ab,
    conv_w,
    decay_log,
    dt_bias,
    o_gain,
    w_out,
    ffn_gain,
    w_gu,
    w_down,
):
    rows, width = tokens.shape
    at = Place(rows)
    heads = at.heads
    device_rows = w_down.shape[0]
    devices = at.seq * at.cores

    at_device = at.at_seq * at.cores + at.core

    pieces = []
    for begin, piece_width in QKV + GATE:
        pieces += [
            (begin + turn * at.group * piece_width, piece_width) for turn in range(heads)
        ]
    in_piece = pick_columns(w_in, tuple(pieces), at.group)

    ab_shard = at.head_columns(w_ab, ((0, 1), (H, 1)))
    conv_pieces = at.conv_pieces(conv_w)
    small = (attn_gain, ffn_gain, o_gain, ab_shard.reshape(-1), conv_pieces.reshape(-1))
    lengths_small = [array.shape[0] for array in small]
    filled = sum(lengths_small)
    rows_small = -(-filled // (16 * 128)) * 16
    packed = jnp.concatenate(small + (jnp.zeros((rows_small * 128 - filled,), bf16),))
    packed, in_piece = lax.optimization_barrier((packed, in_piece))
    in_mine = lax.all_gather(in_piece, SHARDED, axis=0, tiled=True)
    packed = small_gather(packed.reshape(rows_small, 128), at.seq, at.cores)
    packed, tokens, cotangent = lax.optimization_barrier((packed, tokens, cotangent))
    packed = packed.reshape(devices, -1)
    full, begin = [], 0
    for count in lengths_small:
        full.append(packed[:, begin : begin + count])
        begin += count
    attn_f, ffn_f, o_f = (array.reshape(-1).astype(f32) for array in full[:3])
    ab_mine = full[3].reshape(width, 2 * heads)
    conv_mine = at.join_conv(full[4]).astype(f32)

    def my_heads(values):
        return lax.dynamic_slice(values.reshape(heads, at.group), (0, at.part), (heads, 1)).reshape(1, -1)

    decay_mine, dt_mine = my_heads(decay_log), my_heads(dt_bias)

    member = (dealing[:, None] == jnp.arange(at.group, dtype=jnp.int32)[None, :]).astype(jnp.int32)
    before = dot(jnp.tril(jnp.ones((rows, rows), f32), -1).astype(bf16), member.astype(bf16))
    before = before.astype(jnp.int32)
    target = jnp.sum((before + at.per * jnp.arange(at.group, dtype=jnp.int32)) * member, axis=1)
    sorting = (target[None, :] == jnp.arange(rows, dtype=jnp.int32)[:, None]).astype(bf16)
    tokens_f = at.deal(dot(sorting, tokens).astype(bf16)).astype(f32)
    normed = rms_scale(tokens_f, attn_f).astype(bf16)
    normed, cotangent, w_out, w_gu, w_down = lax.optimization_barrier(
        (normed, cotangent, w_out, w_gu, w_down)
    )
    normed_all, _ = at.gather_places(normed)
    normed_all, normed_cores = lax.optimization_barrier(
        (normed_all, at.core_columns(normed_all)[0])
    )

    out_mine = at.out_rows(w_out)
    piece = device_rows // at.group
    gu_pieces = tuple((block * device_rows, piece) for block in range(2 * devices))
    gu_mine = lax.all_gather(
        pick_columns(w_gu, gu_pieces, at.group), SHARDED, axis=0, tiled=True
    )
    down_mine = lax.all_gather(
        lax.dynamic_slice(w_down, (at.part * piece, 0), (piece, width)), SHARDED, axis=0, tiled=True
    )
    cot_own = at.deal(dot(sorting, cotangent).astype(bf16))
    normed_all, cot_own = lax.optimization_barrier((normed_all, cot_own))

    lane_lengths = lax.dynamic_index_in_dim(
        at.gather_parts(lengths.reshape(-1)), at.at_seq // at.subs, 0, keepdims=False
    )
    side = side_array(lane_lengths, at.lane)
    gates_ab = at.to_lane(dot(normed_all, ab_mine))
    proj, cot_own = lax.optimization_barrier((dot(normed_all, in_mine), cot_own))
    cot_all = at.gather_any(cot_own)
    proj = at.to_lane(proj)
    mixer_args = (proj, gates_ab, side, conv_mine, o_f[None], decay_mine, dt_mine)
    gated_lane, *kept = mixer_forward(*mixer_args)
    gated_lane, cot_all = lax.optimization_barrier((gated_lane, cot_all))
    gated = at.to_own(gated_lane)
    own, got = at.send_places(dot(gated, out_mine).astype(bf16))
    resid = tokens_f + sum_parts(own, got)

    normed2_f, pull_norm2 = jax.vjp(rms_scale, resid, ffn_f)
    normed2_all = at.gather_any(normed2_f.astype(bf16))
    normed2_all, normed2_cores = lax.optimization_barrier(
        (normed2_all, at.core_columns(normed2_all)[0])
    )
    gate_up = dot(normed2_all, gu_mine)
    hidden_f, pull_ffn = jax.vjp(swiglu, gate_up)
    hidden = hidden_f.astype(bf16)

    d_down = at.core_sum(dot_t(hidden, cot_all).astype(bf16))
    d_down, hidden, cot_back = lax.optimization_barrier((d_down, hidden, cot_all))
    down_shard = at.scatter(d_down)
    d_hidden = dot_back(cot_back, down_mine)
    d_gate_up = pull_ffn(d_hidden)[0].astype(bf16)
    d_normed2_parts = dot_back(d_gate_up, gu_mine).astype(bf16)
    d_normed2_parts, d_gate_up = lax.optimization_barrier((d_normed2_parts, d_gate_up))
    own, got = at.send_any(d_normed2_parts)
    d_gu = at.own_grad(normed2_cores, d_gate_up, at.other_grad(normed2_cores, d_gate_up))
    got, d_gu = lax.optimization_barrier((got, d_gu))
    d_gu, down_shard = lax.optimization_barrier((d_gu, down_shard))
    gu_shard = at.scatter(d_gu)
    d_normed2 = sum_parts(own, got)
    d_resid_norm, d_ffn_gain = pull_norm2(d_normed2)
    d_resid = cot_own.astype(f32) + d_resid_norm

    d_branch_all, output_parts = at.gather_places(
        d_resid.astype(bf16), dot(hidden, down_mine).astype(bf16)
    )
    d_gated = dot_back(d_branch_all, out_mine)
    d_gated, output_parts, down_shard = lax.optimization_barrier(
        (d_gated, output_parts, down_shard)
    )
    output_own, output_got = at.send_any(output_parts)
    down_turns = at.near_turns(down_shard)
    d_proj_lane, d_gates_lane, d_conv_w, d_o_gain, d_heads = mixer_backward(
        *mixer_args, tuple(kept), at.to_lane(d_gated)
    )
    d_proj_lane, output_got, down_turns = lax.optimization_barrier(
        (d_proj_lane, output_got, down_turns)
    )
    once = (at.sub == 0).astype(f32)
    d_conv_w, d_o_gain, d_heads = d_conv_w * once, d_o_gain * once, d_heads * once
    d_proj = at.to_own(d_proj_lane)
    d_ab = at.to_own(d_gates_lane).astype(bf16)
    d_in = at.own_grad(normed_cores, d_proj, at.other_grad(normed_cores, d_proj))
    d_in, d_proj, d_ab, d_branch_all, output_got, gu_shard = lax.optimization_barrier(
        (d_in, d_proj, d_ab, d_branch_all, output_got, gu_shard)
    )
    in_shard = at.scatter(d_in)
    output = (resid + sum_parts(output_own, output_got)).astype(bf16)
    d_normed_parts = (dot_back(d_proj, in_mine) + dot_back(d_ab, ab_mine)).astype(bf16)
    d_normed_parts, d_branch_all, d_ab = lax.optimization_barrier(
        (d_normed_parts, d_branch_all, d_ab)
    )
    own, got = at.send_places(d_normed_parts)
    d_out = at.out_grad(gated, d_branch_all)
    d_w_ab = dot_t(normed_all, d_ab)
    got, d_out, d_w_ab, output = lax.optimization_barrier((got, d_out, d_w_ab, output))
    d_normed = sum_parts(own, got)
    value_norm, pull_norm = jax.vjp(rms_scale, tokens_f, attn_f)
    d_tokens_norm, d_attn_gain = pull_norm(d_normed)
    d_tokens = (d_resid + d_tokens_norm).astype(bf16)


    def to_blocks(array):
        return array.reshape(devices, -1)

    blocks = (
        to_blocks(d_attn_gain),
        to_blocks(d_ffn_gain),
        to_blocks(d_o_gain),
        to_blocks(d_w_ab),
        at.split_conv(d_conv_w),
        jnp.broadcast_to(d_heads, (devices, 2 * heads)),
    )
    sizes = [array.shape[1] for array in blocks]
    filled = sum(sizes)
    rows_small = -(-filled // 1024) * 8
    packed = jnp.concatenate(
        blocks + (jnp.zeros((devices, rows_small * 128 - filled), f32),), axis=1
    )
    summed = small_sum(packed.reshape(devices, rows_small, 128), at.seq, at.cores, at.group)

    grad_w_gu = join_columns(at.gather_parts(gu_shard), ((piece, 2 * devices),))
    grad_w_down = at.by_owner(at.far_turn(down_turns)).reshape(device_rows, width).astype(f32)
    in_runs = tuple((piece_width, heads) for _, piece_width in QKV + GATE)
    in_shard, d_out, summed, grad_w_gu, d_tokens, output = lax.optimization_barrier(
        (in_shard, d_out, summed, grad_w_gu, d_tokens, output)
    )
    out_shard = at.scatter(d_out)
    returned = at.undeal(jnp.concatenate([output, d_tokens], axis=1))
    in_parts = plane_gather(in_shard) if at.group == 4 else at.gather_parts(in_shard)
    in_parts, out_shard, returned = lax.optimization_barrier((in_parts, out_shard, returned))
    returned = dot_t(sorting, returned).astype(bf16)
    grad_w_in = join_columns(in_parts, in_runs)
    grad_w_out = at.out_rows_join(out_shard)

    summed = summed.reshape(at.group, -1)
    parts, begin = [], 0
    for size in sizes:
        parts.append(summed[:, begin : begin + size])
        begin += size
    grad_w_ab = parts[3].reshape(at.group, width // devices, 2, heads).transpose(1, 2, 3, 0)
    grad_heads = parts[5].reshape(at.group, 2, heads).transpose(1, 2, 0).reshape(2, H)
    return (
        returned[:, :width],
        returned[:, width:],
        jnp.sum(parts[0], axis=0),
        grad_w_in,
        grad_w_ab.reshape(width // devices, 2 * H),
        at.join_own_conv(parts[4]),
        grad_heads[0],
        grad_heads[1],
        jnp.sum(parts[2], axis=0),
        grad_w_out,
        jnp.sum(parts[1], axis=0),
        grad_w_gu,
        grad_w_down,
    )


def solution(mesh):
    placed = (
        P(("group", "seq", "wshard"), None),
        P(("group", "seq", "wshard"), None),
        P(("group", "seq", "wshard")),
        P("group", "wshard", None),
        P(("seq", "wshard")),
        P(("seq", "wshard"), None),
        P(("seq", "wshard"), None),
        P(None, ("seq", "wshard")),
        P(),
        P(),
        P(("seq", "wshard")),
        P(("seq", "wshard"), None),
        P(("seq", "wshard")),
        P(("seq", "wshard"), None),
        P(("seq", "wshard"), None),
    )
    return jax.shard_map(
        shards,
        mesh=mesh,
        in_specs=placed,
        out_specs=(
            P(("group", "seq", "wshard"), None),
            P(("group", "seq", "wshard"), None),
            P(("seq", "wshard")),
            P(("seq", "wshard"), None),
            P(("seq", "wshard"), None),
            P(None, ("seq", "wshard")),
            P(),
            P(),
            P(("seq", "wshard")),
            P(("seq", "wshard"), None),
            P(("seq", "wshard")),
            P(("seq", "wshard"), None),
            P(("seq", "wshard"), None),
        ),
        check_vma=False,
    )
```

```python
import functools

import jax
import jax.numpy as jnp
from jax import lax
from jax.experimental import pallas as pl
from jax.experimental.pallas import tpu as pltpu
from jax.sharding import PartitionSpec as P

H = 16
DK = 128
DV = 256
FF = 5632
CONV = 4
SPAN = 64
HK = 2048
HV = 4096
SIDE = 16
EDGE = 32

bf16 = jnp.bfloat16
f32 = jnp.float32
eps_norm = 1e-06


def mm(left, right, over=((1,), (0,))):
    return lax.dot_general(left, right, (over, ((), ())), preferred_element_type=f32)


def halves(value):
    high = value.astype(bf16)
    return high, (value - high.astype(f32)).astype(bf16)


def mm_fine(left, right, over=((1,), (0,))):
    left_high, left_low = halves(left)
    right_high, right_low = halves(right)
    return (
        mm(left_high, right_high, over)
        + mm(left_low, right_high, over)
        + mm(left_high, right_low, over)
    )


def mm_both(left, right, over=((1,), (0,))):
    return mm(left.astype(bf16), right.astype(bf16), over)


def mm_right(left, right, over=((1,), (0,))):
    high, low = halves(right)
    return mm(left, high, over) + mm(left, low, over)


ROWS = ((1,), (1,))
COLS = ((0,), (0,))


def unit_lower_inverses(stricts):
    groups = EDGE // 8
    count = SPAN // EDGE
    places = lax.broadcasted_iota(jnp.int32, (8, EDGE), 0)
    columns = lax.broadcasted_iota(jnp.int32, (8, EDGE), 1)
    blocks = {}
    for at, strict in enumerate(stricts):
        for block in range(count):
            begin = block * EDGE
            blocks[at, block] = (
                strict[begin : begin + EDGE, begin : begin + EDGE],
                [(places + 8 * part == columns).astype(f32) for part in range(groups)],
            )
    for row in range(EDGE - 1):
        first = row // 8
        for own, done in blocks.values():
            line = done[first][row - 8 * first : row - 8 * first + 1, :]
            for part in range(first, groups):
                column = own[8 * part : 8 * part + 8, row : row + 1]
                done[part] = done[part] - column * line
    inverses = []
    for at, strict in enumerate(stricts):
        parts = [jnp.concatenate(blocks[at, block][1], axis=0) for block in range(count)]
        size = EDGE
        while size < SPAN:
            joined = []
            for pair in range(0, len(parts), 2):
                begin = pair * size
                below = strict[begin + size : begin + 2 * size, begin : begin + size]
                upper, lower = parts[pair], parts[pair + 1]
                corner = mm_fine(mm_fine(lower, below), upper)
                joined.append(
                    jnp.concatenate(
                        [
                            jnp.concatenate([upper, jnp.zeros((size, size), f32)], axis=1),
                            jnp.concatenate([-corner, lower], axis=1),
                        ],
                        axis=0,
                    )
                )
            parts = joined
            size *= 2
        inverses.append(parts[0])
    return inverses


def in_turns(workers):
    workers = list(workers)
    while workers:
        for worker in list(workers):
            if next(worker, workers) is workers:
                workers.remove(worker)


def silu_parts(value):
    rate = 1.0 / (1.0 + jnp.exp(-value))
    return value * rate, rate


def gate_terms(heads, gates, decay_log, dt_bias):
    shifted = gates[:, :heads] + dt_bias
    beta = 1.0 / (1.0 + jnp.exp(-gates[:, heads:]))
    soft = jnp.maximum(shifted, 0.0) + jnp.log1p(jnp.exp(-jnp.abs(shifted)))
    return shifted, beta, -jnp.exp(decay_log) * soft


def ones_left(ones, value):
    high, rest = halves(value)
    high_f = high.astype(f32)
    rest, low = halves(value - high_f)
    return mm(ones, high) + mm(ones, rest) + mm(ones, low)


def triangle(upper):
    at_i = lax.broadcasted_iota(jnp.int32, (SPAN, SPAN), 0)
    at_j = lax.broadcasted_iota(jnp.int32, (SPAN, SPAN), 1)
    return jnp.where(at_i <= at_j if upper else at_i >= at_j, 1.0, 0.0).astype(bf16)


def side_columns(heads, gates, side, decay_log, dt_bias):
    shifted, beta, decay = gate_terms(heads, gates, decay_log, dt_bias)
    running = ones_left(triangle(False), decay)
    cols = jnp.concatenate(
        [running, beta, side[:, :CONV], jnp.zeros((SPAN, 128 - 2 * heads - CONV), f32)], axis=1
    )
    return cols, cols.T, shifted, beta, decay


EDGE_ROWS = 16


def shifted_rows(current, before, side):
    at_i = lax.broadcasted_iota(jnp.int32, (SPAN, SPAN + EDGE_ROWS), 0)
    at_j = lax.broadcasted_iota(jnp.int32, (SPAN, SPAN + EDGE_ROWS), 1)
    moves = [
        jnp.where(at_j == at_i + (EDGE_ROWS - back), side[:, back : back + 1], 0.0).astype(bf16)
        for back in range(1, CONV)
    ]
    moved = mm(jnp.concatenate(moves, axis=0), jnp.concatenate([before, current], axis=0))
    return [moved[(back - 1) * SPAN : back * SPAN, :] for back in range(1, CONV)]


def shifted_back(d_conv, later, same_rows, later_rows):
    at_i = lax.broadcasted_iota(jnp.int32, (SPAN, SPAN + EDGE_ROWS), 0)
    at_j = lax.broadcasted_iota(jnp.int32, (SPAN, SPAN + EDGE_ROWS), 1)
    moves = []
    for back in range(1, CONV):
        same = jnp.concatenate(
            [same_rows[back : back + 1, :], later_rows[back : back + 1, :EDGE_ROWS]], axis=1
        )
        moves.append(jnp.where(at_j == at_i + back, same, 0.0).astype(bf16))
    moved = mm(jnp.concatenate(moves, axis=0), jnp.concatenate([d_conv, later], axis=0))
    return [moved[(back - 1) * SPAN : back * SPAN, :] for back in range(1, CONV)]


def conv_forward(current, moved, taps):
    total = taps[0:1, :] * current
    for back in range(1, CONV):
        total = total + taps[back : back + 1, :] * moved[back - 1]
    return total


def block_terms(head, heads, cols, rows):
    cum_c = cols[:, head : head + 1]
    beta_c = cols[:, heads + head : heads + head + 1]
    count_c = cols[:, 2 * heads : 2 * heads + 1]
    cum_r = rows[head : head + 1, :]
    count_r = rows[2 * heads : 2 * heads + 1, :]
    at_i = lax.broadcasted_iota(jnp.int32, (SPAN, SPAN), 0)
    at_j = lax.broadcasted_iota(jnp.int32, (SPAN, SPAN), 1)
    same = count_c == count_r
    lower_eq = same & (at_i >= at_j)
    lower_st = same & (at_i > at_j)
    fall = jnp.where(lower_eq, jnp.exp(jnp.where(lower_eq, cum_c - cum_r, 0.0)), 0.0)
    growth = jnp.where(count_c == 0.0, jnp.exp(cum_c), 0.0)
    last = SPAN - 1
    tail = jnp.where(
        count_c == count_c[last : last + 1, :], jnp.exp(cum_c[last : last + 1, :] - cum_c), 0.0
    )
    return beta_c, lower_st, fall, growth, tail, growth[last : last + 1, :]


def mixer_forward_kernel(
    heads,
    conv_ref,
    gate_ref,
    gates_ref,
    side_ref,
    taps_ref,
    gain_ref,
    log_ref,
    bias_ref,
    gated_ref,
    mixed_ref,
    qkv_ref,
    state_ref,
    inv_ref,
    solved_ref,
    carried,
    before,
):
    @pl.when(pl.program_id(0) == 0)
    def _():
        carried[...] = jnp.zeros_like(carried)
        before[...] = jnp.zeros_like(before)

    side = side_ref[...]
    current = conv_ref[...].astype(bf16)
    moved = shifted_rows(current, before[...], side)
    act, _ = silu_parts(conv_forward(current.astype(f32), moved, taps_ref[...]))
    before[...] = current[SPAN - EDGE_ROWS :, :]
    cols, rows, _, _, _ = side_columns(heads, gates_ref[...], side, log_ref[...], bias_ref[...])
    valid = side[:, CONV : CONV + 1]
    gain = gain_ref[...]
    scale = DK ** (-0.5)
    terms, units, stricts = [], [], []
    for head in range(heads):
        terms.append(block_terms(head, heads, cols, rows))
        beta_c, lower_st, fall = terms[-1][:3]
        unit = []
        for begin in (head * DK, (heads + head) * DK):
            row = act[:, begin : begin + DK]
            row = row * lax.rsqrt(jnp.sum(row * row, axis=1, keepdims=True) + eps_norm)
            row = row.astype(bf16)
            qkv_ref[:, begin : begin + DK] = row
            unit.append(row)
        units.append(unit)
        stricts.append(jnp.where(lower_st, beta_c * mm(unit[1], unit[1], ROWS) * fall, 0.0))
    inverses = unit_lower_inverses(stricts)

    def one_head(head):
        beta_c, lower_st, fall, growth, tail, kept = terms[head]
        queries, keys = units[head]
        inverse = inverses[head]
        inv_ref[0, head] = inverse
        begin = 2 * heads * DK + head * DV
        values = act[:, begin : begin + DV].astype(bf16)
        qkv_ref[:, begin : begin + DV] = values
        state = carried[head]
        state_ref[0, head] = state
        query_prod = mm(queries, keys, ROWS)
        key_state = mm_right(keys, state)
        query_state = mm_right(queries, state)
        yield
        right_side = beta_c * (values.astype(f32) - growth * key_state)
        yield
        solved = mm_fine(inverse, right_side)
        yield
        part = slice(head * DV, (head + 1) * DV)
        solved_ref[:, part] = solved
        inner = mm_fine(query_prod * fall, solved)
        yield
        carried[head] = kept * state + mm_fine(tail * keys.astype(f32), solved, COLS)
        yield
        mixed = scale * (growth * query_state + inner) * valid
        mixed_ref[:, part] = mixed
        shrink = lax.rsqrt(jnp.mean(mixed * mixed, axis=1, keepdims=True) + eps_norm)
        open_gate, _ = silu_parts(gate_ref[:, part])
        gated_ref[:, part] = (mixed * shrink * gain * open_gate).astype(bf16)
        yield

    in_turns([one_head(head) for head in range(heads)])


def mixer_backward_kernel(
    heads,
    conv_ref,
    ahead_ref,
    gate_ref,
    gates_ref,
    side_ref,
    taps_ref,
    gain_ref,
    log_ref,
    bias_ref,
    mixed_ref,
    qkv_ref,
    state_ref,
    inv_ref,
    solved_ref,
    cot_ref,
    dproj_ref,
    dgates_ref,
    dtaps_ref,
    dgain_ref,
    dheads_ref,
    carried,
    after,
    after_side,
):
    @pl.when(pl.program_id(0) == 0)
    def _():
        carried[...] = jnp.zeros_like(carried)
        after[...] = jnp.zeros_like(after)
        after_side[...] = jnp.zeros_like(after_side)
        dtaps_ref[...] = jnp.zeros_like(dtaps_ref)
        dgain_ref[...] = jnp.zeros_like(dgain_ref)
        dheads_ref[...] = jnp.zeros_like(dheads_ref)

    side = side_ref[...]
    taps = taps_ref[...]
    gain = gain_ref[...]
    valid = side[:, CONV : CONV + 1]
    current = conv_ref[...].astype(bf16)
    moved = shifted_rows(current, ahead_ref[...].astype(bf16), side)
    current = current.astype(f32)
    conv_out = conv_forward(current, moved, taps)
    act, rate = silu_parts(conv_out)
    slope = rate * (1.0 + conv_out * (1.0 - rate))
    cols, rows, shifted, beta_all, decay_all = side_columns(
        heads, gates_ref[...], side, log_ref[...], bias_ref[...]
    )
    scale = DK ** (-0.5)
    at_last = lax.broadcasted_iota(jnp.int32, (SPAN, 1), 0) == SPAN - 1
    d_betas, d_cums, d_gains = [None] * heads, [None] * heads, [None] * heads
    d_queries, d_keys, d_values = [None] * heads, [None] * heads, [None] * heads

    def one_head(head):
        beta_c, lower_st, fall, growth, tail, kept = block_terms(head, heads, cols, rows)
        part = slice(head * DV, (head + 1) * DV)
        mixed = mixed_ref[:, part]
        gate = gate_ref[:, part]
        d_gated = cot_ref[:, part]
        shrink = lax.rsqrt(jnp.mean(mixed * mixed, axis=1, keepdims=True) + eps_norm)
        normal = mixed * shrink
        open_gate, gate_rate = silu_parts(gate)
        with_normal = d_gated * normal
        d_gains[head] = jnp.sum(with_normal * open_gate, axis=0, keepdims=True)
        begin = 2 * heads * DK + (heads + head) * DV
        dproj_ref[:, begin : begin + DV] = (
            with_normal * gain * (gate_rate * (1.0 + gate * (1.0 - gate_rate)))
        ).astype(bf16)
        d_normal = d_gated * gain * open_gate
        d_mixed = shrink * (d_normal - normal * jnp.mean(d_normal * normal, axis=1, keepdims=True))
        d_mixed = (scale * valid) * d_mixed
        yield
        queries = qkv_ref[:, head * DK : (head + 1) * DK]
        keys = qkv_ref[:, (heads + head) * DK : (heads + head + 1) * DK]
        begin = 2 * heads * DK + head * DV
        values = qkv_ref[:, begin : begin + DV]
        keys_f = keys.astype(f32)
        queries_f = queries.astype(f32)
        state = state_ref[0, head]
        inverse = inv_ref[0, head]
        solved = solved_ref[:, part]
        d_state = carried[head]
        key_prod = mm(keys, keys, ROWS)
        query_prod = mm(queries, keys, ROWS)
        strict = jnp.where(lower_st, beta_c * key_prod * fall, 0.0)
        mixing = query_prod * fall
        key_state = mm_right(keys, state)
        query_state = mm_right(queries, state)
        yield
        d_solved = mm_fine(mixing, d_mixed, COLS) + mm_fine(tail * keys_f, d_state)
        d_mixing = mm_both(d_mixed, solved, ROWS)
        yield
        d_right = mm_fine(inverse, d_solved, COLS)
        yield
        d_query_prod = d_mixing * fall
        d_strict = jnp.where(lower_st, -mm_both(d_right, solved, ROWS), 0.0)
        d_key_prod = d_strict * beta_c * fall
        d_key_state = -(beta_c * growth) * d_right
        yield
        carried[head] = (
            kept * d_state
            + mm_fine(growth * queries_f, d_mixed, COLS)
            + mm_right(keys, d_key_state, COLS)
        )
        yield
        d_query = mm_both(growth * d_mixed, state, ROWS) + mm_both(d_query_prod, keys_f)
        yield
        both = d_key_prod + d_key_prod.T
        from_tail = mm_both(solved, d_state, ROWS)
        d_key = (
            mm_both(d_key_state, state, ROWS)
            + mm_both(both, keys_f)
            + mm_both(d_query_prod, queries_f, COLS)
            + tail * from_tail
        )
        yield
        residual = values.astype(f32) - growth * key_state
        d_betas[head] = jnp.sum(d_right * residual, axis=1, keepdims=True) + jnp.sum(
            d_strict * key_prod * fall, axis=1, keepdims=True
        )
        spread = d_strict * strict + d_mixing * mixing
        from_last = tail * jnp.sum(keys_f * from_tail, axis=1, keepdims=True)
        d_growth = jnp.sum(d_mixed * query_state, axis=1, keepdims=True) - beta_c * jnp.sum(
            d_right * key_state, axis=1, keepdims=True
        )
        at_end = jnp.sum(from_last, axis=0, keepdims=True) + kept * jnp.sum(
            jnp.sum(d_state * state, axis=1, keepdims=True), axis=0, keepdims=True
        )
        yield
        d_cums[head] = (
            jnp.sum(spread, axis=1, keepdims=True)
            - jnp.sum(spread.T, axis=1, keepdims=True)
            + growth * d_growth
            - from_last
            + jnp.where(at_last, at_end, 0.0)
        )
        yield
        for grads, grad, start in ((d_queries, d_query, head * DK), (d_keys, d_key, (heads + head) * DK)):
            row = act[:, start : start + DK]
            small = lax.rsqrt(jnp.sum(row * row, axis=1, keepdims=True) + eps_norm)
            along = jnp.sum(row * grad, axis=1, keepdims=True) * small * small
            grads[head] = small * (grad - row * along)
        d_values[head] = beta_c * d_right
        yield

    in_turns([one_head(head) for head in range(heads)])
    dgain_ref[...] += sum(d_gains)
    d_conv = jnp.concatenate(d_queries + d_keys + d_values, axis=1) * slope
    d_low = d_conv.astype(bf16)
    same_rows = rows[2 * heads : 2 * heads + CONV, :]
    back_rows = shifted_back(d_low, after[...], same_rows, after_side[...])
    d_in = taps[0:1, :] * d_conv
    d_taps = [jnp.sum(d_conv * current, axis=0, keepdims=True)]
    for back in range(1, CONV):
        d_taps.append(jnp.sum(d_conv * moved[back - 1], axis=0, keepdims=True))
        d_in = d_in + taps[back : back + 1, :] * back_rows[back - 1]
    dtaps_ref[...] += jnp.concatenate(d_taps, axis=0)
    dproj_ref[:, : heads * (2 * DK + DV)] = d_in.astype(bf16)
    after[...] = d_low[:EDGE_ROWS, :]
    after_side[...] = same_rows
    d_decay = ones_left(triangle(True), jnp.concatenate(d_cums, axis=1))
    d_beta = jnp.concatenate(d_betas, axis=1)
    d_shifted = -d_decay * jnp.exp(log_ref[...]) / (1.0 + jnp.exp(-shifted))
    dgates_ref[...] = jnp.concatenate([d_shifted, d_beta * beta_all * (1.0 - beta_all)], axis=1)
    dheads_ref[...] += jnp.concatenate(
        [
            jnp.sum(d_decay * decay_all, axis=0, keepdims=True),
            jnp.sum(d_shifted, axis=0, keepdims=True),
        ],
        axis=1,
    )


BESIDE = pl.CostEstimate(flops=1, bytes_accessed=1, transcendentals=0)


def whole_block(shape):
    return pl.BlockSpec(shape, lambda i: (0,) * len(shape))


MIXER_PARAMS = pltpu.CompilerParams(vmem_limit_bytes=48 * 1024 * 1024)


def mixer_forward(proj, gates, side, taps, gain, decay_log, dt_bias):
    length = proj.shape[0]
    width = taps.shape[1]
    heads = decay_log.shape[1]
    gate_at = width // (heads * DV)
    blocks = length // SPAN
    return pl.pallas_call(
        functools.partial(mixer_forward_kernel, heads),
        grid=(blocks,),
        in_specs=[
            pl.BlockSpec((SPAN, width), lambda i: (i, 0)),
            pl.BlockSpec((SPAN, heads * DV), lambda i: (i, gate_at)),
            pl.BlockSpec((SPAN, 2 * heads), lambda i: (i, 0)),
            pl.BlockSpec((SPAN, SIDE), lambda i: (i, 0)),
            whole_block((CONV, width)),
            whole_block((1, DV)),
            whole_block((1, heads)),
            whole_block((1, heads)),
        ],
        out_specs=[
            pl.BlockSpec((SPAN, heads * DV), lambda i: (i, 0)),
            pl.BlockSpec((SPAN, heads * DV), lambda i: (i, 0)),
            pl.BlockSpec((SPAN, width), lambda i: (i, 0)),
            pl.BlockSpec((1, heads, DK, DV), lambda i: (i, 0, 0, 0)),
            pl.BlockSpec((1, heads, SPAN, SPAN), lambda i: (i, 0, 0, 0)),
            pl.BlockSpec((SPAN, heads * DV), lambda i: (i, 0)),
        ],
        out_shape=[
            jax.ShapeDtypeStruct((length, heads * DV), bf16),
            jax.ShapeDtypeStruct((length, heads * DV), f32),
            jax.ShapeDtypeStruct((length, width), bf16),
            jax.ShapeDtypeStruct((blocks, heads, DK, DV), f32),
            jax.ShapeDtypeStruct((blocks, heads, SPAN, SPAN), f32),
            jax.ShapeDtypeStruct((length, heads * DV), f32),
        ],
        scratch_shapes=[pltpu.VMEM((heads, DK, DV), f32), pltpu.VMEM((EDGE_ROWS, width), bf16)],
        compiler_params=MIXER_PARAMS,
        cost_estimate=BESIDE,
        name="mixer_forward",
    )(proj, proj, gates, side, taps, gain, decay_log, dt_bias)


def mixer_backward(proj, gates, side, taps, gain, decay_log, dt_bias, kept, d_gated):
    length = proj.shape[0]
    width = taps.shape[1]
    heads = decay_log.shape[1]
    gate_at = width // (heads * DV)
    blocks = length // SPAN
    end = blocks - 1
    ahead_rows = EDGE_ROWS
    per = SPAN // ahead_rows
    return pl.pallas_call(
        functools.partial(mixer_backward_kernel, heads),
        grid=(blocks,),
        in_specs=[
            pl.BlockSpec((SPAN, width), lambda i: (end - i, 0)),
            pl.BlockSpec((ahead_rows, width), lambda i: (jnp.maximum((end - i) * per - 1, 0), 0)),
            pl.BlockSpec((SPAN, heads * DV), lambda i: (end - i, gate_at)),
            pl.BlockSpec((SPAN, 2 * heads), lambda i: (end - i, 0)),
            pl.BlockSpec((SPAN, SIDE), lambda i: (end - i, 0)),
            whole_block((CONV, width)),
            whole_block((1, DV)),
            whole_block((1, heads)),
            whole_block((1, heads)),
            pl.BlockSpec((SPAN, heads * DV), lambda i: (end - i, 0)),
            pl.BlockSpec((SPAN, width), lambda i: (end - i, 0)),
            pl.BlockSpec((1, heads, DK, DV), lambda i: (end - i, 0, 0, 0)),
            pl.BlockSpec((1, heads, SPAN, SPAN), lambda i: (end - i, 0, 0, 0)),
            pl.BlockSpec((SPAN, heads * DV), lambda i: (end - i, 0)),
            pl.BlockSpec((SPAN, heads * DV), lambda i: (end - i, 0)),
        ],
        out_specs=[
            pl.BlockSpec((SPAN, width + heads * DV), lambda i: (end - i, 0)),
            pl.BlockSpec((SPAN, 2 * heads), lambda i: (end - i, 0)),
            whole_block((CONV, width)),
            whole_block((1, DV)),
            whole_block((1, 2 * heads)),
        ],
        out_shape=[
            jax.ShapeDtypeStruct((length, width + heads * DV), bf16),
            jax.ShapeDtypeStruct((length, 2 * heads), f32),
            jax.ShapeDtypeStruct((CONV, width), f32),
            jax.ShapeDtypeStruct((1, DV), f32),
            jax.ShapeDtypeStruct((1, 2 * heads), f32),
        ],
        scratch_shapes=[
            pltpu.VMEM((heads, DK, DV), f32),
            pltpu.VMEM((EDGE_ROWS, width), bf16),
            pltpu.VMEM((CONV, SPAN), f32),
        ],
        compiler_params=MIXER_PARAMS,
        cost_estimate=BESIDE,
        name="mixer_backward",
    )(proj, proj, proj, gates, side, taps, gain, decay_log, dt_bias, *kept, d_gated)


MESH = pl.DeviceIdType.MESH


def column_peers(seq, cores):
    count = seq * cores
    me = lax.axis_index("seq") * cores + lax.axis_index("wshard")
    peers = []
    for step in range(1, count):
        place = lax.rem(me + step, count)
        peers.append((place, {"seq": place // cores, "wshard": lax.rem(place, cores)}))
    return me, peers


def greet(ids):
    barrier = pltpu.get_barrier_semaphore()
    for device in ids:
        pl.semaphore_signal(barrier, inc=1, device_id=device, device_id_type=MESH)
    pl.semaphore_wait(barrier, len(ids))


def small_gather_kernel(seq, cores, in_ref, out_ref, send_sem, recv_sem):
    me, peers = column_peers(seq, cores)
    greet([device for _, device in peers])
    copies = []
    for at, (_, device) in enumerate(peers):
        copies.append(
            pltpu.make_async_remote_copy(
                src_ref=in_ref,
                dst_ref=out_ref.at[me],
                send_sem=send_sem.at[at],
                recv_sem=recv_sem.at[at],
                device_id=device,
                device_id_type=MESH,
            )
        )
        copies[-1].start()
    out_ref[me] = in_ref[...]
    for copy in copies:
        copy.wait()


def small_gather(values, seq, cores):
    count = seq * cores
    return pl.pallas_call(
        functools.partial(small_gather_kernel, seq, cores),
        out_shape=jax.ShapeDtypeStruct((count,) + values.shape, values.dtype),
        in_specs=[pl.BlockSpec(memory_space=pltpu.VMEM)],
        out_specs=pl.BlockSpec(memory_space=pltpu.VMEM),
        scratch_shapes=[pltpu.SemaphoreType.DMA((count - 1,)), pltpu.SemaphoreType.DMA((count - 1,))],
        compiler_params=pltpu.CompilerParams(collective_id=0, has_side_effects=True),
        cost_estimate=BESIDE,
        name="small_gather",
    )(values)


def small_sum_kernel(seq, cores, group, in_ref, out_ref, landed, send_sem, recv_sem, plane_send, plane_recv):
    me, peers = column_peers(seq, cores)
    part = lax.axis_index("group")
    plane = [{"group": lax.rem(part + step, group)} for step in range(1, group)]
    greet([device for _, device in peers] + plane)
    copies = []
    for at, (place, device) in enumerate(peers):
        copies.append(
            pltpu.make_async_remote_copy(
                src_ref=in_ref.at[place],
                dst_ref=landed.at[at],
                send_sem=send_sem.at[at],
                recv_sem=recv_sem.at[at],
                device_id=device,
                device_id_type=MESH,
            )
        )
        copies[-1].start()
    total = in_ref[me]
    for at, copy in enumerate(copies):
        copy.wait()
        total = total + landed[at]
    out_ref[part] = total
    copies = []
    for at, device in enumerate(plane):
        copies.append(
            pltpu.make_async_remote_copy(
                src_ref=out_ref.at[part],
                dst_ref=out_ref.at[part],
                send_sem=plane_send.at[at],
                recv_sem=plane_recv.at[at],
                device_id=device,
                device_id_type=MESH,
            )
        )
        copies[-1].start()
    for copy in copies:
        copy.wait()


def small_sum(values, seq, cores, group):
    count = seq * cores
    shape = values.shape[1:]
    return pl.pallas_call(
        functools.partial(small_sum_kernel, seq, cores, group),
        out_shape=jax.ShapeDtypeStruct((group,) + shape, values.dtype),
        in_specs=[pl.BlockSpec(memory_space=pltpu.VMEM)],
        out_specs=pl.BlockSpec(memory_space=pltpu.VMEM),
        scratch_shapes=[
            pltpu.VMEM((count - 1,) + shape, values.dtype),
            pltpu.SemaphoreType.DMA((count - 1,)),
            pltpu.SemaphoreType.DMA((count - 1,)),
            pltpu.SemaphoreType.DMA((group - 1,)),
            pltpu.SemaphoreType.DMA((group - 1,)),
        ],
        compiler_params=pltpu.CompilerParams(collective_id=1, has_side_effects=True),
        cost_estimate=BESIDE,
        name="small_sum",
    )(values)


def plane_gather_kernel(in_ref, out_ref, done, send_sem, recv_sem):
    part = lax.axis_index("group")
    near = part + 1 - 2 * lax.rem(part, 2)
    far = lax.rem(part + 2, 4)
    half = in_ref.shape[0] // 2
    first, second = pl.ds(0, half), pl.ds(half, half)
    greet([{"group": near}, {"group": far}])

    def send(source, block, rows, target, at):
        copy = pltpu.make_async_remote_copy(
            src_ref=source,
            dst_ref=out_ref.at[block, rows],
            send_sem=send_sem.at[at],
            recv_sem=recv_sem.at[at],
            device_id={"group": target},
            device_id_type=MESH,
        )
        copy.start()
        return copy

    copies = [
        send(in_ref.at[second], part, second, near, 0),
        send(in_ref.at[first], part, first, far, 1),
        send(in_ref.at[first], part, first, near, 2),
        send(in_ref.at[second], part, second, far, 3),
    ]
    own = pltpu.make_async_copy(in_ref, out_ref.at[part], done)
    own.start()
    copies[1].wait_recv()
    copies.append(send(out_ref.at[far, first], far, first, near, 4))
    copies[0].wait_recv()
    copies.append(send(out_ref.at[near, second], near, second, far, 5))
    for at, copy in enumerate(copies):
        copy.wait_send()
        if at >= 2:
            copy.wait_recv()
    own.wait()


def plane_gather(value):
    return pl.pallas_call(
        plane_gather_kernel,
        out_shape=jax.ShapeDtypeStruct((4,) + value.shape, value.dtype),
        in_specs=[pl.BlockSpec(memory_space=pltpu.VMEM)],
        out_specs=pl.BlockSpec(memory_space=pltpu.VMEM),
        scratch_shapes=[
            pltpu.SemaphoreType.DMA,
            pltpu.SemaphoreType.DMA((6,)),
            pltpu.SemaphoreType.DMA((6,)),
        ],
        compiler_params=pltpu.CompilerParams(
            collective_id=2, has_side_effects=True, vmem_limit_bytes=32 * 1024 * 1024
        ),
        cost_estimate=BESIDE,
        name="plane_gather",
    )(value)


def pick_columns_kernel(pieces, group, array_ref, out_ref):
    part = lax.axis_index("group")
    for own in range(group):

        @pl.when(part == own)
        def _():
            out_ref[...] = jnp.concatenate(
                [
                    array_ref[:, first + own * width : first + (own + 1) * width]
                    for first, width in pieces
                ],
                axis=1,
            )


def pick_columns(array, pieces, group):
    rows, columns = array.shape
    step = min(rows, 64)
    picked = sum(width for _, width in pieces)
    return pl.pallas_call(
        functools.partial(pick_columns_kernel, pieces, group),
        grid=(rows // step,),
        in_specs=[pl.BlockSpec((step, columns), lambda i: (i, 0))],
        out_specs=pl.BlockSpec((step, picked), lambda i: (i, 0)),
        out_shape=jax.ShapeDtypeStruct((rows, picked), array.dtype),
        compiler_params=MIXER_PARAMS,
        cost_estimate=BESIDE,
        name="pick_columns",
    )(array)


def join_columns_kernel(group, runs, parts_ref, *refs):
    out_ref = refs[-1]
    source, target = 0, 0
    for width, count in runs:
        pack = 1
        while pack < count and (pack * group * width) % 128:
            pack *= 2
        for first in range(0, count, pack):
            pieces = []
            for run in range(first, first + pack):
                for part in range(group):
                    begin = source + run * width
                    pieces.append(parts_ref[part, :, begin : begin + width].astype(f32))
            size = pack * group * width
            out_ref[:, target : target + size] = jnp.concatenate(pieces, axis=1)
            target += size
        source += count * width


def join_columns(parts, runs, total_rows=None, into=None):
    group, rows, columns = parts.shape
    step = min(rows, 32)
    total_rows = into.shape[0] if into is not None else total_rows or rows
    first = (total_rows - rows) // step if into is not None else 0
    args, specs, aliases = (parts,), [pl.BlockSpec((group, step, columns), lambda i: (0, i, 0))], {}
    if into is not None:
        args, aliases = (parts, into), {1: 0}
        specs.append(pl.BlockSpec(memory_space=pl.ANY))
    return pl.pallas_call(
        functools.partial(join_columns_kernel, group, runs),
        grid=(rows // step,),
        in_specs=specs,
        out_specs=pl.BlockSpec((step, group * columns), lambda i: (first + i, 0)),
        out_shape=jax.ShapeDtypeStruct((total_rows, group * columns), f32),
        input_output_aliases=aliases,
        compiler_params=MIXER_PARAMS,
        cost_estimate=BESIDE,
        name="join_columns",
    )(*args)


def rms_scale(values, gain):
    return values * lax.rsqrt(jnp.mean(values * values, axis=-1, keepdims=True) + eps_norm) * gain


def swiglu(gate_up):
    half = gate_up.shape[1] // 2
    return jax.nn.silu(gate_up[:, :half]) * gate_up[:, half:]


def sum_parts(own, others):
    total = own.astype(f32)
    for part in others:
        total = total + part.astype(f32)
    return total


def dot(left, right):
    return jnp.dot(left, right, preferred_element_type=f32)


def dot_t(left, right):
    return lax.dot_general(left, right, (((0,), (0,)), ((), ())), preferred_element_type=f32)


def dot_back(left, right):
    return lax.dot_general(left, right, (((1,), (1,)), ((), ())), preferred_element_type=f32)


SHARDED = ("seq", "wshard")


class Place:
    def __init__(self, rows):
        self.group = lax.axis_size("group")
        self.seq = lax.axis_size("seq")
        self.cores = lax.axis_size("wshard")
        self.part = lax.axis_index("group")
        self.at_seq = lax.axis_index("seq")
        self.core = lax.axis_index("wshard")
        self.rows = rows
        self.per = rows // self.group
        self.subs = self.seq // self.group
        self.sources = self.seq // self.subs
        self.sub = self.at_seq % self.subs
        self.heads = H // self.group
        self.lane = self.seq * rows

    def deal(self, sorted_rows):
        width = sorted_rows.shape[1]
        if self.subs == 1:
            return lax.all_to_all(sorted_rows, "seq", split_axis=0, concat_axis=0, tiled=True)
        sent = jnp.zeros((self.group, self.subs, self.per, width), sorted_rows.dtype)
        sent = lax.dynamic_update_slice(
            sent,
            sorted_rows.reshape(self.group, 1, self.per, width),
            (0, self.at_seq // self.sources, 0, 0),
        )
        got = lax.all_to_all(
            sent.reshape(-1, width), "seq", split_axis=0, concat_axis=0, tiled=True
        )
        return lax.dynamic_slice(got, (self.sub * self.rows, 0), (self.rows, width))

    def undeal(self, rows):
        width = rows.shape[1]
        if self.subs == 1:
            return lax.all_to_all(rows, "seq", split_axis=0, concat_axis=0, tiled=True)
        sent = jnp.zeros((self.subs * self.rows, width), rows.dtype)
        sent = lax.dynamic_update_slice(sent, rows, (self.sub * self.rows, 0))
        got = lax.all_to_all(sent, "seq", split_axis=0, concat_axis=0, tiled=True)
        got = got.reshape(self.group, self.subs, self.per, width)
        got = lax.dynamic_slice(
            got, (0, self.at_seq // self.sources, 0, 0), (self.group, 1, self.per, width)
        )
        return got.reshape(self.rows, width)

    def swap(self, value, turn):
        if turn == 0:
            return value
        return lax.ppermute(value, "group", [(i, i ^ turn) for i in range(self.group)])

    def gather_any(self, rows):
        return jnp.concatenate([self.swap(rows, turn) for turn in range(self.group)], axis=0)

    def send_any(self, partial):
        own = partial[: self.rows]
        got = [
            self.swap(partial[turn * self.rows : (turn + 1) * self.rows], turn)
            for turn in range(1, self.group)
        ]
        return own, got

    def gather_places(self, rows, beside=()):
        width = rows.shape[1]
        got = [self.swap(rows, turn) for turn in range(1, self.group)]
        got, beside = lax.optimization_barrier((got, beside))
        lane = jnp.zeros((self.sources, self.group, self.per, width), rows.dtype)
        for turn, part in enumerate([rows] + got):
            part = part.reshape(self.sources, 1, self.per, width)
            lane = lax.dynamic_update_slice(lane, part, (0, self.part ^ turn, 0, 0))
        return lane.reshape(-1, width), beside

    def send_places(self, partial):
        width = partial.shape[1]
        lane = partial.reshape(self.sources, self.group, self.per, width)
        parts = [
            lax.dynamic_slice(
                lane, (0, self.part ^ turn, 0, 0), (self.sources, 1, self.per, width)
            ).reshape(self.rows, width)
            for turn in range(self.group)
        ]
        return parts[0], [self.swap(parts[turn], turn) for turn in range(1, self.group)]

    def near_turns(self, value):
        return (value, self.swap(value, 1), self.swap(value, 2))

    def far_turn(self, near):
        rows = near[0].shape[0] // 2
        return near + ((self.swap(near[2][:rows], 1), self.swap(near[1][rows:], 2)),)

    def turns_of(self, value):
        if self.group == 4 and value.ndim == 2 and value.shape[0] % 2 == 0:
            return self.far_turn(self.near_turns(value))
        return tuple(self.swap(value, turn) for turn in range(self.group))

    def by_owner(self, turns):
        value = turns[0]
        parts = jnp.zeros((self.group,) + value.shape, value.dtype)
        for turn, got in enumerate(turns):
            owner, begin = self.part ^ turn, 0
            for piece in got if isinstance(got, tuple) else (got,):
                parts = lax.dynamic_update_slice(
                    parts, piece[None], (owner, begin) + (0,) * (value.ndim - 1)
                )
                begin += piece.shape[0]
        return parts

    def gather_parts(self, value):
        return self.by_owner(self.turns_of(value))

    def to_lane(self, rows):
        if self.subs == 1:
            return rows
        every = lax.all_gather(rows, "seq", axis=0, tiled=True)
        length = rows.shape[0] * self.subs
        return lax.dynamic_slice(
            every, ((self.at_seq // self.subs) * length, 0), (length, rows.shape[1])
        )

    def to_own(self, lane_rows):
        if self.subs == 1:
            return lane_rows
        length = lane_rows.shape[0] // self.subs
        return lax.dynamic_slice(lane_rows, (self.sub * length, 0), (length, lane_rows.shape[1]))

    def head_columns(self, array, sections):
        pieces = []
        for begin, width in sections:
            for turn in range(self.heads):
                pieces.append(
                    lax.dynamic_slice(
                        array,
                        (0, begin + (turn * self.group + self.part) * width),
                        (array.shape[0], width),
                    )
                )
        return jnp.concatenate(pieces, axis=1)

    def core_rows(self, array, core):
        split = array.reshape(self.seq, self.cores, -1, array.shape[1])
        return lax.dynamic_index_in_dim(split, core, 1, keepdims=False).reshape(-1, array.shape[1])

    def core_sum(self, grad):
        if self.cores != 2:
            return grad
        got = lax.ppermute(self.core_rows(grad, 1 - self.core), "wshard", [(0, 1), (1, 0)])
        return (self.core_rows(grad, self.core).astype(f32) + got.astype(f32)).astype(bf16)

    def core_columns(self, array, halves_of=1):
        rows, columns = array.shape
        run = columns // (self.seq * self.cores)
        size = run // halves_of
        out = []
        for half in range(halves_of):
            picked = []
            for core in (1 - self.core, self.core) if self.cores == 2 else range(self.cores):
                picked.append(
                    [
                        lax.dynamic_slice(
                            array,
                            (0, (place * self.cores + core) * run + half * size),
                            (rows, size),
                        )
                        for place in range(self.seq)
                    ]
                )
            if self.cores == 2:
                out.append(tuple(jnp.concatenate(pieces, axis=1) for pieces in picked))
            else:
                every = [pieces[place] for place in range(self.seq) for pieces in picked]
                out.append((jnp.concatenate(every, axis=1),))
        return out

    def other_grad(self, lefts, right):
        if self.cores != 2:
            return None
        return lax.ppermute(dot_t(lefts[0], right).astype(bf16), "wshard", [(0, 1), (1, 0)])

    def own_grad(self, lefts, right, got):
        own = dot_t(lefts[-1], right)
        return (own if got is None else own + got.astype(f32)).astype(bf16)

    def scatter(self, grad):
        axes = "seq" if self.cores == 2 else SHARDED
        return lax.psum_scatter(grad, axes, scatter_dimension=0, tiled=True)

    def out_rows(self, w_out):
        width = w_out.shape[1]
        if self.subs == 1 and self.cores == 2:
            mine = lax.dynamic_slice(w_out, ((self.part % 2) * DV, 0), (DV, width))
            half = DV // 2
            kept = lax.dynamic_slice(mine, (self.core * half, 0), (half, width))
            other = lax.dynamic_slice(mine, ((1 - self.core) * half, 0), (half, width))
            got = lax.ppermute(other, "wshard", [(0, 1), (1, 0)])
            piece = jnp.where(self.core == self.part // 2, kept, got)
            return lax.all_gather(piece, SHARDED, axis=0, tiled=True)
        every = lax.all_gather(w_out, SHARDED, axis=0, tiled=True)
        every = every.reshape(self.heads, self.group, DV, width)
        return lax.dynamic_slice(
            every, (0, self.part, 0, 0), (self.heads, 1, DV, width)
        ).reshape(-1, width)

    def out_grad(self, gated, d_branch):
        if self.subs == 1 and self.cores == 2:
            lefts = self.core_columns(gated)[0]
            return self.own_grad(lefts, d_branch, self.other_grad(lefts, d_branch))
        width = d_branch.shape[1]
        grad = dot_t(gated, d_branch).astype(bf16)
        every = jnp.zeros((self.heads, self.group, DV, width), bf16)
        every = lax.dynamic_update_slice(
            every, grad.reshape(self.heads, 1, DV, width), (0, self.part, 0, 0)
        ).reshape(-1, width)
        return self.core_sum(every)

    def out_rows_join(self, turns):
        shard = turns[0]
        width = shard.shape[1]
        if self.subs == 1 and self.cores == 2:
            halves_all = self.by_owner(turns)
            here = lax.dynamic_slice(halves_all, (2 * self.core, 0, 0), (2, DV // 2, width))
            there = lax.dynamic_slice(halves_all, (2 - 2 * self.core, 0, 0), (2, DV // 2, width))
            got = lax.ppermute(there, "wshard", [(0, 1), (1, 0)])
            first = jnp.where(self.core == 0, here, got)
            second = jnp.where(self.core == 0, got, here)
            return jnp.stack([first, second], axis=1).reshape(2 * DV, width).astype(f32)
        return lax.psum(shard, "group").astype(f32)

    def conv_pieces(self, conv_w):
        if self.subs > 1:
            return conv_w
        columns = conv_w.shape[1]
        wide = lax.dynamic_slice(conv_w, (0, self.part * DV), (CONV, DV))
        narrow = self.head_columns_of(conv_w, DK)
        return jnp.where(self.at_seq * self.cores + self.core >= 2 * HK // columns, wide, narrow)

    def head_columns_of(self, array, head_width):
        count = array.shape[1] // (self.group * head_width)
        return jnp.concatenate(
            [
                lax.dynamic_slice(
                    array,
                    (0, (turn * self.group + self.part) * head_width),
                    (array.shape[0], head_width),
                )
                for turn in range(count)
            ],
            axis=1,
        )

    def join_conv(self, pieces):
        pieces = pieces.reshape(self.seq * self.cores, CONV, -1).transpose(1, 0, 2)
        pieces = pieces.reshape(CONV, -1)
        return self.head_columns(pieces, QKV) if self.subs > 1 else pieces

    def split_conv(self, grad):
        devices = self.seq * self.cores
        if self.subs > 1:
            pieces, begin = [], 0
            mine = (jnp.arange(self.group) == self.part).astype(f32)[:, None]
            for _, head_width in QKV:
                end = begin + self.heads * head_width
                section = grad[:, begin:end].reshape(CONV, self.heads, 1, head_width) * mine
                pieces.append(section.reshape(CONV, -1))
                begin = end
            grad = jnp.concatenate(pieces, axis=1)
        return grad.reshape(CONV, devices, -1).transpose(1, 0, 2).reshape(devices, -1)

    def join_own_conv(self, parts):
        parts = parts.reshape(self.group, CONV, -1)
        if self.subs > 1:
            return jnp.sum(parts, axis=0)
        columns = parts.shape[2] * self.group
        wide = parts.transpose(1, 0, 2).reshape(CONV, columns)
        narrow = parts.reshape(self.group, CONV, -1, DK).transpose(1, 2, 0, 3).reshape(CONV, columns)
        return jnp.where(self.at_seq * self.cores + self.core >= 2 * HK // columns, wide, narrow)


QKV = ((0, DK), (HK, DK), (2 * HK, DV))
GATE = ((2 * HK + HV, DV),)


def side_array(lane_lengths, length):
    ends = jnp.cumsum(lane_lengths)
    bounds = jnp.concatenate([jnp.zeros((1,), jnp.int32), ends])
    places = jnp.arange(length, dtype=jnp.int32)
    crossed = places[:, None] >= bounds[None, :]
    block_begin = (places // SPAN) * SPAN
    counted = jnp.sum((crossed & (bounds[None, :] >= block_begin[:, None])).astype(jnp.int32), axis=1)
    segment = jnp.sum(crossed.astype(jnp.int32), axis=1)
    columns = [counted.astype(f32)]
    for back in range(1, CONV):
        earlier = jnp.sum((places[:, None] - back >= bounds[None, :]).astype(jnp.int32), axis=1)
        columns.append(((earlier == segment) & (places >= back)).astype(f32))
    columns.append((places < ends[-1]).astype(f32))
    columns += [jnp.zeros((length,), f32)] * (SIDE - len(columns))
    return jnp.stack(columns, axis=1)


def shards(
    tokens,
    cotangent,
    dealing,
    lengths,
    attn_gain,
    w_in,
    w_ab,
    conv_w,
    decay_log,
    dt_bias,
    o_gain,
    w_out,
    ffn_gain,
    w_gu,
    w_down,
):
    rows, width = tokens.shape
    at = Place(rows)
    heads = at.heads
    device_rows = w_down.shape[0]
    devices = at.seq * at.cores

    at_device = at.at_seq * at.cores + at.core

    pieces = []
    for begin, piece_width in QKV + GATE:
        pieces += [
            (begin + turn * at.group * piece_width, piece_width) for turn in range(heads)
        ]
    in_piece = pick_columns(w_in, tuple(pieces), at.group)

    ab_shard = at.head_columns(w_ab, ((0, 1), (H, 1)))
    conv_pieces = at.conv_pieces(conv_w)
    small = (attn_gain, ffn_gain, o_gain, ab_shard.reshape(-1), conv_pieces.reshape(-1))
    lengths_small = [array.shape[0] for array in small]
    filled = sum(lengths_small)
    rows_small = -(-filled // (16 * 128)) * 16
    packed = jnp.concatenate(small + (jnp.zeros((rows_small * 128 - filled,), bf16),))
    packed, in_piece = lax.optimization_barrier((packed, in_piece))
    in_mine = lax.all_gather(in_piece, SHARDED, axis=0, tiled=True)
    packed = small_gather(packed.reshape(rows_small, 128), at.seq, at.cores)
    packed, tokens, cotangent = lax.optimization_barrier((packed, tokens, cotangent))
    packed = packed.reshape(devices, -1)
    full, begin = [], 0
    for count in lengths_small:
        full.append(packed[:, begin : begin + count])
        begin += count
    attn_f, ffn_f, o_f = (array.reshape(-1).astype(f32) for array in full[:3])
    ab_mine = full[3].reshape(width, 2 * heads)
    conv_mine = at.join_conv(full[4]).astype(f32)

    def my_heads(values):
        return lax.dynamic_slice(values.reshape(heads, at.group), (0, at.part), (heads, 1)).reshape(1, -1)

    decay_mine, dt_mine = my_heads(decay_log), my_heads(dt_bias)

    member = (dealing[:, None] == jnp.arange(at.group, dtype=jnp.int32)[None, :]).astype(jnp.int32)
    before = dot(jnp.tril(jnp.ones((rows, rows), f32), -1).astype(bf16), member.astype(bf16))
    before = before.astype(jnp.int32)
    target = jnp.sum((before + at.per * jnp.arange(at.group, dtype=jnp.int32)) * member, axis=1)
    sorting = (target[None, :] == jnp.arange(rows, dtype=jnp.int32)[:, None]).astype(bf16)
    tokens_f = at.deal(dot(sorting, tokens).astype(bf16)).astype(f32)
    normed = rms_scale(tokens_f, attn_f).astype(bf16)
    normed, cotangent, w_out, w_gu, w_down = lax.optimization_barrier(
        (normed, cotangent, w_out, w_gu, w_down)
    )
    normed_all, _ = at.gather_places(normed)
    normed_all, normed_cores = lax.optimization_barrier(
        (normed_all, at.core_columns(normed_all, 2))
    )

    out_mine = at.out_rows(w_out)
    piece = device_rows // at.group
    gu_pieces = tuple((block * device_rows, piece) for block in range(2 * devices))
    gu_mine = lax.all_gather(
        pick_columns(w_gu, gu_pieces, at.group), SHARDED, axis=0, tiled=True
    )
    down_mine = lax.all_gather(
        lax.dynamic_slice(w_down, (at.part * piece, 0), (piece, width)), SHARDED, axis=0, tiled=True
    )
    cot_own = at.deal(dot(sorting, cotangent).astype(bf16))
    normed_all, cot_own = lax.optimization_barrier((normed_all, cot_own))

    lane_lengths = lax.dynamic_index_in_dim(
        at.gather_parts(lengths.reshape(-1)), at.at_seq // at.subs, 0, keepdims=False
    )
    side = side_array(lane_lengths, at.lane)
    gates_ab = at.to_lane(dot(normed_all, ab_mine))
    proj, cot_own = lax.optimization_barrier((dot(normed_all, in_mine), cot_own))
    cot_all = at.gather_any(cot_own)
    proj = at.to_lane(proj)
    mixer_args = (proj, gates_ab, side, conv_mine, o_f[None], decay_mine, dt_mine)
    gated_lane, *kept = mixer_forward(*mixer_args)
    gated_lane, cot_all = lax.optimization_barrier((gated_lane, cot_all))
    gated = at.to_own(gated_lane)
    own, got = at.send_places(dot(gated, out_mine).astype(bf16))
    resid = tokens_f + sum_parts(own, got)

    normed2_f, pull_norm2 = jax.vjp(rms_scale, resid, ffn_f)
    normed2_all = at.gather_any(normed2_f.astype(bf16))
    normed2_all, normed2_cores = lax.optimization_barrier(
        (normed2_all, at.core_columns(normed2_all)[0])
    )
    gate_up = dot(normed2_all, gu_mine)
    hidden_f, pull_ffn = jax.vjp(swiglu, gate_up)
    hidden = hidden_f.astype(bf16)

    d_down = at.core_sum(dot_t(hidden, cot_all).astype(bf16))
    d_down, hidden, cot_back = lax.optimization_barrier((d_down, hidden, cot_all))
    down_shard = at.scatter(d_down)
    d_hidden = dot_back(cot_back, down_mine)
    d_gate_up = pull_ffn(d_hidden)[0].astype(bf16)
    d_normed2_parts = dot_back(d_gate_up, gu_mine).astype(bf16)
    d_normed2_parts, d_gate_up = lax.optimization_barrier((d_normed2_parts, d_gate_up))
    own, got = at.send_any(d_normed2_parts)
    gu_got = at.other_grad(normed2_cores, d_gate_up)
    normed2_cores, down_shard = lax.optimization_barrier((normed2_cores, down_shard))
    d_gu = at.own_grad(normed2_cores, d_gate_up, gu_got)
    got, d_gu = lax.optimization_barrier((got, d_gu))
    gu_shard = at.scatter(d_gu)
    d_normed2 = sum_parts(own, got)
    d_resid_norm, d_ffn_gain = pull_norm2(d_normed2)
    d_resid = cot_own.astype(f32) + d_resid_norm

    d_branch_all, output_parts = at.gather_places(
        d_resid.astype(bf16), dot(hidden, down_mine).astype(bf16)
    )
    d_gated = dot_back(d_branch_all, out_mine)
    d_out = at.out_grad(gated, d_branch_all)
    d_gated, output_parts, down_shard, d_out = lax.optimization_barrier(
        (d_gated, output_parts, down_shard, d_out)
    )
    out_shard = at.scatter(d_out)
    output_own, output_got = at.send_any(output_parts)
    down_turns = at.near_turns(down_shard)
    d_proj_lane, d_gates_lane, d_conv_w, d_o_gain, d_heads = mixer_backward(
        *mixer_args, tuple(kept), at.to_lane(d_gated)
    )
    d_proj_lane, output_got, down_turns, gu_shard = lax.optimization_barrier(
        (d_proj_lane, output_got, down_turns, gu_shard)
    )
    gu_turns = at.near_turns(gu_shard)
    once = (at.sub == 0).astype(f32)
    d_conv_w, d_o_gain, d_heads = d_conv_w * once, d_o_gain * once, d_heads * once
    d_proj = at.to_own(d_proj_lane)
    d_ab = at.to_own(d_gates_lane).astype(bf16)
    in_got = [at.other_grad(lefts, d_proj) for lefts in normed_cores]
    first = at.own_grad(normed_cores[0], d_proj, in_got[0])
    first, in_got, d_proj = lax.optimization_barrier((first, in_got[1], d_proj))
    in_shards = [at.scatter(first)]
    second = at.own_grad(normed_cores[1], d_proj, in_got)
    second, d_proj, d_ab, out_shard = lax.optimization_barrier(
        (second, d_proj, d_ab, out_shard)
    )
    in_shards.append(at.scatter(second))
    d_normed_parts = (dot_back(d_proj, in_mine) + dot_back(d_ab, ab_mine)).astype(bf16)
    d_normed_parts, d_ab, gu_turns, output_got = lax.optimization_barrier(
        (d_normed_parts, d_ab, gu_turns, output_got)
    )
    output = (resid + sum_parts(output_own, output_got)).astype(bf16)
    own, got = at.send_places(d_normed_parts)
    d_w_ab = dot_t(normed_all, d_ab)
    got, d_w_ab = lax.optimization_barrier((got, d_w_ab))
    d_normed = sum_parts(own, got)
    value_norm, pull_norm = jax.vjp(rms_scale, tokens_f, attn_f)
    d_tokens_norm, d_attn_gain = pull_norm(d_normed)
    d_tokens = (d_resid + d_tokens_norm).astype(bf16)
    d_tokens, gu_turns, down_turns = lax.optimization_barrier((d_tokens, gu_turns, down_turns))
    gu_turns = at.far_turn(gu_turns)
    down_turns = at.far_turn(down_turns)
    back = jnp.concatenate([output, d_tokens], axis=1)


    def to_blocks(array):
        return array.reshape(devices, -1)

    blocks = (
        to_blocks(d_attn_gain),
        to_blocks(d_ffn_gain),
        to_blocks(d_o_gain),
        to_blocks(d_w_ab),
        at.split_conv(d_conv_w),
        jnp.broadcast_to(d_heads, (devices, 2 * heads)),
    )
    sizes = [array.shape[1] for array in blocks]
    filled = sum(sizes)
    rows_small = -(-filled // 1024) * 8
    packed = jnp.concatenate(
        blocks + (jnp.zeros((devices, rows_small * 128 - filled), f32),), axis=1
    )
    summed = small_sum(packed.reshape(devices, rows_small, 128), at.seq, at.cores, at.group)

    in_runs = tuple((piece_width, heads) for _, piece_width in QKV + GATE)
    gather = plane_gather if at.group == 4 else at.gather_parts
    in_first, in_second = in_shards
    in_first, summed = lax.optimization_barrier((in_first, summed))
    out_turns = at.turns_of(out_shard)
    in_parts, gu_turns, down_turns, out_turns = lax.optimization_barrier(
        (gather(in_first), gu_turns, down_turns, out_turns)
    )
    grad_w_in = join_columns(in_parts, in_runs, total_rows=w_in.shape[0])
    in_second, grad_w_in, gu_turns, down_turns, out_turns, back = lax.optimization_barrier(
        (in_second, grad_w_in, gu_turns, down_turns, out_turns, back)
    )
    returned = at.undeal(back)
    in_turns = at.near_turns(in_second)
    grad_w_gu = join_columns(at.by_owner(gu_turns), ((piece, 2 * devices),))
    in_turns, grad_w_gu = lax.optimization_barrier((in_turns, grad_w_gu))
    in_turns = at.far_turn(in_turns)
    grad_w_down = at.by_owner(down_turns).reshape(device_rows, width).astype(f32)
    grad_w_out = at.out_rows_join(out_turns)
    in_turns, grad_w_down, grad_w_out, returned = lax.optimization_barrier(
        (in_turns, grad_w_down, grad_w_out, returned)
    )
    in_parts = at.by_owner(in_turns)
    grad_w_in = join_columns(in_parts, in_runs, into=grad_w_in)
    returned = dot_t(sorting, returned).astype(bf16)

    summed = summed.reshape(at.group, -1)
    parts, begin = [], 0
    for size in sizes:
        parts.append(summed[:, begin : begin + size])
        begin += size
    grad_w_ab = parts[3].reshape(at.group, width // devices, 2, heads).transpose(1, 2, 3, 0)
    grad_heads = parts[5].reshape(at.group, 2, heads).transpose(1, 2, 0).reshape(2, H)
    return (
        returned[:, :width],
        returned[:, width:],
        jnp.sum(parts[0], axis=0),
        grad_w_in,
        grad_w_ab.reshape(width // devices, 2 * H),
        at.join_own_conv(parts[4]),
        grad_heads[0],
        grad_heads[1],
        jnp.sum(parts[2], axis=0),
        grad_w_out,
        jnp.sum(parts[1], axis=0),
        grad_w_gu,
        grad_w_down,
    )


def solution(mesh):
    placed = (
        P(("group", "seq", "wshard"), None),
        P(("group", "seq", "wshard"), None),
        P(("group", "seq", "wshard")),
        P("group", "wshard", None),
        P(("seq", "wshard")),
        P(("seq", "wshard"), None),
        P(("seq", "wshard"), None),
        P(None, ("seq", "wshard")),
        P(),
        P(),
        P(("seq", "wshard")),
        P(("seq", "wshard"), None),
        P(("seq", "wshard")),
        P(("seq", "wshard"), None),
        P(("seq", "wshard"), None),
    )
    return jax.shard_map(
        shards,
        mesh=mesh,
        in_specs=placed,
        out_specs=(
            P(("group", "seq", "wshard"), None),
            P(("group", "seq", "wshard"), None),
            P(("seq", "wshard")),
            P(("seq", "wshard"), None),
            P(("seq", "wshard"), None),
            P(None, ("seq", "wshard")),
            P(),
            P(),
            P(("seq", "wshard")),
            P(("seq", "wshard"), None),
            P(("seq", "wshard")),
            P(("seq", "wshard"), None),
            P(("seq", "wshard"), None),
        ),
        check_vma=False,
    )
```

```python
import functools

import jax
import jax.numpy as jnp
from jax import lax
from jax.experimental import pallas as pl
from jax.experimental.pallas import tpu as pltpu
from jax.sharding import PartitionSpec as P

H = 16
DK = 128
DV = 256
FF = 5632
CONV = 4
SPAN = 64
HK = 2048
HV = 4096
SIDE = 16
EDGE = 32

bf16 = jnp.bfloat16
f32 = jnp.float32
eps_norm = 1e-06


def mm(left, right, over=((1,), (0,))):
    return lax.dot_general(left, right, (over, ((), ())), preferred_element_type=f32)


def halves(value):
    high = value.astype(bf16)
    return high, (value - high.astype(f32)).astype(bf16)


def mm_fine(left, right, over=((1,), (0,))):
    left_high, left_low = halves(left)
    right_high, right_low = halves(right)
    return (
        mm(left_high, right_high, over)
        + mm(left_low, right_high, over)
        + mm(left_high, right_low, over)
    )


def mm_both(left, right, over=((1,), (0,))):
    return mm(left.astype(bf16), right.astype(bf16), over)


def mm_right(left, right, over=((1,), (0,))):
    high, low = halves(right)
    return mm(left, high, over) + mm(left, low, over)


ROWS = ((1,), (1,))
COLS = ((0,), (0,))


def unit_lower_inverses(stricts):
    groups = EDGE // 8
    count = SPAN // EDGE
    places = lax.broadcasted_iota(jnp.int32, (8, EDGE), 0)
    columns = lax.broadcasted_iota(jnp.int32, (8, EDGE), 1)
    blocks = {}
    for at, strict in enumerate(stricts):
        for block in range(count):
            begin = block * EDGE
            blocks[at, block] = (
                strict[begin : begin + EDGE, begin : begin + EDGE],
                [(places + 8 * part == columns).astype(f32) for part in range(groups)],
            )
    for row in range(EDGE - 1):
        first = row // 8
        for own, done in blocks.values():
            line = done[first][row - 8 * first : row - 8 * first + 1, :]
            for part in range(first, groups):
                column = own[8 * part : 8 * part + 8, row : row + 1]
                done[part] = done[part] - column * line
    inverses = []
    for at, strict in enumerate(stricts):
        parts = [jnp.concatenate(blocks[at, block][1], axis=0) for block in range(count)]
        size = EDGE
        while size < SPAN:
            joined = []
            for pair in range(0, len(parts), 2):
                begin = pair * size
                below = strict[begin + size : begin + 2 * size, begin : begin + size]
                upper, lower = parts[pair], parts[pair + 1]
                corner = mm_fine(mm_fine(lower, below), upper)
                joined.append(
                    jnp.concatenate(
                        [
                            jnp.concatenate([upper, jnp.zeros((size, size), f32)], axis=1),
                            jnp.concatenate([-corner, lower], axis=1),
                        ],
                        axis=0,
                    )
                )
            parts = joined
            size *= 2
        inverses.append(parts[0])
    return inverses


def in_turns(workers):
    workers = list(workers)
    while workers:
        for worker in list(workers):
            if next(worker, workers) is workers:
                workers.remove(worker)


def silu_parts(value):
    rate = 1.0 / (1.0 + jnp.exp(-value))
    return value * rate, rate


def gate_terms(heads, gates, decay_log, dt_bias):
    shifted = gates[:, :heads] + dt_bias
    beta = 1.0 / (1.0 + jnp.exp(-gates[:, heads:]))
    soft = jnp.maximum(shifted, 0.0) + jnp.log1p(jnp.exp(-jnp.abs(shifted)))
    return shifted, beta, -jnp.exp(decay_log) * soft


def ones_left(ones, value):
    high, rest = halves(value)
    high_f = high.astype(f32)
    rest, low = halves(value - high_f)
    return mm(ones, high) + mm(ones, rest) + mm(ones, low)


def triangle(upper):
    at_i = lax.broadcasted_iota(jnp.int32, (SPAN, SPAN), 0)
    at_j = lax.broadcasted_iota(jnp.int32, (SPAN, SPAN), 1)
    return jnp.where(at_i <= at_j if upper else at_i >= at_j, 1.0, 0.0).astype(bf16)


def side_columns(heads, gates, side, decay_log, dt_bias):
    shifted, beta, decay = gate_terms(heads, gates, decay_log, dt_bias)
    running = ones_left(triangle(False), decay)
    cols = jnp.concatenate(
        [running, beta, side[:, :CONV], jnp.zeros((SPAN, 128 - 2 * heads - CONV), f32)], axis=1
    )
    return cols, cols.T, shifted, beta, decay


EDGE_ROWS = 16


def shifted_rows(current, before, side):
    at_i = lax.broadcasted_iota(jnp.int32, (SPAN, SPAN + EDGE_ROWS), 0)
    at_j = lax.broadcasted_iota(jnp.int32, (SPAN, SPAN + EDGE_ROWS), 1)
    moves = [
        jnp.where(at_j == at_i + (EDGE_ROWS - back), side[:, back : back + 1], 0.0).astype(bf16)
        for back in range(1, CONV)
    ]
    moved = mm(jnp.concatenate(moves, axis=0), jnp.concatenate([before, current], axis=0))
    return [moved[(back - 1) * SPAN : back * SPAN, :] for back in range(1, CONV)]


def shifted_back(d_conv, later, same_rows, later_rows):
    at_i = lax.broadcasted_iota(jnp.int32, (SPAN, SPAN + EDGE_ROWS), 0)
    at_j = lax.broadcasted_iota(jnp.int32, (SPAN, SPAN + EDGE_ROWS), 1)
    moves = []
    for back in range(1, CONV):
        same = jnp.concatenate(
            [same_rows[back : back + 1, :], later_rows[back : back + 1, :EDGE_ROWS]], axis=1
        )
        moves.append(jnp.where(at_j == at_i + back, same, 0.0).astype(bf16))
    moved = mm(jnp.concatenate(moves, axis=0), jnp.concatenate([d_conv, later], axis=0))
    return [moved[(back - 1) * SPAN : back * SPAN, :] for back in range(1, CONV)]


def conv_forward(current, moved, taps):
    total = taps[0:1, :] * current
    for back in range(1, CONV):
        total = total + taps[back : back + 1, :] * moved[back - 1]
    return total


def block_terms(head, heads, cols, rows):
    cum_c = cols[:, head : head + 1]
    beta_c = cols[:, heads + head : heads + head + 1]
    count_c = cols[:, 2 * heads : 2 * heads + 1]
    cum_r = rows[head : head + 1, :]
    count_r = rows[2 * heads : 2 * heads + 1, :]
    at_i = lax.broadcasted_iota(jnp.int32, (SPAN, SPAN), 0)
    at_j = lax.broadcasted_iota(jnp.int32, (SPAN, SPAN), 1)
    same = count_c == count_r
    lower_eq = same & (at_i >= at_j)
    lower_st = same & (at_i > at_j)
    fall = jnp.where(lower_eq, jnp.exp(jnp.where(lower_eq, cum_c - cum_r, 0.0)), 0.0)
    growth = jnp.where(count_c == 0.0, jnp.exp(cum_c), 0.0)
    last = SPAN - 1
    tail = jnp.where(
        count_c == count_c[last : last + 1, :], jnp.exp(cum_c[last : last + 1, :] - cum_c), 0.0
    )
    return beta_c, lower_st, fall, growth, tail, growth[last : last + 1, :]


def mixer_forward_kernel(
    heads,
    conv_ref,
    gate_ref,
    gates_ref,
    side_ref,
    taps_ref,
    gain_ref,
    log_ref,
    bias_ref,
    gated_ref,
    mixed_ref,
    qkv_ref,
    state_ref,
    inv_ref,
    solved_ref,
    carried,
    before,
):
    @pl.when(pl.program_id(0) == 0)
    def _():
        carried[...] = jnp.zeros_like(carried)
        before[...] = jnp.zeros_like(before)

    side = side_ref[...]
    current = conv_ref[...].astype(bf16)
    moved = shifted_rows(current, before[...], side)
    act, _ = silu_parts(conv_forward(current.astype(f32), moved, taps_ref[...]))
    before[...] = current[SPAN - EDGE_ROWS :, :]
    cols, rows, _, _, _ = side_columns(heads, gates_ref[...], side, log_ref[...], bias_ref[...])
    valid = side[:, CONV : CONV + 1]
    gain = gain_ref[...]
    scale = DK ** (-0.5)
    terms, units, stricts = [], [], []
    for head in range(heads):
        terms.append(block_terms(head, heads, cols, rows))
        beta_c, lower_st, fall = terms[-1][:3]
        unit = []
        for begin in (head * DK, (heads + head) * DK):
            row = act[:, begin : begin + DK]
            row = row * lax.rsqrt(jnp.sum(row * row, axis=1, keepdims=True) + eps_norm)
            row = row.astype(bf16)
            qkv_ref[:, begin : begin + DK] = row
            unit.append(row)
        units.append(unit)
        stricts.append(jnp.where(lower_st, beta_c * mm(unit[1], unit[1], ROWS) * fall, 0.0))
    inverses = unit_lower_inverses(stricts)

    def one_head(head):
        beta_c, lower_st, fall, growth, tail, kept = terms[head]
        queries, keys = units[head]
        inverse = inverses[head]
        inv_ref[0, head] = inverse
        begin = 2 * heads * DK + head * DV
        values = act[:, begin : begin + DV].astype(bf16)
        qkv_ref[:, begin : begin + DV] = values
        state = carried[head]
        state_ref[0, head] = state
        query_prod = mm(queries, keys, ROWS)
        key_state = mm_right(keys, state)
        query_state = mm_right(queries, state)
        yield
        right_side = beta_c * (values.astype(f32) - growth * key_state)
        yield
        solved = mm_fine(inverse, right_side)
        yield
        part = slice(head * DV, (head + 1) * DV)
        solved_ref[:, part] = solved
        inner = mm_fine(query_prod * fall, solved)
        yield
        carried[head] = kept * state + mm_fine(tail * keys.astype(f32), solved, COLS)
        yield
        mixed = scale * (growth * query_state + inner) * valid
        mixed_ref[:, part] = mixed
        shrink = lax.rsqrt(jnp.mean(mixed * mixed, axis=1, keepdims=True) + eps_norm)
        open_gate, _ = silu_parts(gate_ref[:, part])
        gated_ref[:, part] = (mixed * shrink * gain * open_gate).astype(bf16)
        yield

    in_turns([one_head(head) for head in range(heads)])


def mixer_backward_kernel(
    heads,
    conv_ref,
    ahead_ref,
    gate_ref,
    gates_ref,
    side_ref,
    taps_ref,
    gain_ref,
    log_ref,
    bias_ref,
    mixed_ref,
    qkv_ref,
    state_ref,
    inv_ref,
    solved_ref,
    cot_ref,
    dproj_ref,
    dgates_ref,
    dtaps_ref,
    dgain_ref,
    dheads_ref,
    carried,
    after,
    after_side,
):
    @pl.when(pl.program_id(0) == 0)
    def _():
        carried[...] = jnp.zeros_like(carried)
        after[...] = jnp.zeros_like(after)
        after_side[...] = jnp.zeros_like(after_side)
        dtaps_ref[...] = jnp.zeros_like(dtaps_ref)
        dgain_ref[...] = jnp.zeros_like(dgain_ref)
        dheads_ref[...] = jnp.zeros_like(dheads_ref)

    side = side_ref[...]
    taps = taps_ref[...]
    gain = gain_ref[...]
    valid = side[:, CONV : CONV + 1]
    current = conv_ref[...].astype(bf16)
    moved = shifted_rows(current, ahead_ref[...].astype(bf16), side)
    current = current.astype(f32)
    conv_out = conv_forward(current, moved, taps)
    act, rate = silu_parts(conv_out)
    slope = rate * (1.0 + conv_out * (1.0 - rate))
    cols, rows, shifted, beta_all, decay_all = side_columns(
        heads, gates_ref[...], side, log_ref[...], bias_ref[...]
    )
    scale = DK ** (-0.5)
    at_last = lax.broadcasted_iota(jnp.int32, (SPAN, 1), 0) == SPAN - 1
    d_betas, d_cums, d_gains = [None] * heads, [None] * heads, [None] * heads
    d_queries, d_keys, d_values = [None] * heads, [None] * heads, [None] * heads

    def one_head(head):
        beta_c, lower_st, fall, growth, tail, kept = block_terms(head, heads, cols, rows)
        part = slice(head * DV, (head + 1) * DV)
        mixed = mixed_ref[:, part]
        gate = gate_ref[:, part]
        d_gated = cot_ref[:, part]
        shrink = lax.rsqrt(jnp.mean(mixed * mixed, axis=1, keepdims=True) + eps_norm)
        normal = mixed * shrink
        open_gate, gate_rate = silu_parts(gate)
        with_normal = d_gated * normal
        d_gains[head] = jnp.sum(with_normal * open_gate, axis=0, keepdims=True)
        begin = 2 * heads * DK + (heads + head) * DV
        dproj_ref[:, begin : begin + DV] = (
            with_normal * gain * (gate_rate * (1.0 + gate * (1.0 - gate_rate)))
        ).astype(bf16)
        d_normal = d_gated * gain * open_gate
        d_mixed = shrink * (d_normal - normal * jnp.mean(d_normal * normal, axis=1, keepdims=True))
        d_mixed = (scale * valid) * d_mixed
        yield
        queries = qkv_ref[:, head * DK : (head + 1) * DK]
        keys = qkv_ref[:, (heads + head) * DK : (heads + head + 1) * DK]
        begin = 2 * heads * DK + head * DV
        values = qkv_ref[:, begin : begin + DV]
        keys_f = keys.astype(f32)
        queries_f = queries.astype(f32)
        state = state_ref[0, head]
        inverse = inv_ref[0, head]
        solved = solved_ref[:, part]
        d_state = carried[head]
        key_prod = mm(keys, keys, ROWS)
        query_prod = mm(queries, keys, ROWS)
        strict = jnp.where(lower_st, beta_c * key_prod * fall, 0.0)
        mixing = query_prod * fall
        key_state = mm_right(keys, state)
        query_state = mm_right(queries, state)
        yield
        d_solved = mm_fine(mixing, d_mixed, COLS) + mm_fine(tail * keys_f, d_state)
        d_mixing = mm_both(d_mixed, solved, ROWS)
        yield
        d_right = mm_fine(inverse, d_solved, COLS)
        yield
        d_query_prod = d_mixing * fall
        d_strict = jnp.where(lower_st, -mm_both(d_right, solved, ROWS), 0.0)
        d_key_prod = d_strict * beta_c * fall
        d_key_state = -(beta_c * growth) * d_right
        yield
        carried[head] = (
            kept * d_state
            + mm_fine(growth * queries_f, d_mixed, COLS)
            + mm_right(keys, d_key_state, COLS)
        )
        yield
        d_query = mm_both(growth * d_mixed, state, ROWS) + mm_both(d_query_prod, keys_f)
        yield
        both = d_key_prod + d_key_prod.T
        from_tail = mm_both(solved, d_state, ROWS)
        d_key = (
            mm_both(d_key_state, state, ROWS)
            + mm_both(both, keys_f)
            + mm_both(d_query_prod, queries_f, COLS)
            + tail * from_tail
        )
        yield
        residual = values.astype(f32) - growth * key_state
        d_betas[head] = jnp.sum(d_right * residual, axis=1, keepdims=True) + jnp.sum(
            d_strict * key_prod * fall, axis=1, keepdims=True
        )
        spread = d_strict * strict + d_mixing * mixing
        from_last = tail * jnp.sum(keys_f * from_tail, axis=1, keepdims=True)
        d_growth = jnp.sum(d_mixed * query_state, axis=1, keepdims=True) - beta_c * jnp.sum(
            d_right * key_state, axis=1, keepdims=True
        )
        at_end = jnp.sum(from_last, axis=0, keepdims=True) + kept * jnp.sum(
            jnp.sum(d_state * state, axis=1, keepdims=True), axis=0, keepdims=True
        )
        yield
        d_cums[head] = (
            jnp.sum(spread, axis=1, keepdims=True)
            - jnp.sum(spread.T, axis=1, keepdims=True)
            + growth * d_growth
            - from_last
            + jnp.where(at_last, at_end, 0.0)
        )
        yield
        for grads, grad, start in ((d_queries, d_query, head * DK), (d_keys, d_key, (heads + head) * DK)):
            row = act[:, start : start + DK]
            small = lax.rsqrt(jnp.sum(row * row, axis=1, keepdims=True) + eps_norm)
            along = jnp.sum(row * grad, axis=1, keepdims=True) * small * small
            grads[head] = small * (grad - row * along)
        d_values[head] = beta_c * d_right
        yield

    in_turns([one_head(head) for head in range(heads)])
    dgain_ref[...] += sum(d_gains)
    d_conv = jnp.concatenate(d_queries + d_keys + d_values, axis=1) * slope
    d_low = d_conv.astype(bf16)
    same_rows = rows[2 * heads : 2 * heads + CONV, :]
    back_rows = shifted_back(d_low, after[...], same_rows, after_side[...])
    d_in = taps[0:1, :] * d_conv
    d_taps = [jnp.sum(d_conv * current, axis=0, keepdims=True)]
    for back in range(1, CONV):
        d_taps.append(jnp.sum(d_conv * moved[back - 1], axis=0, keepdims=True))
        d_in = d_in + taps[back : back + 1, :] * back_rows[back - 1]
    dtaps_ref[...] += jnp.concatenate(d_taps, axis=0)
    dproj_ref[:, : heads * (2 * DK + DV)] = d_in.astype(bf16)
    after[...] = d_low[:EDGE_ROWS, :]
    after_side[...] = same_rows
    d_decay = ones_left(triangle(True), jnp.concatenate(d_cums, axis=1))
    d_beta = jnp.concatenate(d_betas, axis=1)
    d_shifted = -d_decay * jnp.exp(log_ref[...]) / (1.0 + jnp.exp(-shifted))
    dgates_ref[...] = jnp.concatenate([d_shifted, d_beta * beta_all * (1.0 - beta_all)], axis=1)
    dheads_ref[...] += jnp.concatenate(
        [
            jnp.sum(d_decay * decay_all, axis=0, keepdims=True),
            jnp.sum(d_shifted, axis=0, keepdims=True),
        ],
        axis=1,
    )


BESIDE = pl.CostEstimate(flops=1, bytes_accessed=1, transcendentals=0)


def whole_block(shape):
    return pl.BlockSpec(shape, lambda i: (0,) * len(shape))


MIXER_PARAMS = pltpu.CompilerParams(vmem_limit_bytes=48 * 1024 * 1024)


def mixer_forward(proj, gates, side, taps, gain, decay_log, dt_bias):
    length = proj.shape[0]
    width = taps.shape[1]
    heads = decay_log.shape[1]
    gate_at = width // (heads * DV)
    blocks = length // SPAN
    return pl.pallas_call(
        functools.partial(mixer_forward_kernel, heads),
        grid=(blocks,),
        in_specs=[
            pl.BlockSpec((SPAN, width), lambda i: (i, 0)),
            pl.BlockSpec((SPAN, heads * DV), lambda i: (i, gate_at)),
            pl.BlockSpec((SPAN, 2 * heads), lambda i: (i, 0)),
            pl.BlockSpec((SPAN, SIDE), lambda i: (i, 0)),
            whole_block((CONV, width)),
            whole_block((1, DV)),
            whole_block((1, heads)),
            whole_block((1, heads)),
        ],
        out_specs=[
            pl.BlockSpec((SPAN, heads * DV), lambda i: (i, 0)),
            pl.BlockSpec((SPAN, heads * DV), lambda i: (i, 0)),
            pl.BlockSpec((SPAN, width), lambda i: (i, 0)),
            pl.BlockSpec((1, heads, DK, DV), lambda i: (i, 0, 0, 0)),
            pl.BlockSpec((1, heads, SPAN, SPAN), lambda i: (i, 0, 0, 0)),
            pl.BlockSpec((SPAN, heads * DV), lambda i: (i, 0)),
        ],
        out_shape=[
            jax.ShapeDtypeStruct((length, heads * DV), bf16),
            jax.ShapeDtypeStruct((length, heads * DV), f32),
            jax.ShapeDtypeStruct((length, width), bf16),
            jax.ShapeDtypeStruct((blocks, heads, DK, DV), f32),
            jax.ShapeDtypeStruct((blocks, heads, SPAN, SPAN), f32),
            jax.ShapeDtypeStruct((length, heads * DV), f32),
        ],
        scratch_shapes=[pltpu.VMEM((heads, DK, DV), f32), pltpu.VMEM((EDGE_ROWS, width), bf16)],
        compiler_params=MIXER_PARAMS,
        cost_estimate=BESIDE,
        name="mixer_forward",
    )(proj, proj, gates, side, taps, gain, decay_log, dt_bias)


def mixer_backward(proj, gates, side, taps, gain, decay_log, dt_bias, kept, d_gated):
    length = proj.shape[0]
    width = taps.shape[1]
    heads = decay_log.shape[1]
    gate_at = width // (heads * DV)
    blocks = length // SPAN
    end = blocks - 1
    ahead_rows = EDGE_ROWS
    per = SPAN // ahead_rows
    return pl.pallas_call(
        functools.partial(mixer_backward_kernel, heads),
        grid=(blocks,),
        in_specs=[
            pl.BlockSpec((SPAN, width), lambda i: (end - i, 0)),
            pl.BlockSpec((ahead_rows, width), lambda i: (jnp.maximum((end - i) * per - 1, 0), 0)),
            pl.BlockSpec((SPAN, heads * DV), lambda i: (end - i, gate_at)),
            pl.BlockSpec((SPAN, 2 * heads), lambda i: (end - i, 0)),
            pl.BlockSpec((SPAN, SIDE), lambda i: (end - i, 0)),
            whole_block((CONV, width)),
            whole_block((1, DV)),
            whole_block((1, heads)),
            whole_block((1, heads)),
            pl.BlockSpec((SPAN, heads * DV), lambda i: (end - i, 0)),
            pl.BlockSpec((SPAN, width), lambda i: (end - i, 0)),
            pl.BlockSpec((1, heads, DK, DV), lambda i: (end - i, 0, 0, 0)),
            pl.BlockSpec((1, heads, SPAN, SPAN), lambda i: (end - i, 0, 0, 0)),
            pl.BlockSpec((SPAN, heads * DV), lambda i: (end - i, 0)),
            pl.BlockSpec((SPAN, heads * DV), lambda i: (end - i, 0)),
        ],
        out_specs=[
            pl.BlockSpec((SPAN, width + heads * DV), lambda i: (end - i, 0)),
            pl.BlockSpec((SPAN, 2 * heads), lambda i: (end - i, 0)),
            whole_block((CONV, width)),
            whole_block((1, DV)),
            whole_block((1, 2 * heads)),
        ],
        out_shape=[
            jax.ShapeDtypeStruct((length, width + heads * DV), bf16),
            jax.ShapeDtypeStruct((length, 2 * heads), f32),
            jax.ShapeDtypeStruct((CONV, width), f32),
            jax.ShapeDtypeStruct((1, DV), f32),
            jax.ShapeDtypeStruct((1, 2 * heads), f32),
        ],
        scratch_shapes=[
            pltpu.VMEM((heads, DK, DV), f32),
            pltpu.VMEM((EDGE_ROWS, width), bf16),
            pltpu.VMEM((CONV, SPAN), f32),
        ],
        compiler_params=MIXER_PARAMS,
        cost_estimate=BESIDE,
        name="mixer_backward",
    )(proj, proj, proj, gates, side, taps, gain, decay_log, dt_bias, *kept, d_gated)


MESH = pl.DeviceIdType.MESH


def column_peers(seq, cores):
    count = seq * cores
    me = lax.axis_index("seq") * cores + lax.axis_index("wshard")
    peers = []
    for step in range(1, count):
        place = lax.rem(me + step, count)
        peers.append((place, {"seq": place // cores, "wshard": lax.rem(place, cores)}))
    return me, peers


def greet(ids):
    barrier = pltpu.get_barrier_semaphore()
    for device in ids:
        pl.semaphore_signal(barrier, inc=1, device_id=device, device_id_type=MESH)
    pl.semaphore_wait(barrier, len(ids))


def small_gather_kernel(seq, cores, in_ref, out_ref, send_sem, recv_sem):
    me, peers = column_peers(seq, cores)
    greet([device for _, device in peers])
    copies = []
    for at, (_, device) in enumerate(peers):
        copies.append(
            pltpu.make_async_remote_copy(
                src_ref=in_ref,
                dst_ref=out_ref.at[me],
                send_sem=send_sem.at[at],
                recv_sem=recv_sem.at[at],
                device_id=device,
                device_id_type=MESH,
            )
        )
        copies[-1].start()
    out_ref[me] = in_ref[...]
    for copy in copies:
        copy.wait()


def small_gather(values, seq, cores):
    count = seq * cores
    return pl.pallas_call(
        functools.partial(small_gather_kernel, seq, cores),
        out_shape=jax.ShapeDtypeStruct((count,) + values.shape, values.dtype),
        in_specs=[pl.BlockSpec(memory_space=pltpu.VMEM)],
        out_specs=pl.BlockSpec(memory_space=pltpu.VMEM),
        scratch_shapes=[pltpu.SemaphoreType.DMA((count - 1,)), pltpu.SemaphoreType.DMA((count - 1,))],
        compiler_params=pltpu.CompilerParams(collective_id=0, has_side_effects=True),
        cost_estimate=BESIDE,
        name="small_gather",
    )(values)


def small_sum_kernel(seq, cores, group, in_ref, out_ref, landed, send_sem, recv_sem, plane_send, plane_recv):
    me, peers = column_peers(seq, cores)
    part = lax.axis_index("group")
    plane = [{"group": lax.rem(part + step, group)} for step in range(1, group)]
    greet([device for _, device in peers] + plane)
    copies = []
    for at, (place, device) in enumerate(peers):
        copies.append(
            pltpu.make_async_remote_copy(
                src_ref=in_ref.at[place],
                dst_ref=landed.at[at],
                send_sem=send_sem.at[at],
                recv_sem=recv_sem.at[at],
                device_id=device,
                device_id_type=MESH,
            )
        )
        copies[-1].start()
    total = in_ref[me]
    for at, copy in enumerate(copies):
        copy.wait()
        total = total + landed[at]
    out_ref[part] = total
    copies = []
    for at, device in enumerate(plane):
        copies.append(
            pltpu.make_async_remote_copy(
                src_ref=out_ref.at[part],
                dst_ref=out_ref.at[part],
                send_sem=plane_send.at[at],
                recv_sem=plane_recv.at[at],
                device_id=device,
                device_id_type=MESH,
            )
        )
        copies[-1].start()
    for copy in copies:
        copy.wait()


def small_sum(values, seq, cores, group):
    count = seq * cores
    shape = values.shape[1:]
    return pl.pallas_call(
        functools.partial(small_sum_kernel, seq, cores, group),
        out_shape=jax.ShapeDtypeStruct((group,) + shape, values.dtype),
        in_specs=[pl.BlockSpec(memory_space=pltpu.VMEM)],
        out_specs=pl.BlockSpec(memory_space=pltpu.VMEM),
        scratch_shapes=[
            pltpu.VMEM((count - 1,) + shape, values.dtype),
            pltpu.SemaphoreType.DMA((count - 1,)),
            pltpu.SemaphoreType.DMA((count - 1,)),
            pltpu.SemaphoreType.DMA((group - 1,)),
            pltpu.SemaphoreType.DMA((group - 1,)),
        ],
        compiler_params=pltpu.CompilerParams(collective_id=1, has_side_effects=True),
        cost_estimate=BESIDE,
        name="small_sum",
    )(values)


def plane_gather_kernel(in_ref, out_ref, done, send_sem, recv_sem):
    part = lax.axis_index("group")
    near = part + 1 - 2 * lax.rem(part, 2)
    far = lax.rem(part + 2, 4)
    half = in_ref.shape[0] // 2
    first, second = pl.ds(0, half), pl.ds(half, half)
    greet([{"group": near}, {"group": far}])

    def send(source, block, rows, target, at):
        copy = pltpu.make_async_remote_copy(
            src_ref=source,
            dst_ref=out_ref.at[block, rows],
            send_sem=send_sem.at[at],
            recv_sem=recv_sem.at[at],
            device_id={"group": target},
            device_id_type=MESH,
        )
        copy.start()
        return copy

    copies = [
        send(in_ref.at[second], part, second, near, 0),
        send(in_ref.at[first], part, first, far, 1),
        send(in_ref.at[first], part, first, near, 2),
        send(in_ref.at[second], part, second, far, 3),
    ]
    own = pltpu.make_async_copy(in_ref, out_ref.at[part], done)
    own.start()
    copies[1].wait_recv()
    copies.append(send(out_ref.at[far, first], far, first, near, 4))
    copies[0].wait_recv()
    copies.append(send(out_ref.at[near, second], near, second, far, 5))
    for at, copy in enumerate(copies):
        copy.wait_send()
        if at >= 2:
            copy.wait_recv()
    own.wait()


def plane_gather(value):
    return pl.pallas_call(
        plane_gather_kernel,
        out_shape=jax.ShapeDtypeStruct((4,) + value.shape, value.dtype),
        in_specs=[pl.BlockSpec(memory_space=pltpu.VMEM)],
        out_specs=pl.BlockSpec(memory_space=pltpu.VMEM),
        scratch_shapes=[
            pltpu.SemaphoreType.DMA,
            pltpu.SemaphoreType.DMA((6,)),
            pltpu.SemaphoreType.DMA((6,)),
        ],
        compiler_params=pltpu.CompilerParams(
            collective_id=2, has_side_effects=True, vmem_limit_bytes=32 * 1024 * 1024
        ),
        cost_estimate=BESIDE,
        name="plane_gather",
    )(value)


def pick_columns_kernel(pieces, group, array_ref, out_ref):
    part = lax.axis_index("group")
    for own in range(group):

        @pl.when(part == own)
        def _():
            out_ref[...] = jnp.concatenate(
                [
                    array_ref[:, first + own * width : first + (own + 1) * width]
                    for first, width in pieces
                ],
                axis=1,
            )


def pick_columns(array, pieces, group):
    rows, columns = array.shape
    step = min(rows, 64)
    picked = sum(width for _, width in pieces)
    return pl.pallas_call(
        functools.partial(pick_columns_kernel, pieces, group),
        grid=(rows // step,),
        in_specs=[pl.BlockSpec((step, columns), lambda i: (i, 0))],
        out_specs=pl.BlockSpec((step, picked), lambda i: (i, 0)),
        out_shape=jax.ShapeDtypeStruct((rows, picked), array.dtype),
        compiler_params=MIXER_PARAMS,
        cost_estimate=BESIDE,
        name="pick_columns",
    )(array)


def join_columns_kernel(group, runs, parts_ref, *refs):
    out_ref = refs[-1]
    source, target = 0, 0
    for width, count in runs:
        pack = 1
        while pack < count and (pack * group * width) % 128:
            pack *= 2
        for first in range(0, count, pack):
            pieces = []
            for run in range(first, first + pack):
                for part in range(group):
                    begin = source + run * width
                    pieces.append(parts_ref[part, :, begin : begin + width].astype(f32))
            size = pack * group * width
            out_ref[:, target : target + size] = jnp.concatenate(pieces, axis=1)
            target += size
        source += count * width


def join_columns(parts, runs, total_rows=None, into=None):
    group, rows, columns = parts.shape
    step = min(rows, 32)
    total_rows = into.shape[0] if into is not None else total_rows or rows
    first = (total_rows - rows) // step if into is not None else 0
    args, specs, aliases = (parts,), [pl.BlockSpec((group, step, columns), lambda i: (0, i, 0))], {}
    if into is not None:
        args, aliases = (parts, into), {1: 0}
        specs.append(pl.BlockSpec(memory_space=pl.ANY))
    return pl.pallas_call(
        functools.partial(join_columns_kernel, group, runs),
        grid=(rows // step,),
        in_specs=specs,
        out_specs=pl.BlockSpec((step, group * columns), lambda i: (first + i, 0)),
        out_shape=jax.ShapeDtypeStruct((total_rows, group * columns), f32),
        input_output_aliases=aliases,
        compiler_params=MIXER_PARAMS,
        cost_estimate=BESIDE,
        name="join_columns",
    )(*args)


def join_turns_kernel(group, runs, halfway, near_ref, one_ref, two_ref, first_ref, second_ref, *refs):
    out_ref, far = refs[-2:]
    part = lax.axis_index("group")

    @pl.when(pl.program_id(0) < halfway)
    def _():
        far[...] = first_ref[...]

    @pl.when(pl.program_id(0) >= halfway)
    def _():
        far[...] = second_ref[...]

    turns = (near_ref, one_ref, two_ref, far)
    for own in range(group):

        @pl.when(part == own)
        def _():
            source, target = 0, 0
            for width, count in runs:
                pack = 1
                while pack < count and (pack * group * width) % 128:
                    pack *= 2
                for first in range(0, count, pack):
                    pieces = []
                    for run in range(first, first + pack):
                        begin = source + run * width
                        for owner in range(group):
                            pieces.append(
                                turns[own ^ owner][:, begin : begin + width].astype(f32)
                            )
                    size = pack * group * width
                    out_ref[:, target : target + size] = jnp.concatenate(pieces, axis=1)
                    target += size
                source += count * width


def join_turns(turns, runs, total_rows=None, into=None):
    near, one, two, (first_half, second_half) = turns
    rows, columns = near.shape
    half = first_half.shape[0]
    step = 32 if half % 32 == 0 else 16
    halfway = half // step
    total_rows = into.shape[0] if into is not None else total_rows or rows
    first = (total_rows - rows) // step if into is not None else 0
    block = pl.BlockSpec((step, columns), lambda i: (i, 0))
    args = [near, one, two, first_half, second_half]
    specs = [
        block,
        block,
        block,
        pl.BlockSpec((step, columns), lambda i: (jnp.minimum(i, halfway - 1), 0)),
        pl.BlockSpec((step, columns), lambda i: (jnp.maximum(i - halfway, 0), 0)),
    ]
    aliases = {}
    if into is not None:
        args.append(into)
        specs.append(pl.BlockSpec(memory_space=pl.ANY))
        aliases = {5: 0}
    return pl.pallas_call(
        functools.partial(join_turns_kernel, 4, runs, halfway),
        grid=(rows // step,),
        in_specs=specs,
        out_specs=pl.BlockSpec((step, 4 * columns), lambda i: (first + i, 0)),
        out_shape=jax.ShapeDtypeStruct((total_rows, 4 * columns), f32),
        scratch_shapes=[pltpu.VMEM((step, columns), near.dtype)],
        input_output_aliases=aliases,
        compiler_params=MIXER_PARAMS,
        cost_estimate=BESIDE,
        name="join_turns",
    )(*args)


def stack_turns_kernel(near_ref, one_ref, two_ref, first_ref, second_ref, out_ref):
    turn = lax.bitwise_xor(lax.axis_index("group"), pl.program_id(0))
    half = first_ref.shape[0]
    for at, ref in enumerate((near_ref, one_ref, two_ref)):

        @pl.when(turn == at)
        def _():
            out_ref[0] = ref[...].astype(out_ref.dtype)

    @pl.when(turn == 3)
    def _():
        out_ref[0, :half] = first_ref[...].astype(out_ref.dtype)
        out_ref[0, half:] = second_ref[...].astype(out_ref.dtype)


def stack_turns(turns, dtype):
    near, one, two, (first_half, second_half) = turns
    rows, columns = near.shape
    half = first_half.shape[0]
    whole = pl.BlockSpec((rows, columns), lambda i: (0, 0))
    halved = pl.BlockSpec((half, columns), lambda i: (0, 0))
    return pl.pallas_call(
        stack_turns_kernel,
        grid=(4,),
        in_specs=[whole, whole, whole, halved, halved],
        out_specs=pl.BlockSpec((1, rows, columns), lambda i: (i, 0, 0)),
        out_shape=jax.ShapeDtypeStruct((4, rows, columns), dtype),
        compiler_params=MIXER_PARAMS,
        cost_estimate=BESIDE,
        name="stack_turns",
    )(near, one, two, first_half, second_half)


def rms_scale(values, gain):
    return values * lax.rsqrt(jnp.mean(values * values, axis=-1, keepdims=True) + eps_norm) * gain


def swiglu(gate_up):
    half = gate_up.shape[1] // 2
    return jax.nn.silu(gate_up[:, :half]) * gate_up[:, half:]


def sum_parts(own, others):
    total = own.astype(f32)
    for part in others:
        total = total + part.astype(f32)
    return total


def dot(left, right):
    return jnp.dot(left, right, preferred_element_type=f32)


def dot_t(left, right):
    return lax.dot_general(left, right, (((0,), (0,)), ((), ())), preferred_element_type=f32)


def dot_back(left, right):
    return lax.dot_general(left, right, (((1,), (1,)), ((), ())), preferred_element_type=f32)


SHARDED = ("seq", "wshard")


class Place:
    def __init__(self, rows):
        self.group = lax.axis_size("group")
        self.seq = lax.axis_size("seq")
        self.cores = lax.axis_size("wshard")
        self.part = lax.axis_index("group")
        self.at_seq = lax.axis_index("seq")
        self.core = lax.axis_index("wshard")
        self.rows = rows
        self.per = rows // self.group
        self.subs = self.seq // self.group
        self.sources = self.seq // self.subs
        self.sub = self.at_seq % self.subs
        self.heads = H // self.group
        self.lane = self.seq * rows

    def deal(self, sorted_rows):
        width = sorted_rows.shape[1]
        if self.subs == 1:
            return lax.all_to_all(sorted_rows, "seq", split_axis=0, concat_axis=0, tiled=True)
        sent = jnp.zeros((self.group, self.subs, self.per, width), sorted_rows.dtype)
        sent = lax.dynamic_update_slice(
            sent,
            sorted_rows.reshape(self.group, 1, self.per, width),
            (0, self.at_seq // self.sources, 0, 0),
        )
        got = lax.all_to_all(
            sent.reshape(-1, width), "seq", split_axis=0, concat_axis=0, tiled=True
        )
        return lax.dynamic_slice(got, (self.sub * self.rows, 0), (self.rows, width))

    def undeal(self, rows):
        width = rows.shape[1]
        if self.subs == 1:
            return lax.all_to_all(rows, "seq", split_axis=0, concat_axis=0, tiled=True)
        sent = jnp.zeros((self.subs * self.rows, width), rows.dtype)
        sent = lax.dynamic_update_slice(sent, rows, (self.sub * self.rows, 0))
        got = lax.all_to_all(sent, "seq", split_axis=0, concat_axis=0, tiled=True)
        got = got.reshape(self.group, self.subs, self.per, width)
        got = lax.dynamic_slice(
            got, (0, self.at_seq // self.sources, 0, 0), (self.group, 1, self.per, width)
        )
        return got.reshape(self.rows, width)

    def swap(self, value, turn):
        if turn == 0:
            return value
        return lax.ppermute(value, "group", [(i, i ^ turn) for i in range(self.group)])

    def gather_any(self, rows):
        return jnp.concatenate([self.swap(rows, turn) for turn in range(self.group)], axis=0)

    def send_any(self, partial):
        own = partial[: self.rows]
        got = [
            self.swap(partial[turn * self.rows : (turn + 1) * self.rows], turn)
            for turn in range(1, self.group)
        ]
        return own, got

    def gather_places(self, rows, beside=()):
        width = rows.shape[1]
        got = [self.swap(rows, turn) for turn in range(1, self.group)]
        got, beside = lax.optimization_barrier((got, beside))
        lane = jnp.zeros((self.sources, self.group, self.per, width), rows.dtype)
        for turn, part in enumerate([rows] + got):
            part = part.reshape(self.sources, 1, self.per, width)
            lane = lax.dynamic_update_slice(lane, part, (0, self.part ^ turn, 0, 0))
        return lane.reshape(-1, width), beside

    def send_places(self, partial):
        width = partial.shape[1]
        lane = partial.reshape(self.sources, self.group, self.per, width)
        parts = [
            lax.dynamic_slice(
                lane, (0, self.part ^ turn, 0, 0), (self.sources, 1, self.per, width)
            ).reshape(self.rows, width)
            for turn in range(self.group)
        ]
        return parts[0], [self.swap(parts[turn], turn) for turn in range(1, self.group)]

    def near_turns(self, value):
        return (value, self.swap(value, 1), self.swap(value, 2))

    def far_turn(self, near):
        rows = near[0].shape[0] // 2
        return near + ((self.swap(near[2][:rows], 1), self.swap(near[1][rows:], 2)),)

    def turns_of(self, value):
        if self.group == 4 and value.ndim == 2 and value.shape[0] % 2 == 0:
            return self.far_turn(self.near_turns(value))
        return tuple(self.swap(value, turn) for turn in range(self.group))

    def joined(self, turns, runs, total_rows=None, into=None):
        if isinstance(turns[-1], tuple) and turns[-1][0].shape[0] % 16 == 0:
            return join_turns(turns, runs, total_rows, into)
        return join_columns(self.by_owner(turns), runs, total_rows, into)

    def stacked(self, turns, dtype):
        if isinstance(turns[-1], tuple) and turns[-1][0].shape[0] % 8 == 0:
            return stack_turns(turns, dtype)
        return self.by_owner(turns).astype(dtype)

    def by_owner(self, turns):
        value = turns[0]
        parts = jnp.zeros((self.group,) + value.shape, value.dtype)
        for turn, got in enumerate(turns):
            owner, begin = self.part ^ turn, 0
            for piece in got if isinstance(got, tuple) else (got,):
                parts = lax.dynamic_update_slice(
                    parts, piece[None], (owner, begin) + (0,) * (value.ndim - 1)
                )
                begin += piece.shape[0]
        return parts

    def gather_parts(self, value):
        return self.by_owner(self.turns_of(value))

    def to_lane(self, rows):
        if self.subs == 1:
            return rows
        every = lax.all_gather(rows, "seq", axis=0, tiled=True)
        length = rows.shape[0] * self.subs
        return lax.dynamic_slice(
            every, ((self.at_seq // self.subs) * length, 0), (length, rows.shape[1])
        )

    def to_own(self, lane_rows):
        if self.subs == 1:
            return lane_rows
        length = lane_rows.shape[0] // self.subs
        return lax.dynamic_slice(lane_rows, (self.sub * length, 0), (length, lane_rows.shape[1]))

    def head_columns(self, array, sections):
        pieces = []
        for begin, width in sections:
            for turn in range(self.heads):
                pieces.append(
                    lax.dynamic_slice(
                        array,
                        (0, begin + (turn * self.group + self.part) * width),
                        (array.shape[0], width),
                    )
                )
        return jnp.concatenate(pieces, axis=1)

    def core_rows(self, array, core):
        split = array.reshape(self.seq, self.cores, -1, array.shape[1])
        return lax.dynamic_index_in_dim(split, core, 1, keepdims=False).reshape(-1, array.shape[1])

    def core_sum(self, grad):
        if self.cores != 2:
            return grad
        got = lax.ppermute(self.core_rows(grad, 1 - self.core), "wshard", [(0, 1), (1, 0)])
        return (self.core_rows(grad, self.core).astype(f32) + got.astype(f32)).astype(bf16)

    def core_columns(self, array, halves_of=1):
        rows, columns = array.shape
        run = columns // (self.seq * self.cores)
        size = run // halves_of
        out = []
        for half in range(halves_of):
            picked = []
            for core in (1 - self.core, self.core) if self.cores == 2 else range(self.cores):
                picked.append(
                    [
                        lax.dynamic_slice(
                            array,
                            (0, (place * self.cores + core) * run + half * size),
                            (rows, size),
                        )
                        for place in range(self.seq)
                    ]
                )
            if self.cores == 2:
                out.append(tuple(jnp.concatenate(pieces, axis=1) for pieces in picked))
            else:
                every = [pieces[place] for place in range(self.seq) for pieces in picked]
                out.append((jnp.concatenate(every, axis=1),))
        return out

    def other_grad(self, lefts, right):
        if self.cores != 2:
            return None
        return lax.ppermute(dot_t(lefts[0], right).astype(bf16), "wshard", [(0, 1), (1, 0)])

    def own_grad(self, lefts, right, got):
        own = dot_t(lefts[-1], right)
        return (own if got is None else own + got.astype(f32)).astype(bf16)

    def scatter(self, grad):
        axes = "seq" if self.cores == 2 else SHARDED
        return lax.psum_scatter(grad, axes, scatter_dimension=0, tiled=True)

    def out_rows(self, w_out):
        width = w_out.shape[1]
        if self.subs == 1 and self.cores == 2:
            mine = lax.dynamic_slice(w_out, ((self.part % 2) * DV, 0), (DV, width))
            half = DV // 2
            kept = lax.dynamic_slice(mine, (self.core * half, 0), (half, width))
            other = lax.dynamic_slice(mine, ((1 - self.core) * half, 0), (half, width))
            got = lax.ppermute(other, "wshard", [(0, 1), (1, 0)])
            piece = jnp.where(self.core == self.part // 2, kept, got)
            return lax.all_gather(piece, SHARDED, axis=0, tiled=True)
        every = lax.all_gather(w_out, SHARDED, axis=0, tiled=True)
        every = every.reshape(self.heads, self.group, DV, width)
        return lax.dynamic_slice(
            every, (0, self.part, 0, 0), (self.heads, 1, DV, width)
        ).reshape(-1, width)

    def out_grad(self, gated, d_branch):
        if self.subs == 1 and self.cores == 2:
            lefts = self.core_columns(gated)[0]
            return self.own_grad(lefts, d_branch, self.other_grad(lefts, d_branch))
        width = d_branch.shape[1]
        grad = dot_t(gated, d_branch).astype(bf16)
        every = jnp.zeros((self.heads, self.group, DV, width), bf16)
        every = lax.dynamic_update_slice(
            every, grad.reshape(self.heads, 1, DV, width), (0, self.part, 0, 0)
        ).reshape(-1, width)
        return self.core_sum(every)

    def out_rows_join(self, turns):
        shard = turns[0]
        width = shard.shape[1]
        if self.subs == 1 and self.cores == 2:
            halves_all = self.stacked(turns, bf16)
            here = lax.dynamic_slice(halves_all, (2 * self.core, 0, 0), (2, DV // 2, width))
            there = lax.dynamic_slice(halves_all, (2 - 2 * self.core, 0, 0), (2, DV // 2, width))
            got = lax.ppermute(there, "wshard", [(0, 1), (1, 0)])
            first = jnp.where(self.core == 0, here, got)
            second = jnp.where(self.core == 0, got, here)
            return jnp.stack([first, second], axis=1).reshape(2 * DV, width).astype(f32)
        return lax.psum(shard, "group").astype(f32)

    def conv_pieces(self, conv_w):
        if self.subs > 1:
            return conv_w
        columns = conv_w.shape[1]
        wide = lax.dynamic_slice(conv_w, (0, self.part * DV), (CONV, DV))
        narrow = self.head_columns_of(conv_w, DK)
        return jnp.where(self.at_seq * self.cores + self.core >= 2 * HK // columns, wide, narrow)

    def head_columns_of(self, array, head_width):
        count = array.shape[1] // (self.group * head_width)
        return jnp.concatenate(
            [
                lax.dynamic_slice(
                    array,
                    (0, (turn * self.group + self.part) * head_width),
                    (array.shape[0], head_width),
                )
                for turn in range(count)
            ],
            axis=1,
        )

    def join_conv(self, pieces):
        pieces = pieces.reshape(self.seq * self.cores, CONV, -1).transpose(1, 0, 2)
        pieces = pieces.reshape(CONV, -1)
        return self.head_columns(pieces, QKV) if self.subs > 1 else pieces

    def split_conv(self, grad):
        devices = self.seq * self.cores
        if self.subs > 1:
            pieces, begin = [], 0
            mine = (jnp.arange(self.group) == self.part).astype(f32)[:, None]
            for _, head_width in QKV:
                end = begin + self.heads * head_width
                section = grad[:, begin:end].reshape(CONV, self.heads, 1, head_width) * mine
                pieces.append(section.reshape(CONV, -1))
                begin = end
            grad = jnp.concatenate(pieces, axis=1)
        return grad.reshape(CONV, devices, -1).transpose(1, 0, 2).reshape(devices, -1)

    def join_own_conv(self, parts):
        parts = parts.reshape(self.group, CONV, -1)
        if self.subs > 1:
            return jnp.sum(parts, axis=0)
        columns = parts.shape[2] * self.group
        wide = parts.transpose(1, 0, 2).reshape(CONV, columns)
        narrow = parts.reshape(self.group, CONV, -1, DK).transpose(1, 2, 0, 3).reshape(CONV, columns)
        return jnp.where(self.at_seq * self.cores + self.core >= 2 * HK // columns, wide, narrow)


QKV = ((0, DK), (HK, DK), (2 * HK, DV))
GATE = ((2 * HK + HV, DV),)


def side_array(lane_lengths, length):
    ends = jnp.cumsum(lane_lengths)
    bounds = jnp.concatenate([jnp.zeros((1,), jnp.int32), ends])
    places = jnp.arange(length, dtype=jnp.int32)
    crossed = places[:, None] >= bounds[None, :]
    block_begin = (places // SPAN) * SPAN
    counted = jnp.sum((crossed & (bounds[None, :] >= block_begin[:, None])).astype(jnp.int32), axis=1)
    segment = jnp.sum(crossed.astype(jnp.int32), axis=1)
    columns = [counted.astype(f32)]
    for back in range(1, CONV):
        earlier = jnp.sum((places[:, None] - back >= bounds[None, :]).astype(jnp.int32), axis=1)
        columns.append(((earlier == segment) & (places >= back)).astype(f32))
    columns.append((places < ends[-1]).astype(f32))
    columns += [jnp.zeros((length,), f32)] * (SIDE - len(columns))
    return jnp.stack(columns, axis=1)


def shards(
    tokens,
    cotangent,
    dealing,
    lengths,
    attn_gain,
    w_in,
    w_ab,
    conv_w,
    decay_log,
    dt_bias,
    o_gain,
    w_out,
    ffn_gain,
    w_gu,
    w_down,
):
    rows, width = tokens.shape
    at = Place(rows)
    heads = at.heads
    device_rows = w_down.shape[0]
    devices = at.seq * at.cores

    at_device = at.at_seq * at.cores + at.core

    pieces = []
    for begin, piece_width in QKV + GATE:
        pieces += [
            (begin + turn * at.group * piece_width, piece_width) for turn in range(heads)
        ]
    in_piece = pick_columns(w_in, tuple(pieces), at.group)

    ab_shard = at.head_columns(w_ab, ((0, 1), (H, 1)))
    conv_pieces = at.conv_pieces(conv_w)
    small = (attn_gain, ffn_gain, o_gain, ab_shard.reshape(-1), conv_pieces.reshape(-1))
    lengths_small = [array.shape[0] for array in small]
    filled = sum(lengths_small)
    rows_small = -(-filled // (16 * 128)) * 16
    packed = jnp.concatenate(small + (jnp.zeros((rows_small * 128 - filled,), bf16),))
    packed, in_piece = lax.optimization_barrier((packed, in_piece))
    in_mine = lax.all_gather(in_piece, SHARDED, axis=0, tiled=True)
    packed = small_gather(packed.reshape(rows_small, 128), at.seq, at.cores)
    packed, tokens, cotangent = lax.optimization_barrier((packed, tokens, cotangent))
    packed = packed.reshape(devices, -1)
    full, begin = [], 0
    for count in lengths_small:
        full.append(packed[:, begin : begin + count])
        begin += count
    attn_f, ffn_f, o_f = (array.reshape(-1).astype(f32) for array in full[:3])
    ab_mine = full[3].reshape(width, 2 * heads)
    conv_mine = at.join_conv(full[4]).astype(f32)

    def my_heads(values):
        return lax.dynamic_slice(values.reshape(heads, at.group), (0, at.part), (heads, 1)).reshape(1, -1)

    decay_mine, dt_mine = my_heads(decay_log), my_heads(dt_bias)

    member = (dealing[:, None] == jnp.arange(at.group, dtype=jnp.int32)[None, :]).astype(jnp.int32)
    before = dot(jnp.tril(jnp.ones((rows, rows), f32), -1).astype(bf16), member.astype(bf16))
    before = before.astype(jnp.int32)
    target = jnp.sum((before + at.per * jnp.arange(at.group, dtype=jnp.int32)) * member, axis=1)
    sorting = (target[None, :] == jnp.arange(rows, dtype=jnp.int32)[:, None]).astype(bf16)
    tokens_f = at.deal(dot(sorting, tokens).astype(bf16)).astype(f32)
    normed = rms_scale(tokens_f, attn_f).astype(bf16)
    normed, cotangent, w_out, w_gu, w_down = lax.optimization_barrier(
        (normed, cotangent, w_out, w_gu, w_down)
    )
    normed_all, _ = at.gather_places(normed)
    normed_all, normed_cores = lax.optimization_barrier(
        (normed_all, at.core_columns(normed_all, 2))
    )

    out_mine = at.out_rows(w_out)
    piece = device_rows // at.group
    gu_pieces = tuple((block * device_rows, piece) for block in range(2 * devices))
    gu_mine = lax.all_gather(
        pick_columns(w_gu, gu_pieces, at.group), SHARDED, axis=0, tiled=True
    )
    down_mine = lax.all_gather(
        lax.dynamic_slice(w_down, (at.part * piece, 0), (piece, width)), SHARDED, axis=0, tiled=True
    )
    cot_own = at.deal(dot(sorting, cotangent).astype(bf16))
    normed_all, cot_own = lax.optimization_barrier((normed_all, cot_own))

    lane_lengths = lax.dynamic_index_in_dim(
        at.gather_parts(lengths.reshape(-1)), at.at_seq // at.subs, 0, keepdims=False
    )
    side = side_array(lane_lengths, at.lane)
    gates_ab = at.to_lane(dot(normed_all, ab_mine))
    proj, cot_own = lax.optimization_barrier((dot(normed_all, in_mine), cot_own))
    cot_all = at.gather_any(cot_own)
    proj = at.to_lane(proj)
    mixer_args = (proj, gates_ab, side, conv_mine, o_f[None], decay_mine, dt_mine)
    gated_lane, *kept = mixer_forward(*mixer_args)
    gated_lane, cot_all = lax.optimization_barrier((gated_lane, cot_all))
    gated = at.to_own(gated_lane)
    own, got = at.send_places(dot(gated, out_mine).astype(bf16))
    resid = tokens_f + sum_parts(own, got)

    normed2_f, pull_norm2 = jax.vjp(rms_scale, resid, ffn_f)
    normed2_all = at.gather_any(normed2_f.astype(bf16))
    normed2_all, normed2_cores = lax.optimization_barrier(
        (normed2_all, at.core_columns(normed2_all)[0])
    )
    gate_up = dot(normed2_all, gu_mine)
    hidden_f, pull_ffn = jax.vjp(swiglu, gate_up)
    hidden = hidden_f.astype(bf16)

    d_down = at.core_sum(dot_t(hidden, cot_all).astype(bf16))
    d_down, hidden, cot_back = lax.optimization_barrier((d_down, hidden, cot_all))
    down_shard = at.scatter(d_down)
    d_hidden = dot_back(cot_back, down_mine)
    d_gate_up = pull_ffn(d_hidden)[0].astype(bf16)
    d_normed2_parts = dot_back(d_gate_up, gu_mine).astype(bf16)
    d_normed2_parts, d_gate_up = lax.optimization_barrier((d_normed2_parts, d_gate_up))
    own, got = at.send_any(d_normed2_parts)
    gu_got = at.other_grad(normed2_cores, d_gate_up)
    normed2_cores, down_shard = lax.optimization_barrier((normed2_cores, down_shard))
    d_gu = at.own_grad(normed2_cores, d_gate_up, gu_got)
    got, d_gu = lax.optimization_barrier((got, d_gu))
    gu_shard = at.scatter(d_gu)
    d_normed2 = sum_parts(own, got)
    d_resid_norm, d_ffn_gain = pull_norm2(d_normed2)
    d_resid = cot_own.astype(f32) + d_resid_norm

    d_branch_all, output_parts = at.gather_places(
        d_resid.astype(bf16), dot(hidden, down_mine).astype(bf16)
    )
    d_gated = dot_back(d_branch_all, out_mine)
    d_out = at.out_grad(gated, d_branch_all)
    d_gated, output_parts, down_shard, d_out = lax.optimization_barrier(
        (d_gated, output_parts, down_shard, d_out)
    )
    out_shard = at.scatter(d_out)
    output_own, output_got = at.send_any(output_parts)
    down_turns = at.near_turns(down_shard)
    d_proj_lane, d_gates_lane, d_conv_w, d_o_gain, d_heads = mixer_backward(
        *mixer_args, tuple(kept), at.to_lane(d_gated)
    )
    d_proj_lane, output_got, down_turns, gu_shard = lax.optimization_barrier(
        (d_proj_lane, output_got, down_turns, gu_shard)
    )
    gu_turns = at.near_turns(gu_shard)
    once = (at.sub == 0).astype(f32)
    d_conv_w, d_o_gain, d_heads = d_conv_w * once, d_o_gain * once, d_heads * once
    d_proj = at.to_own(d_proj_lane)
    d_ab = at.to_own(d_gates_lane).astype(bf16)
    in_got = [at.other_grad(lefts, d_proj) for lefts in normed_cores]
    first = at.own_grad(normed_cores[0], d_proj, in_got[0])
    first, in_got, d_proj = lax.optimization_barrier((first, in_got[1], d_proj))
    in_shards = [at.scatter(first)]
    second = at.own_grad(normed_cores[1], d_proj, in_got)
    second, d_proj, d_ab = lax.optimization_barrier((second, d_proj, d_ab))
    in_shards.append(at.scatter(second))
    d_normed_parts = (dot_back(d_proj, in_mine) + dot_back(d_ab, ab_mine)).astype(bf16)
    d_normed_parts, d_ab, output_got, out_shard = lax.optimization_barrier(
        (d_normed_parts, d_ab, output_got, out_shard)
    )
    output = (resid + sum_parts(output_own, output_got)).astype(bf16)
    own, got = at.send_places(d_normed_parts)
    d_w_ab = dot_t(normed_all, d_ab)
    got, d_w_ab, gu_turns = lax.optimization_barrier((got, d_w_ab, gu_turns))
    d_normed = sum_parts(own, got)
    value_norm, pull_norm = jax.vjp(rms_scale, tokens_f, attn_f)
    d_tokens_norm, d_attn_gain = pull_norm(d_normed)
    d_tokens = (d_resid + d_tokens_norm).astype(bf16)
    d_tokens, gu_turns, down_turns = lax.optimization_barrier((d_tokens, gu_turns, down_turns))
    gu_turns = at.far_turn(gu_turns)
    back = jnp.concatenate([output, d_tokens], axis=1)


    def to_blocks(array):
        return array.reshape(devices, -1)

    blocks = (
        to_blocks(d_attn_gain),
        to_blocks(d_ffn_gain),
        to_blocks(d_o_gain),
        to_blocks(d_w_ab),
        at.split_conv(d_conv_w),
        jnp.broadcast_to(d_heads, (devices, 2 * heads)),
    )
    sizes = [array.shape[1] for array in blocks]
    filled = sum(sizes)
    rows_small = -(-filled // 1024) * 8
    packed = jnp.concatenate(
        blocks + (jnp.zeros((devices, rows_small * 128 - filled), f32),), axis=1
    )
    summed = small_sum(packed.reshape(devices, rows_small, 128), at.seq, at.cores, at.group)

    in_runs = tuple((piece_width, heads) for _, piece_width in QKV + GATE)
    in_first, in_second = in_shards
    out_turns = at.near_turns(out_shard)
    in_first, summed, gu_turns, down_turns, out_turns = lax.optimization_barrier(
        (in_first, summed, gu_turns, down_turns, out_turns)
    )
    out_turns = at.far_turn(out_turns)
    down_turns = at.far_turn(down_turns)
    first_turns = at.near_turns(in_first)
    grad_w_gu = at.joined(gu_turns, ((piece, 2 * devices),))
    first_turns, grad_w_gu = lax.optimization_barrier((first_turns, grad_w_gu))
    first_turns = at.far_turn(first_turns)
    grad_w_down = at.stacked(down_turns, f32).reshape(device_rows, width)
    first_turns, grad_w_down, in_second, back = lax.optimization_barrier(
        (first_turns, grad_w_down, in_second, back)
    )
    second_turns = at.near_turns(in_second)
    returned = at.undeal(back)
    grad_w_in = at.joined(first_turns, in_runs, total_rows=w_in.shape[0])
    grad_w_out = at.out_rows_join(out_turns)
    second_turns, grad_w_in, grad_w_out = lax.optimization_barrier(
        (second_turns, grad_w_in, grad_w_out)
    )
    second_turns = at.far_turn(second_turns)
    second_turns, returned = lax.optimization_barrier((second_turns, returned))
    grad_w_in = at.joined(second_turns, in_runs, into=grad_w_in)
    returned = dot_t(sorting, returned).astype(bf16)

    summed = summed.reshape(at.group, -1)
    parts, begin = [], 0
    for size in sizes:
        parts.append(summed[:, begin : begin + size])
        begin += size
    grad_w_ab = parts[3].reshape(at.group, width // devices, 2, heads).transpose(1, 2, 3, 0)
    grad_heads = parts[5].reshape(at.group, 2, heads).transpose(1, 2, 0).reshape(2, H)
    return (
        returned[:, :width],
        returned[:, width:],
        jnp.sum(parts[0], axis=0),
        grad_w_in,
        grad_w_ab.reshape(width // devices, 2 * H),
        at.join_own_conv(parts[4]),
        grad_heads[0],
        grad_heads[1],
        jnp.sum(parts[2], axis=0),
        grad_w_out,
        jnp.sum(parts[1], axis=0),
        grad_w_gu,
        grad_w_down,
    )


def solution(mesh):
    placed = (
        P(("group", "seq", "wshard"), None),
        P(("group", "seq", "wshard"), None),
        P(("group", "seq", "wshard")),
        P("group", "wshard", None),
        P(("seq", "wshard")),
        P(("seq", "wshard"), None),
        P(("seq", "wshard"), None),
        P(None, ("seq", "wshard")),
        P(),
        P(),
        P(("seq", "wshard")),
        P(("seq", "wshard"), None),
        P(("seq", "wshard")),
        P(("seq", "wshard"), None),
        P(("seq", "wshard"), None),
    )
    return jax.shard_map(
        shards,
        mesh=mesh,
        in_specs=placed,
        out_specs=(
            P(("group", "seq", "wshard"), None),
            P(("group", "seq", "wshard"), None),
            P(("seq", "wshard")),
            P(("seq", "wshard"), None),
            P(("seq", "wshard"), None),
            P(None, ("seq", "wshard")),
            P(),
            P(),
            P(("seq", "wshard")),
            P(("seq", "wshard"), None),
            P(("seq", "wshard")),
            P(("seq", "wshard"), None),
            P(("seq", "wshard"), None),
        ),
        check_vma=False,
    )
```

```python
import functools

import jax
import jax.numpy as jnp
from jax import lax
from jax.experimental import pallas as pl
from jax.experimental.pallas import tpu as pltpu
from jax.sharding import PartitionSpec as P

H = 16
DK = 128
DV = 256
FF = 5632
CONV = 4
SPAN = 64
HK = 2048
HV = 4096
SIDE = 16
EDGE = 32

bf16 = jnp.bfloat16
f32 = jnp.float32
eps_norm = 1e-06


def mm(left, right, over=((1,), (0,))):
    return lax.dot_general(left, right, (over, ((), ())), preferred_element_type=f32)


def halves(value):
    high = value.astype(bf16)
    return high, (value - high.astype(f32)).astype(bf16)


def mm_fine(left, right, over=((1,), (0,))):
    left_high, left_low = halves(left)
    right_high, right_low = halves(right)
    return (
        mm(left_high, right_high, over)
        + mm(left_low, right_high, over)
        + mm(left_high, right_low, over)
    )


def mm_both(left, right, over=((1,), (0,))):
    return mm(left.astype(bf16), right.astype(bf16), over)


def mm_right(left, right, over=((1,), (0,))):
    high, low = halves(right)
    return mm(left, high, over) + mm(left, low, over)


ROWS = ((1,), (1,))
COLS = ((0,), (0,))


def unit_lower_inverses(stricts):
    groups = EDGE // 8
    count = SPAN // EDGE
    places = lax.broadcasted_iota(jnp.int32, (8, EDGE), 0)
    columns = lax.broadcasted_iota(jnp.int32, (8, EDGE), 1)
    blocks = {}
    for at, strict in enumerate(stricts):
        for block in range(count):
            begin = block * EDGE
            blocks[at, block] = (
                strict[begin : begin + EDGE, begin : begin + EDGE],
                [(places + 8 * part == columns).astype(f32) for part in range(groups)],
            )
    for row in range(EDGE - 1):
        first = row // 8
        for own, done in blocks.values():
            line = done[first][row - 8 * first : row - 8 * first + 1, :]
            for part in range(first, groups):
                column = own[8 * part : 8 * part + 8, row : row + 1]
                done[part] = done[part] - column * line
    inverses = []
    for at, strict in enumerate(stricts):
        parts = [jnp.concatenate(blocks[at, block][1], axis=0) for block in range(count)]
        size = EDGE
        while size < SPAN:
            joined = []
            for pair in range(0, len(parts), 2):
                begin = pair * size
                below = strict[begin + size : begin + 2 * size, begin : begin + size]
                upper, lower = parts[pair], parts[pair + 1]
                corner = mm_fine(mm_fine(lower, below), upper)
                joined.append(
                    jnp.concatenate(
                        [
                            jnp.concatenate([upper, jnp.zeros((size, size), f32)], axis=1),
                            jnp.concatenate([-corner, lower], axis=1),
                        ],
                        axis=0,
                    )
                )
            parts = joined
            size *= 2
        inverses.append(parts[0])
    return inverses


def in_turns(workers):
    workers = list(workers)
    while workers:
        for worker in list(workers):
            if next(worker, workers) is workers:
                workers.remove(worker)


def silu_parts(value):
    rate = 1.0 / (1.0 + jnp.exp(-value))
    return value * rate, rate


def gate_terms(heads, gates, decay_log, dt_bias):
    shifted = gates[:, :heads] + dt_bias
    beta = 1.0 / (1.0 + jnp.exp(-gates[:, heads:]))
    soft = jnp.maximum(shifted, 0.0) + jnp.log1p(jnp.exp(-jnp.abs(shifted)))
    return shifted, beta, -jnp.exp(decay_log) * soft


def ones_left(ones, value):
    high, rest = halves(value)
    high_f = high.astype(f32)
    rest, low = halves(value - high_f)
    return mm(ones, high) + mm(ones, rest) + mm(ones, low)


def triangle(upper):
    at_i = lax.broadcasted_iota(jnp.int32, (SPAN, SPAN), 0)
    at_j = lax.broadcasted_iota(jnp.int32, (SPAN, SPAN), 1)
    return jnp.where(at_i <= at_j if upper else at_i >= at_j, 1.0, 0.0).astype(bf16)


def side_columns(heads, gates, side, decay_log, dt_bias):
    shifted, beta, decay = gate_terms(heads, gates, decay_log, dt_bias)
    running = ones_left(triangle(False), decay)
    cols = jnp.concatenate(
        [running, beta, side[:, :CONV], jnp.zeros((SPAN, 128 - 2 * heads - CONV), f32)], axis=1
    )
    return cols, cols.T, shifted, beta, decay


EDGE_ROWS = 16


def shifted_rows(current, before, side):
    at_i = lax.broadcasted_iota(jnp.int32, (SPAN, SPAN + EDGE_ROWS), 0)
    at_j = lax.broadcasted_iota(jnp.int32, (SPAN, SPAN + EDGE_ROWS), 1)
    moves = [
        jnp.where(at_j == at_i + (EDGE_ROWS - back), side[:, back : back + 1], 0.0).astype(bf16)
        for back in range(1, CONV)
    ]
    moved = mm(jnp.concatenate(moves, axis=0), jnp.concatenate([before, current], axis=0))
    return [moved[(back - 1) * SPAN : back * SPAN, :] for back in range(1, CONV)]


def shifted_back(d_conv, later, same_rows, later_rows):
    at_i = lax.broadcasted_iota(jnp.int32, (SPAN, SPAN + EDGE_ROWS), 0)
    at_j = lax.broadcasted_iota(jnp.int32, (SPAN, SPAN + EDGE_ROWS), 1)
    moves = []
    for back in range(1, CONV):
        same = jnp.concatenate(
            [same_rows[back : back + 1, :], later_rows[back : back + 1, :EDGE_ROWS]], axis=1
        )
        moves.append(jnp.where(at_j == at_i + back, same, 0.0).astype(bf16))
    moved = mm(jnp.concatenate(moves, axis=0), jnp.concatenate([d_conv, later], axis=0))
    return [moved[(back - 1) * SPAN : back * SPAN, :] for back in range(1, CONV)]


def conv_forward(current, moved, taps):
    total = taps[0:1, :] * current
    for back in range(1, CONV):
        total = total + taps[back : back + 1, :] * moved[back - 1]
    return total


def block_terms(head, heads, cols, rows):
    cum_c = cols[:, head : head + 1]
    beta_c = cols[:, heads + head : heads + head + 1]
    count_c = cols[:, 2 * heads : 2 * heads + 1]
    cum_r = rows[head : head + 1, :]
    count_r = rows[2 * heads : 2 * heads + 1, :]
    at_i = lax.broadcasted_iota(jnp.int32, (SPAN, SPAN), 0)
    at_j = lax.broadcasted_iota(jnp.int32, (SPAN, SPAN), 1)
    same = count_c == count_r
    lower_eq = same & (at_i >= at_j)
    lower_st = same & (at_i > at_j)
    fall = jnp.where(lower_eq, jnp.exp(jnp.where(lower_eq, cum_c - cum_r, 0.0)), 0.0)
    growth = jnp.where(count_c == 0.0, jnp.exp(cum_c), 0.0)
    last = SPAN - 1
    tail = jnp.where(
        count_c == count_c[last : last + 1, :], jnp.exp(cum_c[last : last + 1, :] - cum_c), 0.0
    )
    return beta_c, lower_st, fall, growth, tail, growth[last : last + 1, :]


def mixer_forward_kernel(
    heads,
    conv_ref,
    gate_ref,
    gates_ref,
    side_ref,
    taps_ref,
    gain_ref,
    log_ref,
    bias_ref,
    gated_ref,
    mixed_ref,
    qkv_ref,
    state_ref,
    inv_ref,
    solved_ref,
    carried,
    before,
):
    @pl.when(pl.program_id(0) == 0)
    def _():
        carried[...] = jnp.zeros_like(carried)
        before[...] = jnp.zeros_like(before)

    side = side_ref[...]
    current = conv_ref[...].astype(bf16)
    moved = shifted_rows(current, before[...], side)
    act, _ = silu_parts(conv_forward(current.astype(f32), moved, taps_ref[...]))
    before[...] = current[SPAN - EDGE_ROWS :, :]
    cols, rows, _, _, _ = side_columns(heads, gates_ref[...], side, log_ref[...], bias_ref[...])
    valid = side[:, CONV : CONV + 1]
    gain = gain_ref[...]
    scale = DK ** (-0.5)
    terms, units, stricts = [], [], []
    for head in range(heads):
        terms.append(block_terms(head, heads, cols, rows))
        beta_c, lower_st, fall = terms[-1][:3]
        unit = []
        for begin in (head * DK, (heads + head) * DK):
            row = act[:, begin : begin + DK]
            row = row * lax.rsqrt(jnp.sum(row * row, axis=1, keepdims=True) + eps_norm)
            row = row.astype(bf16)
            qkv_ref[:, begin : begin + DK] = row
            unit.append(row)
        units.append(unit)
        stricts.append(jnp.where(lower_st, beta_c * mm(unit[1], unit[1], ROWS) * fall, 0.0))
    inverses = unit_lower_inverses(stricts)

    def one_head(head):
        beta_c, lower_st, fall, growth, tail, kept = terms[head]
        queries, keys = units[head]
        inverse = inverses[head]
        inv_ref[0, head] = inverse
        begin = 2 * heads * DK + head * DV
        values = act[:, begin : begin + DV].astype(bf16)
        qkv_ref[:, begin : begin + DV] = values
        state = carried[head]
        state_ref[0, head] = state
        query_prod = mm(queries, keys, ROWS)
        key_state = mm_right(keys, state)
        query_state = mm_right(queries, state)
        yield
        right_side = beta_c * (values.astype(f32) - growth * key_state)
        yield
        solved = mm_fine(inverse, right_side)
        yield
        part = slice(head * DV, (head + 1) * DV)
        solved_ref[:, part] = solved
        inner = mm_fine(query_prod * fall, solved)
        yield
        carried[head] = kept * state + mm_fine(tail * keys.astype(f32), solved, COLS)
        yield
        mixed = scale * (growth * query_state + inner) * valid
        mixed_ref[:, part] = mixed
        shrink = lax.rsqrt(jnp.mean(mixed * mixed, axis=1, keepdims=True) + eps_norm)
        open_gate, _ = silu_parts(gate_ref[:, part])
        gated_ref[:, part] = (mixed * shrink * gain * open_gate).astype(bf16)
        yield

    in_turns([one_head(head) for head in range(heads)])


def mixer_backward_kernel(
    heads,
    conv_ref,
    ahead_ref,
    gate_ref,
    gates_ref,
    side_ref,
    taps_ref,
    gain_ref,
    log_ref,
    bias_ref,
    mixed_ref,
    qkv_ref,
    state_ref,
    inv_ref,
    solved_ref,
    cot_ref,
    dproj_ref,
    dgates_ref,
    dtaps_ref,
    dgain_ref,
    dheads_ref,
    carried,
    after,
    after_side,
):
    @pl.when(pl.program_id(0) == 0)
    def _():
        carried[...] = jnp.zeros_like(carried)
        after[...] = jnp.zeros_like(after)
        after_side[...] = jnp.zeros_like(after_side)
        dtaps_ref[...] = jnp.zeros_like(dtaps_ref)
        dgain_ref[...] = jnp.zeros_like(dgain_ref)
        dheads_ref[...] = jnp.zeros_like(dheads_ref)

    side = side_ref[...]
    taps = taps_ref[...]
    gain = gain_ref[...]
    valid = side[:, CONV : CONV + 1]
    current = conv_ref[...].astype(bf16)
    moved = shifted_rows(current, ahead_ref[...].astype(bf16), side)
    current = current.astype(f32)
    conv_out = conv_forward(current, moved, taps)
    act, rate = silu_parts(conv_out)
    slope = rate * (1.0 + conv_out * (1.0 - rate))
    cols, rows, shifted, beta_all, decay_all = side_columns(
        heads, gates_ref[...], side, log_ref[...], bias_ref[...]
    )
    scale = DK ** (-0.5)
    at_last = lax.broadcasted_iota(jnp.int32, (SPAN, 1), 0) == SPAN - 1
    d_betas, d_cums, d_gains = [None] * heads, [None] * heads, [None] * heads
    d_queries, d_keys, d_values = [None] * heads, [None] * heads, [None] * heads

    def one_head(head):
        beta_c, lower_st, fall, growth, tail, kept = block_terms(head, heads, cols, rows)
        part = slice(head * DV, (head + 1) * DV)
        mixed = mixed_ref[:, part]
        gate = gate_ref[:, part]
        d_gated = cot_ref[:, part]
        shrink = lax.rsqrt(jnp.mean(mixed * mixed, axis=1, keepdims=True) + eps_norm)
        normal = mixed * shrink
        open_gate, gate_rate = silu_parts(gate)
        with_normal = d_gated * normal
        d_gains[head] = jnp.sum(with_normal * open_gate, axis=0, keepdims=True)
        begin = 2 * heads * DK + (heads + head) * DV
        dproj_ref[:, begin : begin + DV] = (
            with_normal * gain * (gate_rate * (1.0 + gate * (1.0 - gate_rate)))
        ).astype(bf16)
        d_normal = d_gated * gain * open_gate
        d_mixed = shrink * (d_normal - normal * jnp.mean(d_normal * normal, axis=1, keepdims=True))
        d_mixed = (scale * valid) * d_mixed
        yield
        queries = qkv_ref[:, head * DK : (head + 1) * DK]
        keys = qkv_ref[:, (heads + head) * DK : (heads + head + 1) * DK]
        begin = 2 * heads * DK + head * DV
        values = qkv_ref[:, begin : begin + DV]
        keys_f = keys.astype(f32)
        queries_f = queries.astype(f32)
        state = state_ref[0, head]
        inverse = inv_ref[0, head]
        solved = solved_ref[:, part]
        d_state = carried[head]
        key_prod = mm(keys, keys, ROWS)
        query_prod = mm(queries, keys, ROWS)
        strict = jnp.where(lower_st, beta_c * key_prod * fall, 0.0)
        mixing = query_prod * fall
        key_state = mm_right(keys, state)
        query_state = mm_right(queries, state)
        yield
        d_solved = mm_fine(mixing, d_mixed, COLS) + mm_fine(tail * keys_f, d_state)
        d_mixing = mm_both(d_mixed, solved, ROWS)
        yield
        d_right = mm_fine(inverse, d_solved, COLS)
        yield
        d_query_prod = d_mixing * fall
        d_strict = jnp.where(lower_st, -mm_both(d_right, solved, ROWS), 0.0)
        d_key_prod = d_strict * beta_c * fall
        d_key_state = -(beta_c * growth) * d_right
        yield
        carried[head] = (
            kept * d_state
            + mm_fine(growth * queries_f, d_mixed, COLS)
            + mm_right(keys, d_key_state, COLS)
        )
        yield
        d_query = mm_both(growth * d_mixed, state, ROWS) + mm_both(d_query_prod, keys_f)
        yield
        both = d_key_prod + d_key_prod.T
        from_tail = mm_both(solved, d_state, ROWS)
        d_key = (
            mm_both(d_key_state, state, ROWS)
            + mm_both(both, keys_f)
            + mm_both(d_query_prod, queries_f, COLS)
            + tail * from_tail
        )
        yield
        residual = values.astype(f32) - growth * key_state
        d_betas[head] = jnp.sum(d_right * residual, axis=1, keepdims=True) + jnp.sum(
            d_strict * key_prod * fall, axis=1, keepdims=True
        )
        spread = d_strict * strict + d_mixing * mixing
        from_last = tail * jnp.sum(keys_f * from_tail, axis=1, keepdims=True)
        d_growth = jnp.sum(d_mixed * query_state, axis=1, keepdims=True) - beta_c * jnp.sum(
            d_right * key_state, axis=1, keepdims=True
        )
        at_end = jnp.sum(from_last, axis=0, keepdims=True) + kept * jnp.sum(
            jnp.sum(d_state * state, axis=1, keepdims=True), axis=0, keepdims=True
        )
        yield
        d_cums[head] = (
            jnp.sum(spread, axis=1, keepdims=True)
            - jnp.sum(spread.T, axis=1, keepdims=True)
            + growth * d_growth
            - from_last
            + jnp.where(at_last, at_end, 0.0)
        )
        yield
        for grads, grad, start in ((d_queries, d_query, head * DK), (d_keys, d_key, (heads + head) * DK)):
            row = act[:, start : start + DK]
            small = lax.rsqrt(jnp.sum(row * row, axis=1, keepdims=True) + eps_norm)
            along = jnp.sum(row * grad, axis=1, keepdims=True) * small * small
            grads[head] = small * (grad - row * along)
        d_values[head] = beta_c * d_right
        yield

    in_turns([one_head(head) for head in range(heads)])
    dgain_ref[...] += sum(d_gains)
    d_conv = jnp.concatenate(d_queries + d_keys + d_values, axis=1) * slope
    d_low = d_conv.astype(bf16)
    same_rows = rows[2 * heads : 2 * heads + CONV, :]
    back_rows = shifted_back(d_low, after[...], same_rows, after_side[...])
    d_in = taps[0:1, :] * d_conv
    d_taps = [jnp.sum(d_conv * current, axis=0, keepdims=True)]
    for back in range(1, CONV):
        d_taps.append(jnp.sum(d_conv * moved[back - 1], axis=0, keepdims=True))
        d_in = d_in + taps[back : back + 1, :] * back_rows[back - 1]
    dtaps_ref[...] += jnp.concatenate(d_taps, axis=0)
    dproj_ref[:, : heads * (2 * DK + DV)] = d_in.astype(bf16)
    after[...] = d_low[:EDGE_ROWS, :]
    after_side[...] = same_rows
    d_decay = ones_left(triangle(True), jnp.concatenate(d_cums, axis=1))
    d_beta = jnp.concatenate(d_betas, axis=1)
    d_shifted = -d_decay * jnp.exp(log_ref[...]) / (1.0 + jnp.exp(-shifted))
    dgates_ref[...] = jnp.concatenate([d_shifted, d_beta * beta_all * (1.0 - beta_all)], axis=1)
    dheads_ref[...] += jnp.concatenate(
        [
            jnp.sum(d_decay * decay_all, axis=0, keepdims=True),
            jnp.sum(d_shifted, axis=0, keepdims=True),
        ],
        axis=1,
    )


BESIDE = pl.CostEstimate(flops=1, bytes_accessed=1, transcendentals=0)


def whole_block(shape):
    return pl.BlockSpec(shape, lambda i: (0,) * len(shape))


MIXER_PARAMS = pltpu.CompilerParams(vmem_limit_bytes=48 * 1024 * 1024)


def mixer_forward(proj, gates, side, taps, gain, decay_log, dt_bias):
    length = proj.shape[0]
    width = taps.shape[1]
    heads = decay_log.shape[1]
    gate_at = width // (heads * DV)
    blocks = length // SPAN
    return pl.pallas_call(
        functools.partial(mixer_forward_kernel, heads),
        grid=(blocks,),
        in_specs=[
            pl.BlockSpec((SPAN, width), lambda i: (i, 0)),
            pl.BlockSpec((SPAN, heads * DV), lambda i: (i, gate_at)),
            pl.BlockSpec((SPAN, 2 * heads), lambda i: (i, 0)),
            pl.BlockSpec((SPAN, SIDE), lambda i: (i, 0)),
            whole_block((CONV, width)),
            whole_block((1, DV)),
            whole_block((1, heads)),
            whole_block((1, heads)),
        ],
        out_specs=[
            pl.BlockSpec((SPAN, heads * DV), lambda i: (i, 0)),
            pl.BlockSpec((SPAN, heads * DV), lambda i: (i, 0)),
            pl.BlockSpec((SPAN, width), lambda i: (i, 0)),
            pl.BlockSpec((1, heads, DK, DV), lambda i: (i, 0, 0, 0)),
            pl.BlockSpec((1, heads, SPAN, SPAN), lambda i: (i, 0, 0, 0)),
            pl.BlockSpec((SPAN, heads * DV), lambda i: (i, 0)),
        ],
        out_shape=[
            jax.ShapeDtypeStruct((length, heads * DV), bf16),
            jax.ShapeDtypeStruct((length, heads * DV), f32),
            jax.ShapeDtypeStruct((length, width), bf16),
            jax.ShapeDtypeStruct((blocks, heads, DK, DV), f32),
            jax.ShapeDtypeStruct((blocks, heads, SPAN, SPAN), f32),
            jax.ShapeDtypeStruct((length, heads * DV), f32),
        ],
        scratch_shapes=[pltpu.VMEM((heads, DK, DV), f32), pltpu.VMEM((EDGE_ROWS, width), bf16)],
        compiler_params=MIXER_PARAMS,
        cost_estimate=BESIDE,
        name="mixer_forward",
    )(proj, proj, gates, side, taps, gain, decay_log, dt_bias)


def mixer_backward(proj, gates, side, taps, gain, decay_log, dt_bias, kept, d_gated):
    length = proj.shape[0]
    width = taps.shape[1]
    heads = decay_log.shape[1]
    gate_at = width // (heads * DV)
    blocks = length // SPAN
    end = blocks - 1
    ahead_rows = EDGE_ROWS
    per = SPAN // ahead_rows
    return pl.pallas_call(
        functools.partial(mixer_backward_kernel, heads),
        grid=(blocks,),
        in_specs=[
            pl.BlockSpec((SPAN, width), lambda i: (end - i, 0)),
            pl.BlockSpec((ahead_rows, width), lambda i: (jnp.maximum((end - i) * per - 1, 0), 0)),
            pl.BlockSpec((SPAN, heads * DV), lambda i: (end - i, gate_at)),
            pl.BlockSpec((SPAN, 2 * heads), lambda i: (end - i, 0)),
            pl.BlockSpec((SPAN, SIDE), lambda i: (end - i, 0)),
            whole_block((CONV, width)),
            whole_block((1, DV)),
            whole_block((1, heads)),
            whole_block((1, heads)),
            pl.BlockSpec((SPAN, heads * DV), lambda i: (end - i, 0)),
            pl.BlockSpec((SPAN, width), lambda i: (end - i, 0)),
            pl.BlockSpec((1, heads, DK, DV), lambda i: (end - i, 0, 0, 0)),
            pl.BlockSpec((1, heads, SPAN, SPAN), lambda i: (end - i, 0, 0, 0)),
            pl.BlockSpec((SPAN, heads * DV), lambda i: (end - i, 0)),
            pl.BlockSpec((SPAN, heads * DV), lambda i: (end - i, 0)),
        ],
        out_specs=[
            pl.BlockSpec((SPAN, width + heads * DV), lambda i: (end - i, 0)),
            pl.BlockSpec((SPAN, 2 * heads), lambda i: (end - i, 0)),
            whole_block((CONV, width)),
            whole_block((1, DV)),
            whole_block((1, 2 * heads)),
        ],
        out_shape=[
            jax.ShapeDtypeStruct((length, width + heads * DV), bf16),
            jax.ShapeDtypeStruct((length, 2 * heads), f32),
            jax.ShapeDtypeStruct((CONV, width), f32),
            jax.ShapeDtypeStruct((1, DV), f32),
            jax.ShapeDtypeStruct((1, 2 * heads), f32),
        ],
        scratch_shapes=[
            pltpu.VMEM((heads, DK, DV), f32),
            pltpu.VMEM((EDGE_ROWS, width), bf16),
            pltpu.VMEM((CONV, SPAN), f32),
        ],
        compiler_params=MIXER_PARAMS,
        cost_estimate=BESIDE,
        name="mixer_backward",
    )(proj, proj, proj, gates, side, taps, gain, decay_log, dt_bias, *kept, d_gated)


MESH = pl.DeviceIdType.MESH


def column_peers(seq, cores):
    count = seq * cores
    me = lax.axis_index("seq") * cores + lax.axis_index("wshard")
    peers = []
    for step in range(1, count):
        place = lax.rem(me + step, count)
        peers.append((place, {"seq": place // cores, "wshard": lax.rem(place, cores)}))
    return me, peers


def greet(ids):
    barrier = pltpu.get_barrier_semaphore()
    for device in ids:
        pl.semaphore_signal(barrier, inc=1, device_id=device, device_id_type=MESH)
    pl.semaphore_wait(barrier, len(ids))


def small_gather_kernel(seq, cores, in_ref, out_ref, send_sem, recv_sem):
    me, peers = column_peers(seq, cores)
    greet([device for _, device in peers])
    copies = []
    for at, (_, device) in enumerate(peers):
        copies.append(
            pltpu.make_async_remote_copy(
                src_ref=in_ref,
                dst_ref=out_ref.at[me],
                send_sem=send_sem.at[at],
                recv_sem=recv_sem.at[at],
                device_id=device,
                device_id_type=MESH,
            )
        )
        copies[-1].start()
    out_ref[me] = in_ref[...]
    for copy in copies:
        copy.wait()


def small_gather(values, seq, cores):
    count = seq * cores
    return pl.pallas_call(
        functools.partial(small_gather_kernel, seq, cores),
        out_shape=jax.ShapeDtypeStruct((count,) + values.shape, values.dtype),
        in_specs=[pl.BlockSpec(memory_space=pltpu.VMEM)],
        out_specs=pl.BlockSpec(memory_space=pltpu.VMEM),
        scratch_shapes=[pltpu.SemaphoreType.DMA((count - 1,)), pltpu.SemaphoreType.DMA((count - 1,))],
        compiler_params=pltpu.CompilerParams(collective_id=0, has_side_effects=True),
        cost_estimate=BESIDE,
        name="small_gather",
    )(values)


def small_sum_kernel(seq, cores, group, in_ref, out_ref, landed, send_sem, recv_sem, plane_send, plane_recv):
    me, peers = column_peers(seq, cores)
    part = lax.axis_index("group")
    plane = [{"group": lax.rem(part + step, group)} for step in range(1, group)]
    greet([device for _, device in peers] + plane)
    copies = []
    for at, (place, device) in enumerate(peers):
        copies.append(
            pltpu.make_async_remote_copy(
                src_ref=in_ref.at[place],
                dst_ref=landed.at[at],
                send_sem=send_sem.at[at],
                recv_sem=recv_sem.at[at],
                device_id=device,
                device_id_type=MESH,
            )
        )
        copies[-1].start()
    total = in_ref[me]
    for at, copy in enumerate(copies):
        copy.wait()
        total = total + landed[at]
    out_ref[part] = total
    copies = []
    for at, device in enumerate(plane):
        copies.append(
            pltpu.make_async_remote_copy(
                src_ref=out_ref.at[part],
                dst_ref=out_ref.at[part],
                send_sem=plane_send.at[at],
                recv_sem=plane_recv.at[at],
                device_id=device,
                device_id_type=MESH,
            )
        )
        copies[-1].start()
    for copy in copies:
        copy.wait()


def small_sum(values, seq, cores, group):
    count = seq * cores
    shape = values.shape[1:]
    return pl.pallas_call(
        functools.partial(small_sum_kernel, seq, cores, group),
        out_shape=jax.ShapeDtypeStruct((group,) + shape, values.dtype),
        in_specs=[pl.BlockSpec(memory_space=pltpu.VMEM)],
        out_specs=pl.BlockSpec(memory_space=pltpu.VMEM),
        scratch_shapes=[
            pltpu.VMEM((count - 1,) + shape, values.dtype),
            pltpu.SemaphoreType.DMA((count - 1,)),
            pltpu.SemaphoreType.DMA((count - 1,)),
            pltpu.SemaphoreType.DMA((group - 1,)),
            pltpu.SemaphoreType.DMA((group - 1,)),
        ],
        compiler_params=pltpu.CompilerParams(collective_id=1, has_side_effects=True),
        cost_estimate=BESIDE,
        name="small_sum",
    )(values)


def plane_gather_kernel(in_ref, out_ref, done, send_sem, recv_sem):
    part = lax.axis_index("group")
    near = part + 1 - 2 * lax.rem(part, 2)
    far = lax.rem(part + 2, 4)
    half = in_ref.shape[0] // 2
    first, second = pl.ds(0, half), pl.ds(half, half)
    greet([{"group": near}, {"group": far}])

    def send(source, block, rows, target, at):
        copy = pltpu.make_async_remote_copy(
            src_ref=source,
            dst_ref=out_ref.at[block, rows],
            send_sem=send_sem.at[at],
            recv_sem=recv_sem.at[at],
            device_id={"group": target},
            device_id_type=MESH,
        )
        copy.start()
        return copy

    copies = [
        send(in_ref.at[second], part, second, near, 0),
        send(in_ref.at[first], part, first, far, 1),
        send(in_ref.at[first], part, first, near, 2),
        send(in_ref.at[second], part, second, far, 3),
    ]
    own = pltpu.make_async_copy(in_ref, out_ref.at[part], done)
    own.start()
    copies[1].wait_recv()
    copies.append(send(out_ref.at[far, first], far, first, near, 4))
    copies[0].wait_recv()
    copies.append(send(out_ref.at[near, second], near, second, far, 5))
    for at, copy in enumerate(copies):
        copy.wait_send()
        if at >= 2:
            copy.wait_recv()
    own.wait()


def plane_gather(value):
    return pl.pallas_call(
        plane_gather_kernel,
        out_shape=jax.ShapeDtypeStruct((4,) + value.shape, value.dtype),
        in_specs=[pl.BlockSpec(memory_space=pltpu.VMEM)],
        out_specs=pl.BlockSpec(memory_space=pltpu.VMEM),
        scratch_shapes=[
            pltpu.SemaphoreType.DMA,
            pltpu.SemaphoreType.DMA((6,)),
            pltpu.SemaphoreType.DMA((6,)),
        ],
        compiler_params=pltpu.CompilerParams(
            collective_id=2, has_side_effects=True, vmem_limit_bytes=32 * 1024 * 1024
        ),
        cost_estimate=BESIDE,
        name="plane_gather",
    )(value)


def pick_columns_kernel(pieces, group, array_ref, out_ref):
    part = lax.axis_index("group")
    for own in range(group):

        @pl.when(part == own)
        def _():
            out_ref[...] = jnp.concatenate(
                [
                    array_ref[:, first + own * width : first + (own + 1) * width]
                    for first, width in pieces
                ],
                axis=1,
            )


def pick_columns(array, pieces, group):
    rows, columns = array.shape
    step = min(rows, 64)
    picked = sum(width for _, width in pieces)
    return pl.pallas_call(
        functools.partial(pick_columns_kernel, pieces, group),
        grid=(rows // step,),
        in_specs=[pl.BlockSpec((step, columns), lambda i: (i, 0))],
        out_specs=pl.BlockSpec((step, picked), lambda i: (i, 0)),
        out_shape=jax.ShapeDtypeStruct((rows, picked), array.dtype),
        compiler_params=MIXER_PARAMS,
        cost_estimate=BESIDE,
        name="pick_columns",
    )(array)


def join_columns_kernel(group, runs, parts_ref, *refs):
    out_ref = refs[-1]
    source, target = 0, 0
    for width, count in runs:
        pack = 1
        while pack < count and (pack * group * width) % 128:
            pack *= 2
        for first in range(0, count, pack):
            pieces = []
            for run in range(first, first + pack):
                for part in range(group):
                    begin = source + run * width
                    pieces.append(parts_ref[part, :, begin : begin + width].astype(f32))
            size = pack * group * width
            out_ref[:, target : target + size] = jnp.concatenate(pieces, axis=1)
            target += size
        source += count * width


def join_columns(parts, runs, total_rows=None, into=None):
    group, rows, columns = parts.shape
    step = min(rows, 32)
    total_rows = into.shape[0] if into is not None else total_rows or rows
    first = (total_rows - rows) // step if into is not None else 0
    args, specs, aliases = (parts,), [pl.BlockSpec((group, step, columns), lambda i: (0, i, 0))], {}
    if into is not None:
        args, aliases = (parts, into), {1: 0}
        specs.append(pl.BlockSpec(memory_space=pl.ANY))
    return pl.pallas_call(
        functools.partial(join_columns_kernel, group, runs),
        grid=(rows // step,),
        in_specs=specs,
        out_specs=pl.BlockSpec((step, group * columns), lambda i: (first + i, 0)),
        out_shape=jax.ShapeDtypeStruct((total_rows, group * columns), f32),
        input_output_aliases=aliases,
        compiler_params=MIXER_PARAMS,
        cost_estimate=BESIDE,
        name="join_columns",
    )(*args)


def join_turns_kernel(group, runs, halfway, near_ref, one_ref, two_ref, first_ref, second_ref, *refs):
    out_ref, far = refs[-2:]
    part = lax.axis_index("group")

    @pl.when(pl.program_id(0) < halfway)
    def _():
        far[...] = first_ref[...]

    @pl.when(pl.program_id(0) >= halfway)
    def _():
        far[...] = second_ref[...]

    turns = (near_ref, one_ref, two_ref, far)
    for own in range(group):

        @pl.when(part == own)
        def _():
            source, target = 0, 0
            for width, count in runs:
                pack = 1
                while pack < count and (pack * group * width) % 128:
                    pack *= 2
                for first in range(0, count, pack):
                    pieces = []
                    for run in range(first, first + pack):
                        begin = source + run * width
                        for owner in range(group):
                            pieces.append(
                                turns[own ^ owner][:, begin : begin + width].astype(f32)
                            )
                    size = pack * group * width
                    out_ref[:, target : target + size] = jnp.concatenate(pieces, axis=1)
                    target += size
                source += count * width


def join_turns(turns, runs, total_rows=None, into=None):
    near, one, two, (first_half, second_half) = turns
    rows, columns = near.shape
    half = first_half.shape[0]
    step = 32 if half % 32 == 0 else 16
    halfway = half // step
    total_rows = into.shape[0] if into is not None else total_rows or rows
    first = (total_rows - rows) // step if into is not None else 0
    block = pl.BlockSpec((step, columns), lambda i: (i, 0))
    args = [near, one, two, first_half, second_half]
    specs = [
        block,
        block,
        block,
        pl.BlockSpec((step, columns), lambda i: (jnp.minimum(i, halfway - 1), 0)),
        pl.BlockSpec((step, columns), lambda i: (jnp.maximum(i - halfway, 0), 0)),
    ]
    aliases = {}
    if into is not None:
        args.append(into)
        specs.append(pl.BlockSpec(memory_space=pl.ANY))
        aliases = {5: 0}
    return pl.pallas_call(
        functools.partial(join_turns_kernel, 4, runs, halfway),
        grid=(rows // step,),
        in_specs=specs,
        out_specs=pl.BlockSpec((step, 4 * columns), lambda i: (first + i, 0)),
        out_shape=jax.ShapeDtypeStruct((total_rows, 4 * columns), f32),
        scratch_shapes=[pltpu.VMEM((step, columns), near.dtype)],
        input_output_aliases=aliases,
        compiler_params=MIXER_PARAMS,
        cost_estimate=BESIDE,
        name="join_turns",
    )(*args)


def stack_turns_kernel(near_ref, one_ref, two_ref, first_ref, second_ref, out_ref):
    turn = lax.bitwise_xor(lax.axis_index("group"), pl.program_id(0))
    half = first_ref.shape[0]
    for at, ref in enumerate((near_ref, one_ref, two_ref)):

        @pl.when(turn == at)
        def _():
            out_ref[0] = ref[...].astype(out_ref.dtype)

    @pl.when(turn == 3)
    def _():
        out_ref[0, :half] = first_ref[...].astype(out_ref.dtype)
        out_ref[0, half:] = second_ref[...].astype(out_ref.dtype)


def stack_turns(turns, dtype):
    near, one, two, (first_half, second_half) = turns
    rows, columns = near.shape
    half = first_half.shape[0]
    whole = pl.BlockSpec((rows, columns), lambda i: (0, 0))
    halved = pl.BlockSpec((half, columns), lambda i: (0, 0))
    return pl.pallas_call(
        stack_turns_kernel,
        grid=(4,),
        in_specs=[whole, whole, whole, halved, halved],
        out_specs=pl.BlockSpec((1, rows, columns), lambda i: (i, 0, 0)),
        out_shape=jax.ShapeDtypeStruct((4, rows, columns), dtype),
        compiler_params=MIXER_PARAMS,
        cost_estimate=BESIDE,
        name="stack_turns",
    )(near, one, two, first_half, second_half)


def rms_scale(values, gain):
    return values * lax.rsqrt(jnp.mean(values * values, axis=-1, keepdims=True) + eps_norm) * gain


def swiglu(gate_up):
    half = gate_up.shape[1] // 2
    return jax.nn.silu(gate_up[:, :half]) * gate_up[:, half:]


def sum_parts(own, others):
    total = own.astype(f32)
    for part in others:
        total = total + part.astype(f32)
    return total


def dot(left, right):
    return jnp.dot(left, right, preferred_element_type=f32)


def dot_t(left, right):
    return lax.dot_general(left, right, (((0,), (0,)), ((), ())), preferred_element_type=f32)


def dot_back(left, right):
    return lax.dot_general(left, right, (((1,), (1,)), ((), ())), preferred_element_type=f32)


SHARDED = ("seq", "wshard")


class Place:
    def __init__(self, rows):
        self.group = lax.axis_size("group")
        self.seq = lax.axis_size("seq")
        self.cores = lax.axis_size("wshard")
        self.part = lax.axis_index("group")
        self.at_seq = lax.axis_index("seq")
        self.core = lax.axis_index("wshard")
        self.rows = rows
        self.per = rows // self.group
        self.subs = self.seq // self.group
        self.sources = self.seq // self.subs
        self.sub = self.at_seq % self.subs
        self.heads = H // self.group
        self.lane = self.seq * rows

    def deal(self, sorted_rows):
        width = sorted_rows.shape[1]
        if self.subs == 1:
            return lax.all_to_all(sorted_rows, "seq", split_axis=0, concat_axis=0, tiled=True)
        sent = jnp.zeros((self.group, self.subs, self.per, width), sorted_rows.dtype)
        sent = lax.dynamic_update_slice(
            sent,
            sorted_rows.reshape(self.group, 1, self.per, width),
            (0, self.at_seq // self.sources, 0, 0),
        )
        got = lax.all_to_all(
            sent.reshape(-1, width), "seq", split_axis=0, concat_axis=0, tiled=True
        )
        return lax.dynamic_slice(got, (self.sub * self.rows, 0), (self.rows, width))

    def undeal(self, rows):
        width = rows.shape[1]
        if self.subs == 1:
            return lax.all_to_all(rows, "seq", split_axis=0, concat_axis=0, tiled=True)
        sent = jnp.zeros((self.subs * self.rows, width), rows.dtype)
        sent = lax.dynamic_update_slice(sent, rows, (self.sub * self.rows, 0))
        got = lax.all_to_all(sent, "seq", split_axis=0, concat_axis=0, tiled=True)
        got = got.reshape(self.group, self.subs, self.per, width)
        got = lax.dynamic_slice(
            got, (0, self.at_seq // self.sources, 0, 0), (self.group, 1, self.per, width)
        )
        return got.reshape(self.rows, width)

    def swap(self, value, turn):
        if turn == 0:
            return value
        return lax.ppermute(value, "group", [(i, i ^ turn) for i in range(self.group)])

    def gather_any(self, rows):
        return jnp.concatenate([self.swap(rows, turn) for turn in range(self.group)], axis=0)

    def send_any(self, partial):
        own = partial[: self.rows]
        got = [
            self.swap(partial[turn * self.rows : (turn + 1) * self.rows], turn)
            for turn in range(1, self.group)
        ]
        return own, got

    def gather_places(self, rows, beside=()):
        width = rows.shape[1]
        got = [self.swap(rows, turn) for turn in range(1, self.group)]
        got, beside = lax.optimization_barrier((got, beside))
        lane = jnp.zeros((self.sources, self.group, self.per, width), rows.dtype)
        for turn, part in enumerate([rows] + got):
            part = part.reshape(self.sources, 1, self.per, width)
            lane = lax.dynamic_update_slice(lane, part, (0, self.part ^ turn, 0, 0))
        return lane.reshape(-1, width), beside

    def send_places(self, partial):
        width = partial.shape[1]
        lane = partial.reshape(self.sources, self.group, self.per, width)
        parts = [
            lax.dynamic_slice(
                lane, (0, self.part ^ turn, 0, 0), (self.sources, 1, self.per, width)
            ).reshape(self.rows, width)
            for turn in range(self.group)
        ]
        return parts[0], [self.swap(parts[turn], turn) for turn in range(1, self.group)]

    def near_turns(self, value):
        return (value, self.swap(value, 1), self.swap(value, 2))

    def far_turn(self, near):
        rows = near[0].shape[0] // 2
        return near + ((self.swap(near[2][:rows], 1), self.swap(near[1][rows:], 2)),)

    def turns_of(self, value):
        if self.group == 4 and value.ndim == 2 and value.shape[0] % 2 == 0:
            return self.far_turn(self.near_turns(value))
        return tuple(self.swap(value, turn) for turn in range(self.group))

    def joined(self, turns, runs, total_rows=None, into=None):
        if isinstance(turns[-1], tuple) and turns[-1][0].shape[0] % 16 == 0:
            return join_turns(turns, runs, total_rows, into)
        return join_columns(self.by_owner(turns), runs, total_rows, into)

    def stacked(self, turns, dtype):
        if isinstance(turns[-1], tuple) and turns[-1][0].shape[0] % 8 == 0:
            return stack_turns(turns, dtype)
        return self.by_owner(turns).astype(dtype)

    def by_owner(self, turns):
        value = turns[0]
        parts = jnp.zeros((self.group,) + value.shape, value.dtype)
        for turn, got in enumerate(turns):
            owner, begin = self.part ^ turn, 0
            for piece in got if isinstance(got, tuple) else (got,):
                parts = lax.dynamic_update_slice(
                    parts, piece[None], (owner, begin) + (0,) * (value.ndim - 1)
                )
                begin += piece.shape[0]
        return parts

    def gather_parts(self, value):
        return self.by_owner(self.turns_of(value))

    def to_lane(self, rows):
        if self.subs == 1:
            return rows
        every = lax.all_gather(rows, "seq", axis=0, tiled=True)
        length = rows.shape[0] * self.subs
        return lax.dynamic_slice(
            every, ((self.at_seq // self.subs) * length, 0), (length, rows.shape[1])
        )

    def to_own(self, lane_rows):
        if self.subs == 1:
            return lane_rows
        length = lane_rows.shape[0] // self.subs
        return lax.dynamic_slice(lane_rows, (self.sub * length, 0), (length, lane_rows.shape[1]))

    def head_columns(self, array, sections):
        pieces = []
        for begin, width in sections:
            for turn in range(self.heads):
                pieces.append(
                    lax.dynamic_slice(
                        array,
                        (0, begin + (turn * self.group + self.part) * width),
                        (array.shape[0], width),
                    )
                )
        return jnp.concatenate(pieces, axis=1)

    def core_rows(self, array, core):
        split = array.reshape(self.seq, self.cores, -1, array.shape[1])
        return lax.dynamic_index_in_dim(split, core, 1, keepdims=False).reshape(-1, array.shape[1])

    def core_sum(self, grad):
        if self.cores != 2:
            return grad
        got = lax.ppermute(self.core_rows(grad, 1 - self.core), "wshard", [(0, 1), (1, 0)])
        return (self.core_rows(grad, self.core).astype(f32) + got.astype(f32)).astype(bf16)

    def core_columns(self, array, halves_of=1):
        rows, columns = array.shape
        run = columns // (self.seq * self.cores)
        size = run // halves_of
        out = []
        for half in range(halves_of):
            picked = []
            for core in (1 - self.core, self.core) if self.cores == 2 else range(self.cores):
                picked.append(
                    [
                        lax.dynamic_slice(
                            array,
                            (0, (place * self.cores + core) * run + half * size),
                            (rows, size),
                        )
                        for place in range(self.seq)
                    ]
                )
            if self.cores == 2:
                out.append(tuple(jnp.concatenate(pieces, axis=1) for pieces in picked))
            else:
                every = [pieces[place] for place in range(self.seq) for pieces in picked]
                out.append((jnp.concatenate(every, axis=1),))
        return out

    def other_grad(self, lefts, right):
        if self.cores != 2:
            return None
        return lax.ppermute(dot_t(lefts[0], right).astype(bf16), "wshard", [(0, 1), (1, 0)])

    def own_grad(self, lefts, right, got):
        own = dot_t(lefts[-1], right)
        return (own if got is None else own + got.astype(f32)).astype(bf16)

    def scatter(self, grad):
        axes = "seq" if self.cores == 2 else SHARDED
        return lax.psum_scatter(grad, axes, scatter_dimension=0, tiled=True)

    def out_rows(self, w_out, down_piece):
        width = w_out.shape[1]
        if self.subs == 1 and self.cores == 2:
            mine = lax.dynamic_slice(w_out, ((self.part % 2) * DV, 0), (DV, width))
            half = DV // 2
            kept = lax.dynamic_slice(mine, (self.core * half, 0), (half, width))
            other = lax.dynamic_slice(mine, ((1 - self.core) * half, 0), (half, width))
            got = lax.ppermute(other, "wshard", [(0, 1), (1, 0)])
            piece = jnp.where(self.core == self.part // 2, kept, got)
            both = lax.all_gather(jnp.concatenate([piece, down_piece], axis=0), SHARDED, axis=0)
            both = both.reshape(self.seq * self.cores, -1, width)
            return both[:, :half].reshape(-1, width), both[:, half:].reshape(-1, width)
        every = lax.all_gather(w_out, SHARDED, axis=0, tiled=True)
        every = every.reshape(self.heads, self.group, DV, width)
        out_mine = lax.dynamic_slice(
            every, (0, self.part, 0, 0), (self.heads, 1, DV, width)
        ).reshape(-1, width)
        return out_mine, lax.all_gather(down_piece, SHARDED, axis=0, tiled=True)

    def out_grad(self, gated, d_branch):
        if self.subs == 1 and self.cores == 2:
            lefts = self.core_columns(gated)[0]
            return self.own_grad(lefts, d_branch, self.other_grad(lefts, d_branch))
        width = d_branch.shape[1]
        grad = dot_t(gated, d_branch).astype(bf16)
        every = jnp.zeros((self.heads, self.group, DV, width), bf16)
        every = lax.dynamic_update_slice(
            every, grad.reshape(self.heads, 1, DV, width), (0, self.part, 0, 0)
        ).reshape(-1, width)
        return self.core_sum(every)

    def out_rows_join(self, turns):
        shard = turns[0]
        width = shard.shape[1]
        if self.subs == 1 and self.cores == 2:
            halves_all = self.stacked(turns, bf16)
            here = lax.dynamic_slice(halves_all, (2 * self.core, 0, 0), (2, DV // 2, width))
            there = lax.dynamic_slice(halves_all, (2 - 2 * self.core, 0, 0), (2, DV // 2, width))
            got = lax.ppermute(there, "wshard", [(0, 1), (1, 0)])
            first = jnp.where(self.core == 0, here, got)
            second = jnp.where(self.core == 0, got, here)
            return jnp.stack([first, second], axis=1).reshape(2 * DV, width).astype(f32)
        return lax.psum(shard, "group").astype(f32)

    def conv_pieces(self, conv_w):
        if self.subs > 1:
            return conv_w
        columns = conv_w.shape[1]
        wide = lax.dynamic_slice(conv_w, (0, self.part * DV), (CONV, DV))
        narrow = self.head_columns_of(conv_w, DK)
        return jnp.where(self.at_seq * self.cores + self.core >= 2 * HK // columns, wide, narrow)

    def head_columns_of(self, array, head_width):
        count = array.shape[1] // (self.group * head_width)
        return jnp.concatenate(
            [
                lax.dynamic_slice(
                    array,
                    (0, (turn * self.group + self.part) * head_width),
                    (array.shape[0], head_width),
                )
                for turn in range(count)
            ],
            axis=1,
        )

    def join_conv(self, pieces):
        pieces = pieces.reshape(self.seq * self.cores, CONV, -1).transpose(1, 0, 2)
        pieces = pieces.reshape(CONV, -1)
        return self.head_columns(pieces, QKV) if self.subs > 1 else pieces

    def split_conv(self, grad):
        devices = self.seq * self.cores
        if self.subs > 1:
            pieces, begin = [], 0
            mine = (jnp.arange(self.group) == self.part).astype(f32)[:, None]
            for _, head_width in QKV:
                end = begin + self.heads * head_width
                section = grad[:, begin:end].reshape(CONV, self.heads, 1, head_width) * mine
                pieces.append(section.reshape(CONV, -1))
                begin = end
            grad = jnp.concatenate(pieces, axis=1)
        return grad.reshape(CONV, devices, -1).transpose(1, 0, 2).reshape(devices, -1)

    def join_own_conv(self, parts):
        parts = parts.reshape(self.group, CONV, -1)
        if self.subs > 1:
            return jnp.sum(parts, axis=0)
        columns = parts.shape[2] * self.group
        wide = parts.transpose(1, 0, 2).reshape(CONV, columns)
        narrow = parts.reshape(self.group, CONV, -1, DK).transpose(1, 2, 0, 3).reshape(CONV, columns)
        return jnp.where(self.at_seq * self.cores + self.core >= 2 * HK // columns, wide, narrow)


QKV = ((0, DK), (HK, DK), (2 * HK, DV))
GATE = ((2 * HK + HV, DV),)


def side_array(lane_lengths, length):
    ends = jnp.cumsum(lane_lengths)
    bounds = jnp.concatenate([jnp.zeros((1,), jnp.int32), ends])
    places = jnp.arange(length, dtype=jnp.int32)
    crossed = places[:, None] >= bounds[None, :]
    block_begin = (places // SPAN) * SPAN
    counted = jnp.sum((crossed & (bounds[None, :] >= block_begin[:, None])).astype(jnp.int32), axis=1)
    segment = jnp.sum(crossed.astype(jnp.int32), axis=1)
    columns = [counted.astype(f32)]
    for back in range(1, CONV):
        earlier = jnp.sum((places[:, None] - back >= bounds[None, :]).astype(jnp.int32), axis=1)
        columns.append(((earlier == segment) & (places >= back)).astype(f32))
    columns.append((places < ends[-1]).astype(f32))
    columns += [jnp.zeros((length,), f32)] * (SIDE - len(columns))
    return jnp.stack(columns, axis=1)


def shards(
    tokens,
    cotangent,
    dealing,
    lengths,
    attn_gain,
    w_in,
    w_ab,
    conv_w,
    decay_log,
    dt_bias,
    o_gain,
    w_out,
    ffn_gain,
    w_gu,
    w_down,
):
    rows, width = tokens.shape
    at = Place(rows)
    heads = at.heads
    device_rows = w_down.shape[0]
    devices = at.seq * at.cores

    at_device = at.at_seq * at.cores + at.core

    pieces = []
    for begin, piece_width in QKV + GATE:
        pieces += [
            (begin + turn * at.group * piece_width, piece_width) for turn in range(heads)
        ]
    in_piece = pick_columns(w_in, tuple(pieces), at.group)

    ab_shard = at.head_columns(w_ab, ((0, 1), (H, 1)))
    conv_pieces = at.conv_pieces(conv_w)
    small = (attn_gain, ffn_gain, o_gain, ab_shard.reshape(-1), conv_pieces.reshape(-1))
    lengths_small = [array.shape[0] for array in small]
    filled = sum(lengths_small)
    rows_small = -(-filled // (16 * 128)) * 16
    packed = jnp.concatenate(small + (jnp.zeros((rows_small * 128 - filled,), bf16),))
    packed, in_piece = lax.optimization_barrier((packed, in_piece))
    in_mine = lax.all_gather(in_piece, SHARDED, axis=0, tiled=True)
    packed = small_gather(packed.reshape(rows_small, 128), at.seq, at.cores)
    packed, tokens, cotangent = lax.optimization_barrier((packed, tokens, cotangent))
    packed = packed.reshape(devices, -1)
    full, begin = [], 0
    for count in lengths_small:
        full.append(packed[:, begin : begin + count])
        begin += count
    attn_f, ffn_f, o_f = (array.reshape(-1).astype(f32) for array in full[:3])
    ab_mine = full[3].reshape(width, 2 * heads)
    conv_mine = at.join_conv(full[4]).astype(f32)

    def my_heads(values):
        return lax.dynamic_slice(values.reshape(heads, at.group), (0, at.part), (heads, 1)).reshape(1, -1)

    decay_mine, dt_mine = my_heads(decay_log), my_heads(dt_bias)

    member = (dealing[:, None] == jnp.arange(at.group, dtype=jnp.int32)[None, :]).astype(jnp.int32)
    before = dot(jnp.tril(jnp.ones((rows, rows), f32), -1).astype(bf16), member.astype(bf16))
    before = before.astype(jnp.int32)
    target = jnp.sum((before + at.per * jnp.arange(at.group, dtype=jnp.int32)) * member, axis=1)
    sorting = (target[None, :] == jnp.arange(rows, dtype=jnp.int32)[:, None]).astype(bf16)
    tokens_f = at.deal(dot(sorting, tokens).astype(bf16)).astype(f32)
    normed = rms_scale(tokens_f, attn_f).astype(bf16)
    normed, cotangent, w_out, w_gu, w_down = lax.optimization_barrier(
        (normed, cotangent, w_out, w_gu, w_down)
    )
    normed_all, _ = at.gather_places(normed)
    normed_all, normed_cores = lax.optimization_barrier(
        (normed_all, at.core_columns(normed_all, 2))
    )

    piece = device_rows // at.group
    out_mine, down_mine = at.out_rows(
        w_out, lax.dynamic_slice(w_down, (at.part * piece, 0), (piece, width))
    )
    gu_pieces = tuple((block * device_rows, piece) for block in range(2 * devices))
    gu_mine = lax.all_gather(
        pick_columns(w_gu, gu_pieces, at.group), SHARDED, axis=0, tiled=True
    )
    cot_own = at.deal(dot(sorting, cotangent).astype(bf16))
    normed_all, cot_own = lax.optimization_barrier((normed_all, cot_own))

    lane_lengths = lax.dynamic_index_in_dim(
        at.gather_parts(lengths.reshape(-1)), at.at_seq // at.subs, 0, keepdims=False
    )
    side = side_array(lane_lengths, at.lane)
    gates_ab = at.to_lane(dot(normed_all, ab_mine))
    proj, cot_own = lax.optimization_barrier((dot(normed_all, in_mine), cot_own))
    cot_all = at.gather_any(cot_own)
    proj = at.to_lane(proj)
    mixer_args = (proj, gates_ab, side, conv_mine, o_f[None], decay_mine, dt_mine)
    gated_lane, *kept = mixer_forward(*mixer_args)
    gated_lane, cot_all, out_mine, down_mine = lax.optimization_barrier(
        (gated_lane, cot_all, out_mine, down_mine)
    )
    gated = at.to_own(gated_lane)
    own, got = at.send_places(dot(gated, out_mine).astype(bf16))
    resid = tokens_f + sum_parts(own, got)

    normed2_f, pull_norm2 = jax.vjp(rms_scale, resid, ffn_f)
    normed2_all = at.gather_any(normed2_f.astype(bf16))
    normed2_all, normed2_cores = lax.optimization_barrier(
        (normed2_all, at.core_columns(normed2_all)[0])
    )
    gate_up = dot(normed2_all, gu_mine)
    hidden_f, pull_ffn = jax.vjp(swiglu, gate_up)
    hidden = hidden_f.astype(bf16)

    d_down = at.core_sum(dot_t(hidden, cot_all).astype(bf16))
    d_down, hidden, cot_back = lax.optimization_barrier((d_down, hidden, cot_all))
    down_shard = at.scatter(d_down)
    d_hidden = dot_back(cot_back, down_mine)
    d_gate_up = pull_ffn(d_hidden)[0].astype(bf16)
    d_normed2_parts = dot_back(d_gate_up, gu_mine).astype(bf16)
    d_normed2_parts, d_gate_up = lax.optimization_barrier((d_normed2_parts, d_gate_up))
    own, got = at.send_any(d_normed2_parts)
    gu_got = at.other_grad(normed2_cores, d_gate_up)
    normed2_cores, down_shard = lax.optimization_barrier((normed2_cores, down_shard))
    d_gu = at.own_grad(normed2_cores, d_gate_up, gu_got)
    got, d_gu = lax.optimization_barrier((got, d_gu))
    gu_shard = at.scatter(d_gu)
    d_normed2 = sum_parts(own, got)
    d_resid_norm, d_ffn_gain = pull_norm2(d_normed2)
    d_resid = cot_own.astype(f32) + d_resid_norm

    d_branch_all, output_parts = at.gather_places(
        d_resid.astype(bf16), dot(hidden, down_mine).astype(bf16)
    )
    d_gated = dot_back(d_branch_all, out_mine)
    d_out = at.out_grad(gated, d_branch_all)
    d_gated, output_parts, down_shard, d_out = lax.optimization_barrier(
        (d_gated, output_parts, down_shard, d_out)
    )
    out_shard = at.scatter(d_out)
    output_own, output_got = at.send_any(output_parts)
    down_turns = at.near_turns(down_shard)
    d_proj_lane, d_gates_lane, d_conv_w, d_o_gain, d_heads = mixer_backward(
        *mixer_args, tuple(kept), at.to_lane(d_gated)
    )
    d_proj_lane, output_got, down_turns, gu_shard = lax.optimization_barrier(
        (d_proj_lane, output_got, down_turns, gu_shard)
    )
    gu_turns = at.near_turns(gu_shard)
    once = (at.sub == 0).astype(f32)
    d_conv_w, d_o_gain, d_heads = d_conv_w * once, d_o_gain * once, d_heads * once
    d_proj = at.to_own(d_proj_lane)
    d_ab = at.to_own(d_gates_lane).astype(bf16)
    in_got = [at.other_grad(lefts, d_proj) for lefts in normed_cores]
    first = at.own_grad(normed_cores[0], d_proj, in_got[0])
    first, in_got, d_proj = lax.optimization_barrier((first, in_got[1], d_proj))
    in_shards = [at.scatter(first)]
    second = at.own_grad(normed_cores[1], d_proj, in_got)
    second, d_proj, d_ab = lax.optimization_barrier((second, d_proj, d_ab))
    in_shards.append(at.scatter(second))
    d_normed_parts = (dot_back(d_proj, in_mine) + dot_back(d_ab, ab_mine)).astype(bf16)
    d_normed_parts, d_ab, output_got, out_shard = lax.optimization_barrier(
        (d_normed_parts, d_ab, output_got, out_shard)
    )
    output = (resid + sum_parts(output_own, output_got)).astype(bf16)
    own, got = at.send_places(d_normed_parts)
    d_w_ab = dot_t(normed_all, d_ab)
    got, d_w_ab, gu_turns = lax.optimization_barrier((got, d_w_ab, gu_turns))
    d_normed = sum_parts(own, got)
    value_norm, pull_norm = jax.vjp(rms_scale, tokens_f, attn_f)
    d_tokens_norm, d_attn_gain = pull_norm(d_normed)
    d_tokens = (d_resid + d_tokens_norm).astype(bf16)
    d_tokens, gu_turns, down_turns = lax.optimization_barrier((d_tokens, gu_turns, down_turns))
    gu_turns = at.far_turn(gu_turns)
    back = jnp.concatenate([output, d_tokens], axis=1)


    def to_blocks(array):
        return array.reshape(devices, -1)

    blocks = (
        to_blocks(d_attn_gain),
        to_blocks(d_ffn_gain),
        to_blocks(d_o_gain),
        to_blocks(d_w_ab),
        at.split_conv(d_conv_w),
        jnp.broadcast_to(d_heads, (devices, 2 * heads)),
    )
    sizes = [array.shape[1] for array in blocks]
    filled = sum(sizes)
    rows_small = -(-filled // 1024) * 8
    packed = jnp.concatenate(
        blocks + (jnp.zeros((devices, rows_small * 128 - filled), f32),), axis=1
    )
    summed = small_sum(packed.reshape(devices, rows_small, 128), at.seq, at.cores, at.group)

    in_runs = tuple((piece_width, heads) for _, piece_width in QKV + GATE)
    in_first, in_second = in_shards
    out_turns = at.near_turns(out_shard)
    in_first, summed, gu_turns, down_turns, out_turns = lax.optimization_barrier(
        (in_first, summed, gu_turns, down_turns, out_turns)
    )
    out_turns = at.far_turn(out_turns)
    down_turns = at.far_turn(down_turns)
    first_turns = at.near_turns(in_first)
    grad_w_gu = at.joined(gu_turns, ((piece, 2 * devices),))
    first_turns, grad_w_gu = lax.optimization_barrier((first_turns, grad_w_gu))
    first_turns = at.far_turn(first_turns)
    grad_w_down = at.stacked(down_turns, f32).reshape(device_rows, width)
    first_turns, grad_w_down, in_second, back = lax.optimization_barrier(
        (first_turns, grad_w_down, in_second, back)
    )
    second_turns = at.near_turns(in_second)
    returned = at.undeal(back)
    grad_w_in = at.joined(first_turns, in_runs, total_rows=w_in.shape[0])
    grad_w_out = at.out_rows_join(out_turns)
    second_turns, grad_w_in, grad_w_out = lax.optimization_barrier(
        (second_turns, grad_w_in, grad_w_out)
    )
    second_turns = at.far_turn(second_turns)
    second_turns, returned = lax.optimization_barrier((second_turns, returned))
    grad_w_in = at.joined(second_turns, in_runs, into=grad_w_in)
    returned = dot_t(sorting, returned).astype(bf16)

    summed = summed.reshape(at.group, -1)
    parts, begin = [], 0
    for size in sizes:
        parts.append(summed[:, begin : begin + size])
        begin += size
    grad_w_ab = parts[3].reshape(at.group, width // devices, 2, heads).transpose(1, 2, 3, 0)
    grad_heads = parts[5].reshape(at.group, 2, heads).transpose(1, 2, 0).reshape(2, H)
    return (
        returned[:, :width],
        returned[:, width:],
        jnp.sum(parts[0], axis=0),
        grad_w_in,
        grad_w_ab.reshape(width // devices, 2 * H),
        at.join_own_conv(parts[4]),
        grad_heads[0],
        grad_heads[1],
        jnp.sum(parts[2], axis=0),
        grad_w_out,
        jnp.sum(parts[1], axis=0),
        grad_w_gu,
        grad_w_down,
    )


def solution(mesh):
    placed = (
        P(("group", "seq", "wshard"), None),
        P(("group", "seq", "wshard"), None),
        P(("group", "seq", "wshard")),
        P("group", "wshard", None),
        P(("seq", "wshard")),
        P(("seq", "wshard"), None),
        P(("seq", "wshard"), None),
        P(None, ("seq", "wshard")),
        P(),
        P(),
        P(("seq", "wshard")),
        P(("seq", "wshard"), None),
        P(("seq", "wshard")),
        P(("seq", "wshard"), None),
        P(("seq", "wshard"), None),
    )
    return jax.shard_map(
        shards,
        mesh=mesh,
        in_specs=placed,
        out_specs=(
            P(("group", "seq", "wshard"), None),
            P(("group", "seq", "wshard"), None),
            P(("seq", "wshard")),
            P(("seq", "wshard"), None),
            P(("seq", "wshard"), None),
            P(None, ("seq", "wshard")),
            P(),
            P(),
            P(("seq", "wshard")),
            P(("seq", "wshard"), None),
            P(("seq", "wshard")),
            P(("seq", "wshard"), None),
            P(("seq", "wshard"), None),
        ),
        check_vma=False,
    )
```
